256 devices in a mesh: seq: 64 (over y, z, core), head: 4 (over x).
Axes of the slice: x: 4, y: 4, z: 8, core: 2. Of those that a mesh axis runs over, the one named last changes fastest.
Arguments:
- query_vectors: float32 [16384, 2048], P('seq', 'head'), may hold values from -8 to 8
- key_vectors: float32 [16384, 2048], P('seq', 'head'), may hold values from -4 to 4
- value_vectors: float32 [16384, 2048], P('seq', 'head'), may hold values from -24 to 24
- norm_gain: float32 [2048], P('head'), may hold values from 0.5 to 1.5
- upstream: float32 [16384, 2048], P('seq', 'head'), may hold values from -6 to 6
Outputs:
- attended: float32 [16384, 2048], P('seq', 'head')
- query_grad: float32 [16384, 2048], P('seq', 'head')
- key_grad: float32 [16384, 2048], P('seq', 'head')
- value_grad: float32 [16384, 2048], P('seq', 'head')
The draws below stay inside these ranges and needn't reach their ends.
All inputs are finite; a program needn't handle non-finite values.
Results may differ from the reference program's by a relative error of at most 0.0012.
Values sent between devices are 32-bit elements; how exact they have to be, the bound alone decides.
No kernel may reach another device: no remote copies, remote signals or barrier semaphores. Data moves between devices by JAX's collectives and lax.ppermute only.
A program may use at most 64 MiB of HBM per device.

```python
import math
import jax
import jax.numpy as jnp
from jax import lax

HEADS = 16
DHEAD = 128
BLOCK = 256
LEVELS = 3
TOKENS = 16384
FEAT = 2048


def draw_query_vectors(key, part):
    key = jax.random.fold_in(key, 1)
    values = jnp.clip(jax.random.normal(key, (TOKENS, FEAT), jnp.float32), -4.0, 4.0)
    return values


def draw_key_vectors(key, part):
    key = jax.random.fold_in(key, 2)
    values = jnp.clip(jax.random.normal(key, (TOKENS, FEAT), jnp.float32), -4.0, 4.0)
    return values


def draw_value_vectors(key, part):
    key = jax.random.fold_in(key, 3)
    columns = 0.3 * jnp.exp(jax.random.uniform(jax.random.fold_in(key, 11), (FEAT,), jnp.float32, 0.0, math.log(10.0)))
    head_index = (jnp.arange(FEAT, dtype=jnp.int32) // DHEAD).astype(jnp.float32)
    head_rise = jnp.exp(math.log(3.0) * head_index / max(HEADS - 1, 1)) / math.sqrt(3.0)
    values = jnp.clip(jax.random.normal(key, (TOKENS, FEAT), jnp.float32), -4.0, 4.0)
    return values * columns[None, :] * head_rise[None, :]


def block_scale(rng, shape, split, least, largest):
    loudness = 1.0
    for position, parts in split:
        steps = jax.random.uniform(jax.random.fold_in(jax.random.fold_in(rng, 6), position), (parts,), jnp.float32, least / len(split), largest / len(split))
        loudness = loudness * jnp.repeat(jnp.exp(steps), shape[position] // parts).reshape((-1,) + (1,) * (len(shape) - 1 - position))
    return loudness


def noise(own_key, shape, deviation, most, split=(), kind=jnp.bfloat16):
    result = jax.random.normal(own_key, shape, jnp.float32) * deviation
    if len(split) > 0:
        result = block_scale(own_key, shape, split, -0.22, 0.18) * result
    return jnp.clip(result, min=-most, max=most).astype(kind)


def setup_inputs(seed: int = 0) -> dict:
    arg_keys = jax.random.split(jax.random.key(seed), 6)
    return {
        "query_vectors": draw_query_vectors(jax.random.fold_in(arg_keys[5], 71), 0),
        "key_vectors": draw_key_vectors(jax.random.fold_in(arg_keys[5], 71), 0),
        "value_vectors": draw_value_vectors(jax.random.fold_in(arg_keys[5], 71), 0),
        "norm_gain": jnp.clip(1.0 + 0.1 * jax.random.normal(arg_keys[3], (FEAT,), jnp.float32), 0.5, 1.5),
        "upstream": noise(arg_keys[4], (TOKENS, FEAT), 1.0, 6.0, ((0, 64), (1, 4)), jnp.float32),
    }


NEGATIVE_FILL = -1e+30
EPSILON = 1e-06
HIGHEST = lax.Precision.HIGHEST

def pooled_means(matrix, factor):
    return lax.optimization_barrier(jnp.mean(matrix.reshape(matrix.shape[0] // factor, factor, matrix.shape[1]), axis=1))

def padded_pool(matrix, factor):
    pooled = pooled_means(matrix, factor)
    length = pooled.shape[0]
    target = (length + BLOCK - 1) // BLOCK * BLOCK
    return jnp.pad(pooled, ((0, target - length), (0, 0)))

def attention_layer(query_vectors, key_vectors, value_vectors):
    block_total = TOKENS // BLOCK
    inv_root = 1.0 / math.sqrt(DHEAD)
    key_padded = jnp.pad(key_vectors, ((BLOCK, BLOCK), (0, 0)))
    value_padded = jnp.pad(value_vectors, ((BLOCK, BLOCK), (0, 0)))
    key_levels = [padded_pool(key_vectors, 4 ** level_index) for level_index in range(1, LEVELS + 1)]
    value_levels = [padded_pool(value_vectors, 4 ** level_index) for level_index in range(1, LEVELS + 1)]

    def one_block(block_index):
        first = block_index * BLOCK
        query_block = lax.dynamic_slice_in_dim(query_vectors, first, BLOCK, 0)
        key_window = lax.dynamic_slice_in_dim(key_padded, first, 3 * BLOCK, 0)
        value_window = lax.dynamic_slice_in_dim(value_padded, first, 3 * BLOCK, 0)
        token_index = first - BLOCK + jnp.arange(3 * BLOCK, dtype=jnp.int32)
        valid_near = (token_index >= 0) & (token_index < TOKENS)
        near_scores = jnp.einsum('qhd,khd->hqk', query_block.reshape(BLOCK, HEADS, DHEAD), key_window.reshape(3 * BLOCK, HEADS, DHEAD), precision=HIGHEST) * inv_root
        score_parts = [jnp.where(valid_near[None, None, :], near_scores, NEGATIVE_FILL)]
        value_parts = [value_window]
        for level_index in range(1, LEVELS + 1):
            factor = 4 ** level_index
            finer = factor // 4
            coarse_query = pooled_means(query_block, factor)
            super_block = block_index // factor
            coarse_keys = lax.dynamic_slice_in_dim(key_levels[level_index - 1], super_block * BLOCK, BLOCK, 0)
            coarse_values = lax.dynamic_slice_in_dim(value_levels[level_index - 1], super_block * BLOCK, BLOCK, 0)
            pooled_index = super_block * BLOCK + jnp.arange(BLOCK, dtype=jnp.int32)
            key_block = pooled_index * factor // BLOCK
            inside = (key_block // finer == block_index // finer) | (jnp.abs(key_block - block_index) <= 1)
            valid_far = (pooled_index < TOKENS // factor) & jnp.logical_not(inside)
            far_scores = jnp.einsum('ghd,khd->hgk', coarse_query.reshape(BLOCK // factor, HEADS, DHEAD), coarse_keys.reshape(BLOCK, HEADS, DHEAD), precision=HIGHEST) * inv_root
            far_scores = far_scores + level_index * math.log(4.0)
            far_scores = jnp.where(valid_far[None, None, :], far_scores, NEGATIVE_FILL)
            score_parts.append(jnp.repeat(far_scores, factor, axis=1))
            value_parts.append(coarse_values)
        scores = jnp.concatenate(score_parts, axis=2)
        row_peak = lax.optimization_barrier(jnp.max(scores, axis=2, keepdims=True))
        weights = jnp.exp(scores - row_peak)
        probabilities = weights / lax.optimization_barrier(jnp.sum(weights, axis=2, keepdims=True))
        all_values = jnp.concatenate(value_parts, axis=0)
        all_values = all_values.reshape(all_values.shape[0], HEADS, DHEAD)
        mixed = jnp.einsum('hqk,khd->qhd', probabilities, all_values, precision=HIGHEST)
        return mixed.reshape(BLOCK, FEAT)
    blocks_out = lax.map(jax.checkpoint(one_block), jnp.arange(block_total, dtype=jnp.int32))
    return blocks_out.reshape(TOKENS, FEAT)

def reference(query_vectors, key_vectors, value_vectors, norm_gain, upstream):

    def layer(query_part, key_part, value_part):
        attention = attention_layer(query_part, key_part, value_part)
        mean_square = lax.optimization_barrier(jnp.mean(attention * attention, axis=1, keepdims=True))
        return attention * lax.rsqrt(mean_square + EPSILON) * norm_gain[None, :]
    attended, pullback = jax.vjp(layer, query_vectors, key_vectors, value_vectors)
    query_grad, key_grad, value_grad = pullback(upstream)
    return (attended, query_grad, key_grad, value_grad)
```

```python
import math

import jax
import jax.numpy as jnp
import numpy as np
from jax import lax
from jax.experimental import pallas as pl
from jax.experimental.pallas import tpu as pltpu
from jax.sharding import PartitionSpec as P

DHEAD = 128
BLOCK = 256
FEAT = 2048
HEADS = 4
WIDTH = HEADS * DHEAD
NEGATIVE_FILL = -1e30
FLOOR = -1e25
EPSILON = 1e-06
INV_ROOT = 1.0 / math.sqrt(DHEAD)
LN4 = math.log(4.0)
VMEM_BYTES = 48 * 1024 * 1024

OWN = 96
LEVEL_ROWS = ((0, 64), (64, 80), (80, 84))
FAR = 512
KV = 2 * WIDTH
GRAD = 2 * WIDTH + DHEAD

QUAD = (4, 8, 12)
HALF2_BLOCKS = QUAD + tuple(2 ^ o for o in QUAD)
HALF3_BLOCKS = (0,) + QUAD + tuple(2 ^ o for o in (0,) + QUAD)
YZ3_BLOCKS = tuple(y ^ o for y in (16, 32, 48) for o in HALF3_BLOCKS)
SLOTS = (
    ((2, 3), 64),
    (HALF2_BLOCKS + tuple(1 ^ o for o in HALF2_BLOCKS), 16),
    (YZ3_BLOCKS + tuple(1 ^ o for o in YZ3_BLOCKS), 4),
)


def slot_table():
    offset = np.concatenate([np.repeat(np.array(blocks, np.int32), rows) for blocks, rows in SLOTS])
    level = np.concatenate([np.full(len(blocks) * rows, n + 1, np.int32) for n, (blocks, rows) in enumerate(SLOTS)])
    own = np.zeros(OWN, np.int32)
    for n, (start, stop) in enumerate(LEVEL_ROWS):
        own[start:stop] = n + 1
    return offset[None, :], level[None, :], own[:, None]


def split3(x):
    high = x.astype(jnp.bfloat16)
    rest = x - high.astype(jnp.float32)
    middle = rest.astype(jnp.bfloat16)
    return high, middle, (rest - middle.astype(jnp.float32)).astype(jnp.bfloat16)


def dot(a, b, dims):
    return lax.dot_general(a, b, (dims, ((), ())), preferred_element_type=jnp.float32)


def nt3(a, b):
    a1, a2, a3 = split3(a)
    b1, b2, b3 = split3(b)
    left = jnp.concatenate([a1, a2, a1, a2, a1, a3], axis=1)
    right = jnp.concatenate([b1, b1, b2, b2, b3, b1], axis=1)
    return dot(left, right, ((1,), (1,)))


def nn3(a, b):
    a1, a2, a3 = split3(a)
    b1, b2, b3 = split3(b)
    right = jnp.concatenate([b1, b2], axis=1)
    main = dot(jnp.concatenate([a1, a2], axis=1), jnp.concatenate([right, right], axis=0), ((1,), (0,)))
    small = dot(jnp.concatenate([a1, a3], axis=1), jnp.concatenate([b3, b1], axis=0), ((1,), (0,)))
    return main[:, :DHEAD] + (main[:, DHEAD:] + small)


def cols(h, base=0):
    return slice(base + h * DHEAD, base + (h + 1) * DHEAD)


def quarters(ref, value):
    rows = value.shape[0] // 4
    ref[pl.ds(0, 4 * rows), :] = value
    return [ref[pl.ds(j, rows, stride=4), :] for j in range(4)]


def mean4(ref, value):
    parts = quarters(ref, value)
    return ((parts[0] + parts[1]) + (parts[2] + parts[3])) * 0.25


def expand(ref, value):
    rows = value.shape[0]
    for j in range(4):
        ref[pl.ds(j, rows, stride=4), :] = value
    return ref[pl.ds(0, 4 * rows), :]


def expand_levels(ref, value, scales):
    total = value[80:84] * scales[2]
    total = value[64:80] * scales[1] + expand(ref, total)
    total = value[0:64] * scales[0] + expand(ref, total)
    return expand(ref, total)


def lane_index(rows):
    return lax.broadcasted_iota(jnp.int32, (rows, DHEAD), 1)


def wide(column):
    return jnp.broadcast_to(column, (column.shape[0], DHEAD))


def gathered(refs, lanes):
    l1a, l1b, l2a, l2b, l2c, l2d, l3a, l3b = refs
    pieces = [l1a[:, lanes], l1b[:, lanes]]
    pieces += [ref[0:48, lanes] for ref in (l2a, l2b, l2c, l2d)]
    pieces += [l3a[:, lanes], l3b[:, lanes]]
    return jnp.concatenate(pieces, axis=0)


def pool_kernel(
    k_ref, v_ref, q_ref, own_ref, first_ref, rest_ref, pair_ref, query_ref, e0_ref, e1_ref, e2_ref, in_ref, sems
):
    copies = [pltpu.make_async_copy(ref, in_ref.at[i], sems.at[i]) for i, ref in enumerate((k_ref, v_ref, q_ref))]
    for copy in copies:
        copy.start()
    own_ref[84:96, :] = jnp.zeros((12, 3 * WIDTH), jnp.float32)
    for part, copy in enumerate(copies):
        copy.wait()
        for h in range(HEADS):
            dst = cols(h, part * WIDTH)
            value = in_ref[part, :, cols(h)]
            one = mean4(e0_ref.at[(part * HEADS + h) % 2], value)
            two = mean4(e1_ref, one)
            three = mean4(e2_ref, two)
            own_ref[0:64, dst] = one
            own_ref[64:80, dst] = two
            own_ref[80:84, dst] = three
            if part < 2:
                first_ref[:, dst] = one
                rest_ref[0:16, dst] = two
                rest_ref[16:20, dst] = three
                pair_ref[:, dst] = value
            else:
                query_ref[:, cols(h)] = value


def merge_kernel(own_ref, a_ref, b_ref, c_ref, out_ref):
    for i, ref in enumerate((a_ref, b_ref, c_ref)):
        out_ref[16 * i : 16 * i + 16, :] = ref[0:16, :]
    out_ref[48:52, :] = own_ref[16:20, :]
    for i, ref in enumerate((a_ref, b_ref, c_ref)):
        out_ref[52 + 4 * i : 56 + 4 * i, :] = ref[16:20, :]


def thirds_kernel(a_ref, b_ref, out_ref):
    out_ref[0:16, :] = a_ref[48:64, :]
    out_ref[16:32, :] = b_ref[48:64, :]


def stack_kernel(a_ref, b_ref, c_ref, out_ref):
    out_ref[0:32, :] = a_ref[...]
    out_ref[32:64, :] = b_ref[...]
    out_ref[64:96, :] = c_ref[...]


def near_forward_kernel(
    edge_ref, q_ref, kp_ref, ko_ref, kn_ref, vp_ref, vo_ref, vn_ref, w_ref, peak_ref, mass_ref, sum_ref
):
    keys = jnp.concatenate([kp_ref[...], ko_ref[...], kn_ref[...]], axis=0)
    values = jnp.concatenate([vp_ref[...], vo_ref[...], vn_ref[...]], axis=0)
    scores = nt3(q_ref[...], keys) * INV_ROOT + edge_ref[0:1, :]
    peak = jnp.max(scores, axis=1, keepdims=True)
    weights = jnp.exp(scores - peak)
    w_ref[0] = weights
    peak_ref[...] = wide(peak)
    mass_ref[...] = wide(jnp.sum(weights, axis=1, keepdims=True))
    sum_ref[...] = nn3(weights, values)


def merge(one, two):
    peak = jnp.maximum(one[0], two[0])
    left = jnp.exp(one[0] - peak)
    right = jnp.exp(two[0] - peak)
    return peak, left * one[1] + right * two[1], left * one[2] + right * two[2]


def far_forward_kernel(
    bias_ref, own_ref, a0, a1, a2, a3, a4, a5, a6, a7,
    peak_ref, mass_ref, sum_ref, up_ref, gain_ref,
    att_ref, lse_ref, stat_ref,
    e0_ref, e1_ref, e2_ref, square_ref, cross_ref,
):
    far = (a0, a1, a2, a3, a4, a5, a6, a7)
    bias = bias_ref[...]
    for h in range(HEADS):
        k = cols(h)
        v = cols(h, WIDTH)
        scores = nt3(own_ref[:, cols(h, 2 * WIDTH)], gathered(far, k)) * INV_ROOT + bias
        peak = jnp.maximum(jnp.max(scores, axis=1, keepdims=True), FLOOR)
        weights = jnp.exp(scores - peak)
        mass = jnp.sum(weights, axis=1, keepdims=True)
        levels = (wide(peak), wide(mass), nn3(weights, gathered(far, v)))
        state = tuple(x[80:84] for x in levels)
        for start, stop in (LEVEL_ROWS[1], LEVEL_ROWS[0]):
            state = tuple(expand(ref.at[h % 2], x) for ref, x in zip((e0_ref, e1_ref, e2_ref), state))
            state = merge(state, tuple(x[start:stop] for x in levels))
        state = tuple(expand(ref.at[h % 2], x) for ref, x in zip((e0_ref, e1_ref, e2_ref), state))
        state = merge(state, (peak_ref[:, k], mass_ref[:, k], sum_ref[:, k]))
        attention = state[2] / state[1]
        att_ref[:, k] = attention
        lse_ref[:, k] = state[0] + jnp.log(state[1])
        square = attention * attention
        cross = up_ref[:, k] * gain_ref[0:1, k] * attention
        if h == 0:
            square_ref[...] = square
            cross_ref[...] = cross
        else:
            square_ref[...] += square
            cross_ref[...] += cross
    square = wide(jnp.sum(square_ref[...], axis=1, keepdims=True))
    cross = wide(jnp.sum(cross_ref[...], axis=1, keepdims=True))
    packed = jnp.where(lane_index(BLOCK) == 0, square, cross)
    stat_ref[...] = jnp.transpose(packed)[0:8, :]


def pooled_cotangent(scratch, lows, dots, grads):
    lows, dots, grads = (quarters(ref, x) for ref, x in zip(scratch, (lows, dots, grads)))
    low = jnp.minimum(jnp.minimum(lows[0], lows[1]), jnp.minimum(lows[2], lows[3]))
    scale = [jnp.exp(low - x) for x in lows]
    total = scale[0] * dots[0]
    grad = scale[0] * grads[0]
    for j in range(1, 4):
        total = total + scale[j] * dots[j]
        grad = grad + scale[j] * grads[j]
    return low, total, grad


def cotangent_kernel(
    s0_ref, s1_ref, s2_ref, s3_ref, own_ref, att_ref, lse_ref, up_ref, gain_ref,
    out_ref, dout_ref, delta_ref, first_ref, rest_ref,
    e0_ref, e1_ref, e2_ref,
):
    total = (s0_ref[...] + s1_ref[...]) + (s2_ref[...] + s3_ref[...])
    square = jnp.transpose(jnp.broadcast_to(total[0:1, :], (DHEAD, BLOCK)))
    cross = jnp.transpose(jnp.broadcast_to(total[1:2, :], (DHEAD, BLOCK)))
    inverse = lax.rsqrt(square / FEAT + EPSILON)
    pull = inverse * inverse * inverse * cross / FEAT
    lane = lane_index(BLOCK)
    packed = jnp.zeros((BLOCK, DHEAD), jnp.float32)
    stats = [jnp.zeros((rows, DHEAD), jnp.float32) for rows in (64, 16, 4)]
    first_ref[:, WIDTH:KV] = own_ref[0:64, KV:]
    rest_ref[:, WIDTH:KV] = own_ref[64:84, KV:]
    for h in range(HEADS):
        k = cols(h)
        attention = att_ref[:, k]
        out_ref[:, k] = attention * inverse * gain_ref[0:1, k]
        d_out = inverse * (up_ref[:, k] * gain_ref[0:1, k]) - attention * pull
        dout_ref[0:BLOCK, k] = d_out
        delta = wide(jnp.sum(d_out * attention, axis=1, keepdims=True))
        delta_ref[:, k] = delta
        packed = jnp.where(lane == h, lse_ref[:, k], packed)
        packed = jnp.where(lane == HEADS + h, delta, packed)
        level = (lse_ref[:, k], delta, d_out)
        for n, (ref, start) in enumerate(((first_ref, 0), (rest_ref, 0), (rest_ref, 16))):
            level = pooled_cotangent([e.at[h % 2] for e in (e0_ref, e1_ref, e2_ref)], *level)
            rows = level[0].shape[0]
            ref[start : start + rows, k] = level[2]
            short = lane[0:rows]
            stats[n] = jnp.where(short == h, level[0], jnp.where(short == HEADS + h, level[1], stats[n]))
    first_ref[:, KV:] = stats[0]
    rest_ref[0:16, KV:] = stats[1]
    rest_ref[16:20, KV:] = stats[2]
    dout_ref[BLOCK:, 0:256] = jnp.transpose(packed)[0:8, :]
    dout_ref[BLOCK:, 256:] = jnp.zeros((8, 256), jnp.float32)


def near_query_kernel(
    w_ref, peak_ref, lse_ref, delta_ref, dout_ref, kp_ref, ko_ref, kn_ref, vp_ref, vo_ref, vn_ref, dq_ref
):
    keys = jnp.concatenate([kp_ref[...], ko_ref[...], kn_ref[...]], axis=0)
    values = jnp.concatenate([vp_ref[...], vo_ref[...], vn_ref[...]], axis=0)
    factor = jnp.exp(peak_ref[:, 0:1] - lse_ref[:, 0:1])
    weights = w_ref[0] * factor
    d_scores = weights * (nt3(dout_ref[...], values) - delta_ref[:, 0:1])
    dq_ref[...] = nn3(d_scores, keys) * INV_ROOT


def far_query_kernel(
    bias_ref, own_ref, a0, a1, a2, a3, a4, a5, a6, a7, first_ref, rest_ref, near_ref, dq_ref, e0_ref
):
    far = (a0, a1, a2, a3, a4, a5, a6, a7)
    bias = bias_ref[...]

    def grads(lanes):
        fill = jnp.zeros((12, DHEAD), jnp.float32)
        return jnp.concatenate([first_ref[:, lanes], rest_ref[0:16, lanes], rest_ref[16:20, lanes], fill], axis=0)

    stats = grads(slice(KV, GRAD))
    for h in range(HEADS):
        k = cols(h)
        keys = gathered(far, k)
        scores = nt3(own_ref[:, cols(h, 2 * WIDTH)], keys) * INV_ROOT + bias
        weights = jnp.exp(scores - stats[:, h : h + 1])
        d_probs = nt3(grads(k), gathered(far, cols(h, WIDTH)))
        d_scores = weights * (d_probs - stats[:, HEADS + h : HEADS + h + 1])
        grad = nn3(d_scores, keys)
        scales = [INV_ROOT / 4**n for n in (1, 2, 3)]
        dq_ref[:, k] = near_ref[:, k] + expand_levels(e0_ref.at[h % 2], grad, scales)


def near_key_kernel(
    k_ref, v_ref, qp_ref, qo_ref, qn_ref, dp_ref, do_ref, dn_ref, tp_ref, to_ref, tn_ref, dk_ref, dv_ref
):
    h = pl.program_id(0)
    queries = jnp.concatenate([qp_ref[...], qo_ref[...], qn_ref[...]], axis=0)
    grads = jnp.concatenate([dp_ref[...], do_ref[...], dn_ref[...]], axis=0)
    low = jnp.concatenate([ref[pl.ds(h, 1), :] for ref in (tp_ref, to_ref, tn_ref)], axis=1)
    total = jnp.concatenate([ref[pl.ds(h + HEADS, 1), :] for ref in (tp_ref, to_ref, tn_ref)], axis=1)
    weights = jnp.exp(nt3(k_ref[...], queries) * INV_ROOT - low)
    d_scores = weights * (nt3(v_ref[...], grads) - total)
    dk_ref[...] = nn3(d_scores, queries) * INV_ROOT
    dv_ref[...] = nn3(weights, grads)


def far_key_kernel(
    bias_ref, own_ref, a0, a1, a2, a3, a4, a5, a6, a7, dk_in_ref, dv_in_ref, dk_ref, dv_ref, e0_ref, e1_ref
):
    far = (a0, a1, a2, a3, a4, a5, a6, a7)
    bias = bias_ref[...]
    stats = jnp.transpose(gathered(far, slice(KV, GRAD)))[0:8, :]
    for h in range(HEADS):
        k = cols(h)
        queries = gathered(far, cols(h, WIDTH))
        grads = gathered(far, k)
        scores = nt3(own_ref[:, k], queries) * INV_ROOT + bias
        weights = jnp.exp(scores - stats[h : h + 1, :])
        d_scores = weights * (nt3(own_ref[:, cols(h, WIDTH)], grads) - stats[HEADS + h : HEADS + h + 1, :])
        scales = [1.0 / 4**n for n in (1, 2, 3)]
        d_keys = nn3(d_scores, queries) * INV_ROOT
        dk_ref[:, k] = dk_in_ref[:, k] + expand_levels(e0_ref.at[h % 2], d_keys, scales)
        dv_ref[:, k] = dv_in_ref[:, k] + expand_levels(e1_ref.at[h % 2], nn3(weights, grads), scales)


def f32(*shape):
    return jax.ShapeDtypeStruct(shape, jnp.float32)


def params():
    return pltpu.CompilerParams(vmem_limit_bytes=VMEM_BYTES)


def cost(flops, size):
    return pl.CostEstimate(flops=int(flops), bytes_accessed=int(size), transcendentals=0)


def whole_call(kernel, outs, scratch, flops, size, *operands):
    spec = pl.BlockSpec(memory_space=pltpu.VMEM)
    return pl.pallas_call(
        kernel,
        out_shape=outs,
        in_specs=[spec] * len(operands),
        out_specs=[spec] * len(outs),
        scratch_shapes=[pltpu.VMEM(shape, jnp.float32) for shape in scratch],
        compiler_params=params(),
        cost_estimate=cost(flops, size),
    )(*operands)


BLOCK_FLOPS = 2.0 * BLOCK * BLOCK * DHEAD * HEADS * 6


def column():
    return pl.BlockSpec((BLOCK, DHEAD), lambda h: (0, h))


def column_at(first):
    return pl.BlockSpec((BLOCK, DHEAD), lambda h: (0, first + h))


def near_forward(edge, query, kvp, pair, kvn):
    slab = pl.BlockSpec((1, BLOCK, 3 * BLOCK), lambda h: (h, 0, 0))
    edge_spec = pl.BlockSpec((1, 3 * BLOCK), lambda h: (0, 0))
    k, v = column_at(0), column_at(HEADS)
    return pl.pallas_call(
        near_forward_kernel,
        grid=(HEADS,),
        out_shape=[f32(HEADS, BLOCK, 3 * BLOCK), f32(BLOCK, WIDTH), f32(BLOCK, WIDTH), f32(BLOCK, WIDTH)],
        in_specs=[edge_spec, k, k, k, k, v, v, v],
        out_specs=[slab, k, k, k],
        compiler_params=params(),
        cost_estimate=cost(6 * BLOCK_FLOPS, 8e6),
    )(edge, query, kvp, pair, kvn, kvp, pair, kvn)


def near_query(weights, peak, lse, delta, d_out, kvp, pair, kvn):
    slab = pl.BlockSpec((1, BLOCK, 3 * BLOCK), lambda h: (h, 0, 0))
    k, v = column_at(0), column_at(HEADS)
    return pl.pallas_call(
        near_query_kernel,
        grid=(HEADS,),
        out_shape=f32(BLOCK, WIDTH),
        in_specs=[slab, k, k, k, k, k, k, k, v, v, v],
        out_specs=k,
        compiler_params=params(),
        cost_estimate=cost(6 * BLOCK_FLOPS, 8e6),
    )(weights, peak, lse, delta, d_out, kvp, pair, kvn, kvp, pair, kvn)


def near_key(pair, qp, query, qn, dp, d_out, dn):
    stat = pl.BlockSpec((8, 256), lambda h: (BLOCK // 8, 0))
    k, v = column_at(0), column_at(HEADS)
    return pl.pallas_call(
        near_key_kernel,
        grid=(HEADS,),
        out_shape=[f32(BLOCK, WIDTH)] * 2,
        in_specs=[k, v] + [k] * 6 + [stat] * 3,
        out_specs=[k] * 2,
        compiler_params=params(),
        cost_estimate=cost(12 * BLOCK_FLOPS, 8e6),
    )(pair, pair, qp, query, qn, dp, d_out, dn, dp, d_out, dn)


def pool(key, value, query):
    vmem = pl.BlockSpec(memory_space=pltpu.VMEM)
    hbm = pl.BlockSpec(memory_space=pltpu.HBM)
    return pl.pallas_call(
        pool_kernel,
        out_shape=[f32(OWN, 3 * WIDTH), f32(64, KV), f32(20, KV), f32(BLOCK, KV), f32(BLOCK, WIDTH)],
        in_specs=[hbm] * 3,
        out_specs=[vmem] * 5,
        scratch_shapes=[
            pltpu.VMEM((2, BLOCK, DHEAD), jnp.float32),
            pltpu.VMEM((64, DHEAD), jnp.float32),
            pltpu.VMEM((16, DHEAD), jnp.float32),
            pltpu.VMEM((3, BLOCK, WIDTH), jnp.float32),
            pltpu.SemaphoreType.DMA((3,)),
        ],
        compiler_params=params(),
        cost_estimate=cost(1e6, 2e6),
    )(key, value, query)


def far_forward(bias, own, far, peak, mass, summed, upstream, gain):
    return whole_call(
        far_forward_kernel,
        [f32(BLOCK, WIDTH), f32(BLOCK, WIDTH), f32(8, 256)],
        [(2, BLOCK, DHEAD)] * 3 + [(BLOCK, DHEAD)] * 2,
        BLOCK_FLOPS,
        8e6,
        bias, own, *far, peak, mass, summed, upstream, gain,
    )


def cotangent(stats, others, own, attention, lse, upstream, gain):
    return whole_call(
        cotangent_kernel,
        [f32(BLOCK, WIDTH), f32(BLOCK + 8, WIDTH), f32(BLOCK, WIDTH), f32(64, GRAD), f32(20, GRAD)],
        [(2, BLOCK, DHEAD)] * 3,
        1e6,
        4e6,
        stats, *others, own, attention, lse, upstream, gain,
    )


def far_query(bias, own, far, first, rest, near):
    (grad,) = whole_call(
        far_query_kernel,
        [f32(BLOCK, WIDTH)],
        [(2, BLOCK, DHEAD)],
        BLOCK_FLOPS,
        6e6,
        bias, own, *far, first, rest, near,
    )
    return grad


def far_key(bias, own, grads, near_dk, near_dv):
    return whole_call(
        far_key_kernel,
        [f32(BLOCK, WIDTH)] * 2,
        [(2, BLOCK, DHEAD)] * 2,
        BLOCK_FLOPS,
        6e6,
        bias, own, *grads, near_dk, near_dv,
    )


def body(query, key, value, norm_gain, upstream):
    position = lax.axis_index("seq")
    count = lax.axis_size("seq")

    def exchange(array, mask):
        return lax.ppermute(array, "seq", [(i, i ^ mask) for i in range(count)])

    def from_before(array):
        return lax.ppermute(array, "seq", [(i, i + 1) for i in range(count - 1)])

    def from_after(array):
        return lax.ppermute(array, "seq", [(i + 1, i) for i in range(count - 1)])

    head_count = lax.axis_size("head")
    gain = norm_gain.reshape(1, WIDTH)
    offset, slot_level, own_level = slot_table()
    apart = jnp.abs((position ^ offset) - position) > 1
    bias = jnp.where(apart & (slot_level == own_level), slot_level.astype(np.float32) * LN4, NEGATIVE_FILL)
    block = jnp.arange(3 * BLOCK, dtype=jnp.int32)[None, :] // BLOCK + position - 1
    edge = jnp.where((block >= 0) & (block < count), 0.0, NEGATIVE_FILL)

    def after(array, *tokens):
        return lax.optimization_barrier((array,) + tokens)[0]

    def gather(first, rest, hook, work0=None, work1=None):
        width = first.shape[1]
        quads = [exchange(rest, mask) for mask in (8, 4, 12)]
        l1a = exchange(first, 2)
        head_rest = after(rest, l1a) if work0 is None else after(rest, l1a, work0)
        (l2a,) = whole_call(merge_kernel, [f32(64, width)], [], 1e4, 1e5, head_rest, quads[1], quads[0], quads[2])
        l2b = exchange(l2a, 2)
        hook(0, l2a)
        head_l2a = l2a if work1 is None else after(l2a, work1)
        (thirds,) = whole_call(thirds_kernel, [f32(32, width)], [], 1e4, 1e5, head_l2a, l2b)
        many = [exchange(thirds, mask) for mask in (16, 32, 48)]
        l1b = exchange(after(l1a, thirds), 1)
        l2c = exchange(after(l2a, thirds), 1)
        l2d = exchange(l2b, 1)
        (l3a,) = whole_call(stack_kernel, [f32(96, width)], [], 1e4, 1e5, *many)
        l3b = exchange(l3a, 1)
        return l1a, l1b, l2a, l2b, l2c, l2d, l3a, l3b

    own, first, rest, pair, query = pool(key, value, query)
    state = {}

    def forward_hook(stage, token):
        if stage == 0:
            held = after(pair, token)
            state["kvp"], state["kvn"] = from_before(held), from_after(held)

    far = gather(first, rest, forward_hook)
    kvp, kvn = state["kvp"], state["kvn"]
    held = after(query, kvp, kvn)
    qp, qn = from_before(held), from_after(held)

    weights, peak, mass, summed = near_forward(edge, query, kvp, pair, kvn)
    attention, lse, stats = far_forward(bias, own, far, peak, mass, summed, upstream, gain)
    stats = after(stats, qp, qn)
    others = [
        lax.ppermute(stats, "head", [(i, i ^ mask) for i in range(head_count)]) for mask in range(1, head_count)
    ]
    attended, d_out, delta, g1, g23 = cotangent(stats, others, own, attention, lse, upstream, gain)
    near_dq = near_query(weights, peak, lse, delta, d_out, kvp, pair, kvn)
    query_grad = far_query(bias, own, far, g1, g23, near_dq)

    def backward_hook(stage, token):
        if stage == 0:
            held = after(d_out, token)
            state["dp"], state["dn"] = from_before(held), from_after(held)

    grads = gather(g1, g23, backward_hook, near_dq, query_grad)
    near_dk, near_dv = near_key(pair, qp, query, qn, state["dp"], d_out, state["dn"])
    key_grad, value_grad = far_key(bias, own, grads, near_dk, near_dv)
    return attended, query_grad, key_grad, value_grad


def solution(mesh):
    return jax.shard_map(
        body,
        mesh=mesh,
        in_specs=(
            P("seq", "head"),
            P("seq", "head"),
            P("seq", "head"),
            P("head"),
            P("seq", "head"),
        ),
        out_specs=(P("seq", "head"), P("seq", "head"), P("seq", "head"), P("seq", "head")),
        check_vma=False,
    )
```

```python
import math

import jax
import jax.numpy as jnp
import numpy as np
from jax import lax
from jax.experimental import pallas as pl
from jax.experimental.pallas import tpu as pltpu
from jax.sharding import PartitionSpec as P

DHEAD = 128
BLOCK = 256
FEAT = 2048
HEADS = 4
WIDTH = HEADS * DHEAD
NEGATIVE_FILL = -1e30
FLOOR = -1e25
EPSILON = 1e-06
INV_ROOT = 1.0 / math.sqrt(DHEAD)
LN4 = math.log(4.0)
VMEM_BYTES = 24 * 1024 * 1024
POOL_VMEM_BYTES = 56 * 1024 * 1024

OWN = 96
LEVEL_ROWS = ((0, 64), (64, 80), (80, 84))
FAR = 512
KV = 2 * WIDTH
GRAD = 2 * WIDTH + DHEAD

QUAD = (4, 8, 12)
PLANES = (16, 32, 48)
HALF2_BLOCKS = QUAD + tuple(2 ^ o for o in QUAD)
QUARTER3_BLOCKS = tuple(y ^ o for o in (0,) + QUAD for y in PLANES)
HALF3_BLOCKS = QUARTER3_BLOCKS + tuple(2 ^ o for o in QUARTER3_BLOCKS)
SLOTS = (
    ((2, 3), 64),
    (HALF2_BLOCKS + tuple(1 ^ o for o in HALF2_BLOCKS), 16),
    (HALF3_BLOCKS + tuple(1 ^ o for o in HALF3_BLOCKS), 4),
)


def slot_table():
    offset = np.concatenate([np.repeat(np.array(blocks, np.int32), rows) for blocks, rows in SLOTS])
    level = np.concatenate([np.full(len(blocks) * rows, n + 1, np.int32) for n, (blocks, rows) in enumerate(SLOTS)])
    table = np.zeros((8, FAR), np.int32)
    table[0], table[1] = offset, level
    return table


def split3(x):
    high = x.astype(jnp.bfloat16)
    rest = x - high.astype(jnp.float32)
    middle = rest.astype(jnp.bfloat16)
    return high, middle, (rest - middle.astype(jnp.float32)).astype(jnp.bfloat16)


def dot(a, b, dims):
    return lax.dot_general(a, b, (dims, ((), ())), preferred_element_type=jnp.float32)


def nt3(a, b):
    a1, a2, a3 = split3(a)
    b1, b2, b3 = split3(b)
    left = jnp.concatenate([a1, a2, a1, a2, a1, a3], axis=1)
    right = jnp.concatenate([b1, b1, b2, b2, b3, b1], axis=1)
    return dot(left, right, ((1,), (1,)))


def nn3(a, b):
    a1, a2, a3 = split3(a)
    b1, b2, b3 = split3(b)
    right = jnp.concatenate([b1, b2], axis=1)
    main = dot(jnp.concatenate([a1, a2], axis=1), jnp.concatenate([right, right], axis=0), ((1,), (0,)))
    small = dot(jnp.concatenate([a1, a3], axis=1), jnp.concatenate([b3, b1], axis=0), ((1,), (0,)))
    return main[:, :DHEAD] + (main[:, DHEAD:] + small)


def cols(h, base=0):
    return slice(base + h * DHEAD, base + (h + 1) * DHEAD)


def quarters(ref, value):
    rows = value.shape[0] // 4
    ref[pl.ds(0, 4 * rows), :] = value
    return [ref[pl.ds(j, rows, stride=4), :] for j in range(4)]


def mean4(ref, value):
    parts = quarters(ref, value)
    return ((parts[0] + parts[1]) + (parts[2] + parts[3])) * 0.25


def expand(ref, value):
    rows = value.shape[0]
    for j in range(4):
        ref[pl.ds(j, rows, stride=4), :] = value
    return ref[pl.ds(0, 4 * rows), :]


def expand_levels(ref, value, scales):
    total = value[80:84] * scales[2]
    total = value[64:80] * scales[1] + expand(ref, total)
    total = value[0:64] * scales[0] + expand(ref, total)
    return expand(ref, total)


def lane_index(rows):
    return lax.broadcasted_iota(jnp.int32, (rows, DHEAD), 1)


def wide(column):
    return jnp.broadcast_to(column, (column.shape[0], DHEAD))


def gathered(refs, lanes):
    l1a, l2a, l2b, core1, core2 = refs
    pieces = [l1a[:, lanes], core1[0:64, lanes]]
    pieces += [l2a[0:48, lanes], l2b[0:48, lanes], core1[64:112, lanes], core2[0:48, lanes]]
    pieces += [l2a[48:96, lanes], l2b[48:96, lanes], core1[112:160, lanes], core2[48:96, lanes]]
    return jnp.concatenate(pieces, axis=0)


def pool_kernel(
    table_ref, k_ref, v_ref, q_ref,
    own_ref, first_ref, second_ref, third_ref, trio_ref, bias_ref, edge_ref,
    e0_ref, e1_ref, e2_ref, in_ref, sems, out_sems,
):
    copies = []
    for i, ref in enumerate((k_ref, v_ref, q_ref)):
        for j in range(4):
            rows = pl.ds(64 * j, 64)
            copies.append(pltpu.make_async_copy(ref.at[rows, :], in_ref.at[i, rows, :], sems.at[i, j]))
    for copy in copies:
        copy.start()
    place = lax.axis_index("seq")
    last = lax.axis_size("seq") - 1
    offset = table_ref[0:1, :]
    level = table_ref[1:2, :]
    row = lax.broadcasted_iota(jnp.int32, (OWN, FAR), 0)
    mine = jnp.where(row < 64, 1, jnp.where(row < 80, 2, jnp.where(row < 84, 3, 0)))
    allowed = (jnp.abs((offset ^ place) - place) > 1) & (level == mine)
    bias_ref[...] = jnp.where(allowed, level.astype(jnp.float32) * LN4, NEGATIVE_FILL)
    alone = (place == 0) | (place == last)
    edge_ref[...] = jnp.full((8, BLOCK), jnp.where(alone, NEGATIVE_FILL, 0.0), jnp.float32)
    own_ref[84:96, :] = jnp.zeros((12, 3 * WIDTH), jnp.float32)
    stores = []
    for part in range(3):
        for copy in copies[4 * part : 4 * part + 4]:
            copy.wait()
        lanes = pl.ds(part * WIDTH, WIDTH)
        stores.append(pltpu.make_async_copy(in_ref.at[part], trio_ref.at[:, lanes], out_sems.at[part]))
        stores[-1].start()
        for h in range(HEADS):
            dst = cols(h, part * WIDTH)
            value = in_ref[part, :, cols(h)]
            one = mean4(e0_ref.at[(part * HEADS + h) % 2], value)
            two = mean4(e1_ref, one)
            three = mean4(e2_ref, two)
            own_ref[0:64, dst] = one
            own_ref[64:80, dst] = two
            own_ref[80:84, dst] = three
            if part < 2:
                first_ref[:, dst] = one
                second_ref[:, dst] = two
                third_ref[:, dst] = three
    for store in stores:
        store.wait()


def pack_kernel(second_ref, a_ref, b_ref, c_ref, out_ref):
    out_ref[0:16, :] = second_ref[...]
    out_ref[16:20, :] = a_ref[...]
    out_ref[20:24, :] = b_ref[...]
    out_ref[24:28, :] = c_ref[...]


def merge_kernel(first_ref, own_ref, a_ref, b_ref, c_ref, out_ref, bundle_ref):
    bundle_ref[0:64, :] = first_ref[...]
    pieces = [(16 * i, ref[0:16, :]) for i, ref in enumerate((a_ref, b_ref, c_ref))]
    pieces += [(48 + 12 * i, ref[16:28, :]) for i, ref in enumerate((own_ref, a_ref, b_ref, c_ref))]
    for start, piece in pieces:
        stop = start + piece.shape[0]
        out_ref[start:stop, :] = piece
        bundle_ref[64 + start : 64 + stop, :] = piece


def near_state(scores, values, w_ref, peak_ref, mass_ref, sum_ref):
    peak = jnp.maximum(jnp.max(scores, axis=1, keepdims=True), FLOOR)
    weights = jnp.exp(scores - peak)
    w_ref[0] = weights
    peak_ref[...] = wide(peak)
    mass_ref[...] = wide(jnp.sum(weights, axis=1, keepdims=True))
    sum_ref[...] = nn3(weights, values)


def near_inner_kernel(q_ref, ko_ref, ki_ref, vo_ref, vi_ref, *outs):
    keys = jnp.concatenate([ko_ref[...], ki_ref[...]], axis=0)
    values = jnp.concatenate([vo_ref[...], vi_ref[...]], axis=0)
    near_state(nt3(q_ref[...], keys) * INV_ROOT, values, *outs)


def near_outer_kernel(edge_ref, q_ref, k_ref, v_ref, *outs):
    near_state(nt3(q_ref[...], k_ref[...]) * INV_ROOT + edge_ref[0:1, :], v_ref[...], *outs)


def merge(one, two):
    peak = jnp.maximum(one[0], two[0])
    left = jnp.exp(one[0] - peak)
    right = jnp.exp(two[0] - peak)
    return peak, left * one[1] + right * two[1], left * one[2] + right * two[2]


def far_forward_kernel(
    bias_ref, own_ref, a0, a1, a2, a3, a4,
    peak0_ref, mass0_ref, sum0_ref, peak1_ref, mass1_ref, sum1_ref, up_ref, gain_ref,
    att_ref, lse_ref, stat_ref,
    e0_ref, e1_ref, e2_ref, square_ref, cross_ref,
):
    far = (a0, a1, a2, a3, a4)
    bias = bias_ref[...]
    for h in range(HEADS):
        k = cols(h)
        v = cols(h, WIDTH)
        scores = nt3(own_ref[:, cols(h, 2 * WIDTH)], gathered(far, k)) * INV_ROOT + bias
        peak = jnp.maximum(jnp.max(scores, axis=1, keepdims=True), FLOOR)
        weights = jnp.exp(scores - peak)
        mass = jnp.sum(weights, axis=1, keepdims=True)
        levels = (wide(peak), wide(mass), nn3(weights, gathered(far, v)))
        state = tuple(x[80:84] for x in levels)
        for start, stop in (LEVEL_ROWS[1], LEVEL_ROWS[0]):
            state = tuple(expand(ref.at[h % 2], x) for ref, x in zip((e0_ref, e1_ref, e2_ref), state))
            state = merge(state, tuple(x[start:stop] for x in levels))
        state = tuple(expand(ref.at[h % 2], x) for ref, x in zip((e0_ref, e1_ref, e2_ref), state))
        near = merge(
            (peak0_ref[:, k], mass0_ref[:, k], sum0_ref[:, k]), (peak1_ref[:, k], mass1_ref[:, k], sum1_ref[:, k])
        )
        state = merge(state, near)
        attention = state[2] / state[1]
        att_ref[:, k] = attention
        lse_ref[:, k] = state[0] + jnp.log(state[1])
        square = attention * attention
        cross = up_ref[:, k] * gain_ref[0:1, k] * attention
        if h == 0:
            square_ref[...] = square
            cross_ref[...] = cross
        else:
            square_ref[...] += square
            cross_ref[...] += cross
    square = wide(jnp.sum(square_ref[...], axis=1, keepdims=True))
    cross = wide(jnp.sum(cross_ref[...], axis=1, keepdims=True))
    packed = jnp.where(lane_index(BLOCK) == 0, square, cross)
    stat_ref[...] = jnp.transpose(packed)[0:8, :]


def pooled_cotangent(scratch, lows, dots, grads):
    lows, dots, grads = (quarters(ref, x) for ref, x in zip(scratch, (lows, dots, grads)))
    low = jnp.minimum(jnp.minimum(lows[0], lows[1]), jnp.minimum(lows[2], lows[3]))
    scale = [jnp.exp(low - x) for x in lows]
    total = scale[0] * dots[0]
    grad = scale[0] * grads[0]
    for j in range(1, 4):
        total = total + scale[j] * dots[j]
        grad = grad + scale[j] * grads[j]
    return low, total, grad


def cotangent_kernel(
    s0_ref, s1_ref, s2_ref, s3_ref, own_ref, att_ref, lse_ref, up_ref, gain_ref,
    out_ref, dout_ref, delta_ref, first_ref, second_ref, third_ref,
    e0_ref, e1_ref, e2_ref,
):
    total = (s0_ref[...] + s1_ref[...]) + (s2_ref[...] + s3_ref[...])
    square = jnp.transpose(jnp.broadcast_to(total[0:1, :], (DHEAD, BLOCK)))
    cross = jnp.transpose(jnp.broadcast_to(total[1:2, :], (DHEAD, BLOCK)))
    inverse = lax.rsqrt(square / FEAT + EPSILON)
    pull = inverse * inverse * inverse * cross / FEAT
    lane = lane_index(BLOCK)
    packed = jnp.zeros((BLOCK, DHEAD), jnp.float32)
    stats = [jnp.zeros((rows, DHEAD), jnp.float32) for rows in (64, 16, 4)]
    first_ref[:, WIDTH:KV] = own_ref[0:64, KV:]
    second_ref[:, WIDTH:KV] = own_ref[64:80, KV:]
    third_ref[:, WIDTH:KV] = own_ref[80:84, KV:]
    for h in range(HEADS):
        k = cols(h)
        attention = att_ref[:, k]
        out_ref[:, k] = attention * inverse * gain_ref[0:1, k]
        d_out = inverse * (up_ref[:, k] * gain_ref[0:1, k]) - attention * pull
        dout_ref[0:BLOCK, k] = d_out
        delta = wide(jnp.sum(d_out * attention, axis=1, keepdims=True))
        delta_ref[:, k] = delta
        packed = jnp.where(lane == h, lse_ref[:, k], packed)
        packed = jnp.where(lane == HEADS + h, delta, packed)
        level = (lse_ref[:, k], delta, d_out)
        for n, ref in enumerate((first_ref, second_ref, third_ref)):
            level = pooled_cotangent([e.at[h % 2] for e in (e0_ref, e1_ref, e2_ref)], *level)
            rows = level[0].shape[0]
            ref[:, k] = level[2]
            short = lane[0:rows]
            stats[n] = jnp.where(short == h, level[0], jnp.where(short == HEADS + h, level[1], stats[n]))
    first_ref[:, KV:] = stats[0]
    second_ref[:, KV:] = stats[1]
    third_ref[:, KV:] = stats[2]
    dout_ref[BLOCK:, 0:256] = jnp.transpose(packed)[0:8, :]
    dout_ref[BLOCK:, 256:] = jnp.zeros((8, 256), jnp.float32)


def near_query_kernel(
    w0_ref, w1_ref, peak0_ref, peak1_ref, lse_ref, delta_ref, dout_ref,
    k0_ref, k1_ref, k2_ref, v0_ref, v1_ref, v2_ref, dq_ref,
):
    keys = jnp.concatenate([k0_ref[...], k1_ref[...], k2_ref[...]], axis=0)
    values = jnp.concatenate([v0_ref[...], v1_ref[...], v2_ref[...]], axis=0)
    lse = lse_ref[:, 0:1]
    inner = w0_ref[0] * jnp.exp(peak0_ref[:, 0:1] - lse)
    outer = w1_ref[0] * jnp.exp(peak1_ref[:, 0:1] - lse)
    weights = jnp.concatenate([inner, outer], axis=1)
    d_scores = weights * (nt3(dout_ref[...], values) - delta_ref[:, 0:1])
    dq_ref[...] = nn3(d_scores, keys) * INV_ROOT


def far_query_kernel(
    bias_ref, own_ref, a0, a1, a2, a3, a4, first_ref, second_ref, third_ref, near_ref, dq_ref, e0_ref
):
    far = (a0, a1, a2, a3, a4)
    bias = bias_ref[...]

    def grads(lanes):
        fill = jnp.zeros((12, DHEAD), jnp.float32)
        return jnp.concatenate([first_ref[:, lanes], second_ref[:, lanes], third_ref[:, lanes], fill], axis=0)

    stats = grads(slice(KV, GRAD))
    for h in range(HEADS):
        k = cols(h)
        keys = gathered(far, k)
        scores = nt3(own_ref[:, cols(h, 2 * WIDTH)], keys) * INV_ROOT + bias
        weights = jnp.exp(scores - stats[:, h : h + 1])
        d_probs = nt3(grads(k), gathered(far, cols(h, WIDTH)))
        d_scores = weights * (d_probs - stats[:, HEADS + h : HEADS + h + 1])
        grad = nn3(d_scores, keys)
        scales = [INV_ROOT / 4**n for n in (1, 2, 3)]
        dq_ref[:, k] = near_ref[:, k] + expand_levels(e0_ref.at[h % 2], grad, scales)


def near_key_parts(k_ref, v_ref, queries, grads, stats):
    h = pl.program_id(0)
    low = jnp.concatenate([ref[pl.ds(h, 1), :] for ref in stats], axis=1)
    total = jnp.concatenate([ref[pl.ds(h + HEADS, 1), :] for ref in stats], axis=1)
    weights = jnp.exp(nt3(k_ref[...], queries) * INV_ROOT - low)
    d_scores = weights * (nt3(v_ref[...], grads) - total)
    return nn3(d_scores, queries) * INV_ROOT, nn3(weights, grads)


def inner_key_kernel(k_ref, v_ref, q0_ref, q1_ref, d0_ref, d1_ref, t0_ref, t1_ref, dk_ref, dv_ref):
    queries = jnp.concatenate([q0_ref[...], q1_ref[...]], axis=0)
    grads = jnp.concatenate([d0_ref[...], d1_ref[...]], axis=0)
    dk_ref[...], dv_ref[...] = near_key_parts(k_ref, v_ref, queries, grads, (t0_ref, t1_ref))


def outer_key_kernel(k_ref, v_ref, q_ref, d_ref, t_ref, dk_in_ref, dv_in_ref, dk_ref, dv_ref):
    d_keys, d_values = near_key_parts(k_ref, v_ref, q_ref[...], d_ref[...], (t_ref,))
    dk_ref[...] = dk_in_ref[...] + d_keys
    dv_ref[...] = dv_in_ref[...] + d_values


def far_key_kernel(
    bias_ref, own_ref, a0, a1, a2, a3, a4, dk_in_ref, dv_in_ref, dk_ref, dv_ref, e0_ref, e1_ref
):
    far = (a0, a1, a2, a3, a4)
    bias = bias_ref[...]
    stats = jnp.transpose(gathered(far, slice(KV, GRAD)))[0:8, :]
    for h in range(HEADS):
        k = cols(h)
        queries = gathered(far, cols(h, WIDTH))
        grads = gathered(far, k)
        scores = nt3(own_ref[:, k], queries) * INV_ROOT + bias
        weights = jnp.exp(scores - stats[h : h + 1, :])
        d_scores = weights * (nt3(own_ref[:, cols(h, WIDTH)], grads) - stats[HEADS + h : HEADS + h + 1, :])
        scales = [1.0 / 4**n for n in (1, 2, 3)]
        d_keys = nn3(d_scores, queries) * INV_ROOT
        dk_ref[:, k] = dk_in_ref[:, k] + expand_levels(e0_ref.at[h % 2], d_keys, scales)
        dv_ref[:, k] = dv_in_ref[:, k] + expand_levels(e1_ref.at[h % 2], nn3(weights, grads), scales)


def f32(*shape):
    return jax.ShapeDtypeStruct(shape, jnp.float32)


def params():
    return pltpu.CompilerParams(vmem_limit_bytes=VMEM_BYTES)


def cost(flops, size):
    return pl.CostEstimate(flops=int(flops), bytes_accessed=int(size), transcendentals=0)


def whole_call(kernel, outs, scratch, flops, size, *operands):
    spec = pl.BlockSpec(memory_space=pltpu.VMEM)
    return pl.pallas_call(
        kernel,
        out_shape=outs,
        in_specs=[spec] * len(operands),
        out_specs=[spec] * len(outs),
        scratch_shapes=[pltpu.VMEM(shape, jnp.float32) for shape in scratch],
        compiler_params=params(),
        cost_estimate=cost(flops, size),
    )(*operands)


BLOCK_FLOPS = 2.0 * BLOCK * BLOCK * DHEAD * HEADS * 6


def column_at(first):
    return pl.BlockSpec((BLOCK, DHEAD), lambda h: (0, first + h))


def slab(blocks):
    return pl.BlockSpec((1, BLOCK, blocks * BLOCK), lambda h: (h, 0, 0))


def head_call(kernel, outs, out_specs, in_specs, blocks, *operands):
    return pl.pallas_call(
        kernel,
        grid=(HEADS,),
        out_shape=outs,
        in_specs=in_specs,
        out_specs=out_specs,
        compiler_params=params(),
        cost_estimate=cost(blocks * BLOCK_FLOPS, 4e6),
    )(*operands)


def near_inner(trio, inn):
    k, v, q = column_at(0), column_at(HEADS), column_at(2 * HEADS)
    outs = [f32(HEADS, BLOCK, 2 * BLOCK)] + [f32(BLOCK, WIDTH)] * 3
    return head_call(near_inner_kernel, outs, [slab(2), k, k, k], [q, k, k, v, v], 4, trio, trio, inn, trio, inn)


def near_outer(edge, trio, out):
    k, v, q = column_at(0), column_at(HEADS), column_at(2 * HEADS)
    outs = [f32(HEADS, BLOCK, BLOCK)] + [f32(BLOCK, WIDTH)] * 3
    edge_spec = pl.BlockSpec((8, BLOCK), lambda h: (0, 0))
    return head_call(near_outer_kernel, outs, [slab(1), k, k, k], [edge_spec, q, k, v], 2, edge, trio, out, out)


def near_query(w0, w1, peak0, peak1, lse, delta, d_out, trio, inn, out):
    k, v = column_at(0), column_at(HEADS)
    specs = [slab(2), slab(1)] + [k] * 8 + [v] * 3
    return head_call(
        near_query_kernel, f32(BLOCK, WIDTH), k, specs, 6,
        w0, w1, peak0, peak1, lse, delta, d_out, trio, inn, out, trio, inn, out,
    )


def stat_rows():
    return pl.BlockSpec((8, 256), lambda h: (BLOCK // 8, 0))


def inner_key(trio, inn, d_out, d_in):
    k, v, q, t = column_at(0), column_at(HEADS), column_at(2 * HEADS), stat_rows()
    return head_call(
        inner_key_kernel, [f32(BLOCK, WIDTH)] * 2, [k, k], [k, v, q, q, k, k, t, t], 8,
        trio, trio, trio, inn, d_out, d_in, d_out, d_in,
    )


def outer_key(trio, out, d_far, dk, dv):
    k, v, q, t = column_at(0), column_at(HEADS), column_at(2 * HEADS), stat_rows()
    return head_call(
        outer_key_kernel, [f32(BLOCK, WIDTH)] * 2, [k, k], [k, v, q, k, t, k, k], 4,
        trio, trio, out, d_far, d_far, dk, dv,
    )


def pool(key, value, query):
    vmem = pl.BlockSpec(memory_space=pltpu.VMEM)
    hbm = pl.BlockSpec(memory_space=pltpu.HBM)
    return pl.pallas_call(
        pool_kernel,
        out_shape=[
            f32(OWN, 3 * WIDTH), f32(64, KV), f32(16, KV), f32(4, KV), f32(BLOCK, 3 * WIDTH), f32(OWN, FAR), f32(8, BLOCK),
        ],
        in_specs=[vmem] + [hbm] * 3,
        out_specs=[vmem] * 4 + [hbm] + [vmem] * 2,
        scratch_shapes=[
            pltpu.VMEM((2, BLOCK, DHEAD), jnp.float32),
            pltpu.VMEM((64, DHEAD), jnp.float32),
            pltpu.VMEM((16, DHEAD), jnp.float32),
            pltpu.VMEM((3, BLOCK, WIDTH), jnp.float32),
            pltpu.SemaphoreType.DMA((3, 4)),
            pltpu.SemaphoreType.DMA((3,)),
        ],
        compiler_params=pltpu.CompilerParams(vmem_limit_bytes=POOL_VMEM_BYTES),
        cost_estimate=cost(1e6, 2e6),
    )(jnp.asarray(slot_table()), key, value, query)


def far_forward(bias, own, far, inner, outer, upstream, gain):
    return whole_call(
        far_forward_kernel,
        [f32(BLOCK, WIDTH), f32(BLOCK, WIDTH), f32(8, 256)],
        [(2, BLOCK, DHEAD)] * 3 + [(BLOCK, DHEAD)] * 2,
        BLOCK_FLOPS,
        8e6,
        bias, own, *far, *inner, *outer, upstream, gain,
    )


def cotangent(stats, others, own, attention, lse, upstream, gain):
    return whole_call(
        cotangent_kernel,
        [f32(BLOCK, WIDTH), f32(BLOCK + 8, WIDTH), f32(BLOCK, WIDTH), f32(64, GRAD), f32(16, GRAD), f32(4, GRAD)],
        [(2, BLOCK, DHEAD)] * 3,
        1e6,
        4e6,
        stats, *others, own, attention, lse, upstream, gain,
    )


def far_query(bias, own, far, first, second, third, near):
    (grad,) = whole_call(
        far_query_kernel,
        [f32(BLOCK, WIDTH)],
        [(2, BLOCK, DHEAD)],
        BLOCK_FLOPS,
        6e6,
        bias, own, *far, first, second, third, near,
    )
    return grad


def far_key(bias, own, grads, near_dk, near_dv):
    return whole_call(
        far_key_kernel,
        [f32(BLOCK, WIDTH)] * 2,
        [(2, BLOCK, DHEAD)] * 2,
        BLOCK_FLOPS,
        6e6,
        bias, own, *grads, near_dk, near_dv,
    )


def body(query, key, value, norm_gain, upstream):
    count = lax.axis_size("seq")
    head_count = lax.axis_size("head")

    def exchange(array, mask):
        return lax.ppermute(array, "seq", [(i, i ^ mask) for i in range(count)])

    def exchange_outer(array):
        pairs = [(i, i + 1 if i % 2 else i - 1) for i in range(1, count - 1)]
        return lax.ppermute(array, "seq", pairs)

    def after(array, *tokens):
        return lax.optimization_barrier((array,) + tokens)[0]

    def packed(second, thirds):
        return whole_call(pack_kernel, [f32(28, second.shape[1])], [], 1e4, 1e5, second, *thirds)[0]

    def merged(first, pack, quads):
        width = first.shape[1]
        return whole_call(merge_kernel, [f32(96, width), f32(160, width)], [], 1e4, 1e5, first, pack, *quads)

    gain = norm_gain.reshape(1, WIDTH)
    own, first, second, third, trio, bias, edge = pool(key, value, query)

    planes = [exchange(third, mask) for mask in PLANES]
    l1a = exchange(first, 2)
    inn = exchange(trio, 1)
    pack = packed(second, planes)
    quads = [exchange(pack, mask) for mask in QUAD]
    out = exchange_outer(after(trio, pack))
    w0, *inner = near_inner(trio, inn)
    l2a, bundle = merged(l1a, after(pack, w0), quads)
    l2b = exchange(l2a, 2)
    core1 = exchange(bundle, 1)
    core2 = exchange(l2b, 1)
    w1, *outer = near_outer(edge, trio, out)
    far = (l1a, l2a, l2b, core1, core2)
    attention, lse, stats = far_forward(bias, own, far, inner, outer, upstream, gain)

    others = [
        lax.ppermute(stats, "head", [(i, i ^ mask) for i in range(head_count)]) for mask in range(1, head_count)
    ]
    attended, d_out, delta, g1, g2, g3 = cotangent(stats, others, own, attention, lse, upstream, gain)

    planes = [exchange(g3, mask) for mask in PLANES]
    l1a = exchange(g1, 2)
    d_in = exchange(d_out, 1)
    pack = packed(g2, planes)
    quads = [exchange(pack, mask) for mask in QUAD]
    near_dq = near_query(w0, w1, inner[0], outer[0], lse, delta, after(d_out, pack), trio, inn, out)
    near_dk, near_dv = inner_key(trio, inn, d_out, d_in)
    l2a, bundle = merged(l1a, after(pack, near_dq, near_dk), quads)
    l2b = exchange(l2a, 2)
    core1 = exchange(bundle, 1)
    d_far = exchange_outer(after(d_out, l2a))
    query_grad = far_query(bias, own, far, g1, g2, g3, near_dq)
    core2 = exchange(after(l2b, query_grad), 1)
    near_dk, near_dv = outer_key(trio, out, d_far, near_dk, near_dv)
    key_grad, value_grad = far_key(bias, own, (l1a, l2a, l2b, core1, core2), near_dk, near_dv)
    return attended, query_grad, key_grad, value_grad


def solution(mesh):
    return jax.shard_map(
        body,
        mesh=mesh,
        in_specs=(
            P("seq", "head"),
            P("seq", "head"),
            P("seq", "head"),
            P("head"),
            P("seq", "head"),
        ),
        out_specs=(P("seq", "head"), P("seq", "head"), P("seq", "head"), P("seq", "head")),
        check_vma=False,
    )
```

```python
import math

import jax
import jax.numpy as jnp
import numpy as np
from jax import lax
from jax.experimental import pallas as pl
from jax.experimental.pallas import tpu as pltpu
from jax.sharding import PartitionSpec as P

DHEAD = 128
BLOCK = 256
FEAT = 2048
HEADS = 4
WIDTH = HEADS * DHEAD
NEGATIVE_FILL = -1e30
FLOOR = -1e25
EPSILON = 1e-06
INV_ROOT = 1.0 / math.sqrt(DHEAD)
LN4 = math.log(4.0)
VMEM_BYTES = 24 * 1024 * 1024
POOL_VMEM_BYTES = 56 * 1024 * 1024

OWN = 96
LEVEL_ROWS = ((0, 64), (64, 80), (80, 84))
FAR = 512
KV = 2 * WIDTH
GRAD = 2 * WIDTH + DHEAD

QUAD = (4, 12, 8)
PLANES = (16, 32, 48)
THIRD_BLOCKS = tuple(y ^ o for o in (0,) + QUAD for y in PLANES)


def flipped(blocks, mask):
    return tuple(o ^ mask for o in blocks)


SLOTS = (
    (1, (2, 3)),
    (2, QUAD),
    (2, flipped(QUAD, 1)),
    (3, THIRD_BLOCKS),
    (3, flipped(THIRD_BLOCKS, 1)),
    (2, flipped(QUAD, 2)),
    (2, flipped(QUAD, 3)),
    (3, flipped(THIRD_BLOCKS, 2)),
    (3, flipped(THIRD_BLOCKS, 3)),
)
EARLY = 320


def slot_table():
    rows = {1: 64, 2: 16, 3: 4}
    offset = np.concatenate([np.repeat(np.array(blocks, np.int32), rows[n]) for n, blocks in SLOTS])
    level = np.concatenate([np.full(len(blocks) * rows[n], n, np.int32) for n, blocks in SLOTS])
    table = np.zeros((8, FAR), np.int32)
    table[0], table[1] = offset, level
    return table


def split3(x):
    high = x.astype(jnp.bfloat16)
    rest = x - high.astype(jnp.float32)
    middle = rest.astype(jnp.bfloat16)
    return high, middle, (rest - middle.astype(jnp.float32)).astype(jnp.bfloat16)


def dot(a, b, dims):
    return lax.dot_general(a, b, (dims, ((), ())), preferred_element_type=jnp.float32)


def nt3(a, b):
    a1, a2, a3 = split3(a)
    b1, b2, b3 = split3(b)
    left = jnp.concatenate([a1, a2, a1, a2, a1, a3], axis=1)
    right = jnp.concatenate([b1, b1, b2, b2, b3, b1], axis=1)
    return dot(left, right, ((1,), (1,)))


def nn3(a, b):
    a1, a2, a3 = split3(a)
    b1, b2, b3 = split3(b)
    right = jnp.concatenate([b1, b2], axis=1)
    main = dot(jnp.concatenate([a1, a2], axis=1), jnp.concatenate([right, right], axis=0), ((1,), (0,)))
    small = dot(jnp.concatenate([a1, a3], axis=1), jnp.concatenate([b3, b1], axis=0), ((1,), (0,)))
    return main[:, :DHEAD] + (main[:, DHEAD:] + small)


def cols(h, base=0):
    return slice(base + h * DHEAD, base + (h + 1) * DHEAD)


def quarters(ref, value):
    rows = value.shape[0] // 4
    ref[pl.ds(0, 4 * rows), :] = value
    return [ref[pl.ds(j, rows, stride=4), :] for j in range(4)]


def mean4(ref, value):
    parts = quarters(ref, value)
    return ((parts[0] + parts[1]) + (parts[2] + parts[3])) * 0.25


def expand(ref, value):
    rows = value.shape[0]
    for j in range(4):
        ref[pl.ds(j, rows, stride=4), :] = value
    return ref[pl.ds(0, 4 * rows), :]


def expand_levels(ref, value, scales):
    total = value[80:84] * scales[2]
    total = value[64:80] * scales[1] + expand(ref, total)
    total = value[0:64] * scales[0] + expand(ref, total)
    return expand(ref, total)


def lane_index(rows):
    return lax.broadcasted_iota(jnp.int32, (rows, DHEAD), 1)


def wide(column):
    return jnp.broadcast_to(column, (column.shape[0], DHEAD))


def early(refs, lanes):
    l1a, l2a, core1 = refs
    pieces = [l1a[:, lanes], core1[0:64, lanes], l2a[0:48, lanes], core1[64:112, lanes]]
    return pieces + [l2a[48:96, lanes], core1[112:160, lanes]]


def late(refs, lanes):
    l2b, core2 = refs
    return [l2b[0:48, lanes], core2[0:48, lanes], l2b[48:96, lanes], core2[48:96, lanes]]


def gathered(refs, lanes):
    return jnp.concatenate(early(refs[0:3], lanes) + late(refs[3:5], lanes), axis=0)


def pool_kernel(
    table_ref, k_ref, v_ref, q_ref,
    own_ref, first_ref, second_ref, third_ref, bias_ref, edge_ref,
    e0_ref, e1_ref, e2_ref, in_ref, sems,
):
    copies = []
    for i, ref in enumerate((k_ref, v_ref, q_ref)):
        for j in range(4):
            rows = pl.ds(64 * j, 64)
            copies.append(pltpu.make_async_copy(ref.at[rows, :], in_ref.at[i, rows, :], sems.at[i, j]))
    for copy in copies:
        copy.start()
    place = lax.axis_index("seq")
    last = lax.axis_size("seq") - 1
    offset = table_ref[0:1, :]
    level = table_ref[1:2, :]
    row = lax.broadcasted_iota(jnp.int32, (OWN, FAR), 0)
    mine = jnp.where(row < 64, 1, jnp.where(row < 80, 2, jnp.where(row < 84, 3, 0)))
    allowed = (jnp.abs((offset ^ place) - place) > 1) & (level == mine)
    bias_ref[...] = jnp.where(allowed, level.astype(jnp.float32) * LN4, NEGATIVE_FILL)
    alone = (place == 0) | (place == last)
    edge_ref[...] = jnp.full((8, BLOCK), jnp.where(alone, NEGATIVE_FILL, 0.0), jnp.float32)
    own_ref[84:96, :] = jnp.zeros((12, 3 * WIDTH), jnp.float32)
    for part in range(3):
        for copy in copies[4 * part : 4 * part + 4]:
            copy.wait()
        for h in range(HEADS):
            dst = cols(h, part * WIDTH)
            value = in_ref[part, :, cols(h)]
            one = mean4(e0_ref.at[(part * HEADS + h) % 2], value)
            two = mean4(e1_ref, one)
            three = mean4(e2_ref, two)
            own_ref[0:64, dst] = one
            own_ref[64:80, dst] = two
            own_ref[80:84, dst] = three
            if part < 2:
                first_ref[:, dst] = one
                second_ref[:, dst] = two
                third_ref[:, dst] = three


def pack_kernel(second_ref, a_ref, b_ref, c_ref, out_ref):
    out_ref[0:16, :] = second_ref[...]
    out_ref[16:20, :] = a_ref[...]
    out_ref[20:24, :] = b_ref[...]
    out_ref[24:28, :] = c_ref[...]


def double_kernel(own_ref, other_ref, out_ref):
    out_ref[0:28, :] = own_ref[...]
    out_ref[28:56, :] = other_ref[...]


def merge_kernel(first_ref, double_ref, other_ref, out_ref, bundle_ref):
    bundle_ref[0:64, :] = first_ref[...]
    parts = (double_ref[28:56, :], other_ref[0:28, :], other_ref[28:56, :])
    pieces = [(16 * i, part[0:16]) for i, part in enumerate(parts)]
    pieces += [(48 + 12 * i, part[16:28]) for i, part in enumerate((double_ref[0:28, :],) + parts)]
    for start, piece in pieces:
        stop = start + piece.shape[0]
        out_ref[start:stop, :] = piece
        bundle_ref[64 + start : 64 + stop, :] = piece


def near_state(scores, values, w_ref, peak_ref, mass_ref, sum_ref):
    peak = jnp.maximum(jnp.max(scores, axis=1, keepdims=True), FLOOR)
    weights = jnp.exp(scores - peak)
    w_ref[0] = weights
    peak_ref[...] = wide(peak)
    mass_ref[...] = wide(jnp.sum(weights, axis=1, keepdims=True))
    sum_ref[...] = nn3(weights, values)


def near_inner_kernel(q_ref, ko_ref, ki_ref, vo_ref, vi_ref, *outs):
    keys = jnp.concatenate([ko_ref[...], ki_ref[...]], axis=0)
    values = jnp.concatenate([vo_ref[...], vi_ref[...]], axis=0)
    near_state(nt3(q_ref[...], keys) * INV_ROOT, values, *outs)


def near_outer_kernel(edge_ref, q_ref, k_ref, v_ref, *outs):
    near_state(nt3(q_ref[...], k_ref[...]) * INV_ROOT + edge_ref[0:1, :], v_ref[...], *outs)


def merge(one, two):
    peak = jnp.maximum(one[0], two[0])
    left = jnp.exp(one[0] - peak)
    right = jnp.exp(two[0] - peak)
    return peak, left * one[1] + right * two[1], left * one[2] + right * two[2]


def far_forward_kernel(
    bias_ref, own_ref, a0, a1, a2, a3, a4,
    peak0_ref, mass0_ref, sum0_ref, peak1_ref, mass1_ref, sum1_ref, up_ref, gain_ref,
    att_ref, lse_ref, stat_ref,
    e0_ref, e1_ref, e2_ref, square_ref, cross_ref,
):
    far = (a0, a1, a2, a3, a4)
    bias = bias_ref[...]
    for h in range(HEADS):
        k = cols(h)
        v = cols(h, WIDTH)
        scores = nt3(own_ref[:, cols(h, 2 * WIDTH)], gathered(far, k)) * INV_ROOT + bias
        peak = jnp.maximum(jnp.max(scores, axis=1, keepdims=True), FLOOR)
        weights = jnp.exp(scores - peak)
        mass = jnp.sum(weights, axis=1, keepdims=True)
        levels = (wide(peak), wide(mass), nn3(weights, gathered(far, v)))
        state = tuple(x[80:84] for x in levels)
        for start, stop in (LEVEL_ROWS[1], LEVEL_ROWS[0]):
            state = tuple(expand(ref.at[h % 2], x) for ref, x in zip((e0_ref, e1_ref, e2_ref), state))
            state = merge(state, tuple(x[start:stop] for x in levels))
        state = tuple(expand(ref.at[h % 2], x) for ref, x in zip((e0_ref, e1_ref, e2_ref), state))
        near = merge(
            (peak0_ref[:, k], mass0_ref[:, k], sum0_ref[:, k]), (peak1_ref[:, k], mass1_ref[:, k], sum1_ref[:, k])
        )
        state = merge(state, near)
        attention = state[2] / state[1]
        att_ref[:, k] = attention
        lse_ref[:, k] = state[0] + jnp.log(state[1])
        square = attention * attention
        cross = up_ref[:, k] * gain_ref[0:1, k] * attention
        if h == 0:
            square_ref[...] = square
            cross_ref[...] = cross
        else:
            square_ref[...] += square
            cross_ref[...] += cross
    square = wide(jnp.sum(square_ref[...], axis=1, keepdims=True))
    cross = wide(jnp.sum(cross_ref[...], axis=1, keepdims=True))
    packed = jnp.where(lane_index(BLOCK) == 0, square, cross)
    stat_ref[...] = jnp.transpose(packed)[0:8, :]


def pooled_cotangent(scratch, lows, dots, grads):
    lows, dots, grads = (quarters(ref, x) for ref, x in zip(scratch, (lows, dots, grads)))
    low = jnp.minimum(jnp.minimum(lows[0], lows[1]), jnp.minimum(lows[2], lows[3]))
    scale = [jnp.exp(low - x) for x in lows]
    total = scale[0] * dots[0]
    grad = scale[0] * grads[0]
    for j in range(1, 4):
        total = total + scale[j] * dots[j]
        grad = grad + scale[j] * grads[j]
    return low, total, grad


def cotangent_kernel(
    s0_ref, s1_ref, s2_ref, s3_ref, own_ref, att_ref, lse_ref, up_ref, gain_ref,
    out_ref, dout_ref, delta_ref, first_ref, second_ref, third_ref,
    e0_ref, e1_ref, e2_ref,
):
    total = (s0_ref[...] + s1_ref[...]) + (s2_ref[...] + s3_ref[...])
    square = jnp.transpose(jnp.broadcast_to(total[0:1, :], (DHEAD, BLOCK)))
    cross = jnp.transpose(jnp.broadcast_to(total[1:2, :], (DHEAD, BLOCK)))
    inverse = lax.rsqrt(square / FEAT + EPSILON)
    pull = inverse * inverse * inverse * cross / FEAT
    lane = lane_index(BLOCK)
    packed = jnp.zeros((BLOCK, DHEAD), jnp.float32)
    stats = [jnp.zeros((rows, DHEAD), jnp.float32) for rows in (64, 16, 4)]
    first_ref[:, WIDTH:KV] = own_ref[0:64, KV:]
    second_ref[:, WIDTH:KV] = own_ref[64:80, KV:]
    third_ref[:, WIDTH:KV] = own_ref[80:84, KV:]
    for h in range(HEADS):
        k = cols(h)
        attention = att_ref[:, k]
        out_ref[:, k] = attention * inverse * gain_ref[0:1, k]
        d_out = inverse * (up_ref[:, k] * gain_ref[0:1, k]) - attention * pull
        dout_ref[0:BLOCK, k] = d_out
        delta = wide(jnp.sum(d_out * attention, axis=1, keepdims=True))
        delta_ref[:, k] = delta
        packed = jnp.where(lane == h, lse_ref[:, k], packed)
        packed = jnp.where(lane == HEADS + h, delta, packed)
        level = (lse_ref[:, k], delta, d_out)
        for n, ref in enumerate((first_ref, second_ref, third_ref)):
            level = pooled_cotangent([e.at[h % 2] for e in (e0_ref, e1_ref, e2_ref)], *level)
            rows = level[0].shape[0]
            ref[:, k] = level[2]
            short = lane[0:rows]
            stats[n] = jnp.where(short == h, level[0], jnp.where(short == HEADS + h, level[1], stats[n]))
    first_ref[:, KV:] = stats[0]
    second_ref[:, KV:] = stats[1]
    third_ref[:, KV:] = stats[2]
    dout_ref[BLOCK:, 0:256] = jnp.transpose(packed)[0:8, :]
    dout_ref[BLOCK:, 256:] = jnp.zeros((8, 256), jnp.float32)


def near_query_kernel(
    w0_ref, w1_ref, peak0_ref, peak1_ref, lse_ref, delta_ref, dout_ref,
    k0_ref, k1_ref, k2_ref, v0_ref, v1_ref, v2_ref, dq_ref,
):
    keys = jnp.concatenate([k0_ref[...], k1_ref[...], k2_ref[...]], axis=0)
    values = jnp.concatenate([v0_ref[...], v1_ref[...], v2_ref[...]], axis=0)
    lse = lse_ref[:, 0:1]
    inner = w0_ref[0] * jnp.exp(peak0_ref[:, 0:1] - lse)
    outer = w1_ref[0] * jnp.exp(peak1_ref[:, 0:1] - lse)
    weights = jnp.concatenate([inner, outer], axis=1)
    d_scores = weights * (nt3(dout_ref[...], values) - delta_ref[:, 0:1])
    dq_ref[...] = nn3(d_scores, keys) * INV_ROOT


def far_query_kernel(
    bias_ref, own_ref, a0, a1, a2, a3, a4, first_ref, second_ref, third_ref, near_ref, dq_ref, e0_ref
):
    far = (a0, a1, a2, a3, a4)
    bias = bias_ref[...]

    def grads(lanes):
        fill = jnp.zeros((12, DHEAD), jnp.float32)
        return jnp.concatenate([first_ref[:, lanes], second_ref[:, lanes], third_ref[:, lanes], fill], axis=0)

    stats = grads(slice(KV, GRAD))
    for h in range(HEADS):
        k = cols(h)
        keys = gathered(far, k)
        scores = nt3(own_ref[:, cols(h, 2 * WIDTH)], keys) * INV_ROOT + bias
        weights = jnp.exp(scores - stats[:, h : h + 1])
        d_probs = nt3(grads(k), gathered(far, cols(h, WIDTH)))
        d_scores = weights * (d_probs - stats[:, HEADS + h : HEADS + h + 1])
        grad = nn3(d_scores, keys)
        scales = [INV_ROOT / 4**n for n in (1, 2, 3)]
        dq_ref[:, k] = near_ref[:, k] + expand_levels(e0_ref.at[h % 2], grad, scales)


def near_key_parts(k_ref, v_ref, queries, grads, stats):
    h = pl.program_id(0)
    low = jnp.concatenate([ref[pl.ds(h, 1), :] for ref in stats], axis=1)
    total = jnp.concatenate([ref[pl.ds(h + HEADS, 1), :] for ref in stats], axis=1)
    weights = jnp.exp(nt3(k_ref[...], queries) * INV_ROOT - low)
    d_scores = weights * (nt3(v_ref[...], grads) - total)
    return nn3(d_scores, queries) * INV_ROOT, nn3(weights, grads)


def inner_key_kernel(k_ref, v_ref, q0_ref, q1_ref, d0_ref, d1_ref, t0_ref, t1_ref, dk_ref, dv_ref):
    queries = jnp.concatenate([q0_ref[...], q1_ref[...]], axis=0)
    grads = jnp.concatenate([d0_ref[...], d1_ref[...]], axis=0)
    dk_ref[...], dv_ref[...] = near_key_parts(k_ref, v_ref, queries, grads, (t0_ref, t1_ref))


def outer_key_kernel(k_ref, v_ref, q_ref, d_ref, t_ref, dk_in_ref, dv_in_ref, dk_ref, dv_ref):
    d_keys, d_values = near_key_parts(k_ref, v_ref, q_ref[...], d_ref[...], (t_ref,))
    dk_ref[...] = dk_in_ref[...] + d_keys
    dv_ref[...] = dv_in_ref[...] + d_values


def far_key_parts(own_ref, bias, pieces, h):
    def take(lanes):
        return jnp.concatenate(pieces(lanes), axis=0)

    stats = take(slice(KV, GRAD))
    fill = jnp.zeros((64, DHEAD), jnp.float32)
    stats = jnp.transpose(jnp.concatenate([stats, fill], axis=0))[0:8, 0 : stats.shape[0]]
    queries = take(cols(h, WIDTH))
    grads = take(cols(h))
    scores = nt3(own_ref[:, cols(h)], queries) * INV_ROOT + bias
    weights = jnp.exp(scores - stats[h : h + 1, :])
    d_scores = weights * (nt3(own_ref[:, cols(h, WIDTH)], grads) - stats[HEADS + h : HEADS + h + 1, :])
    return nn3(d_scores, queries) * INV_ROOT, nn3(weights, grads)


def early_key_kernel(bias_ref, own_ref, a0, a1, a2, dk_ref, dv_ref):
    bias = bias_ref[:, 0:EARLY]
    for h in range(HEADS):
        k = cols(h)
        dk_ref[:, k], dv_ref[:, k] = far_key_parts(own_ref, bias, lambda lanes: early((a0, a1, a2), lanes), h)


def late_key_kernel(
    bias_ref, own_ref, a0, a1, far_dk_ref, far_dv_ref, dk_in_ref, dv_in_ref, dk_ref, dv_ref, e0_ref, e1_ref
):
    bias = bias_ref[:, EARLY:FAR]
    scales = [1.0 / 4**n for n in (1, 2, 3)]
    for h in range(HEADS):
        k = cols(h)
        d_keys, d_values = far_key_parts(own_ref, bias, lambda lanes: late((a0, a1), lanes), h)
        d_keys = far_dk_ref[:, k] + d_keys
        d_values = far_dv_ref[:, k] + d_values
        dk_ref[:, k] = dk_in_ref[:, k] + expand_levels(e0_ref.at[h % 2], d_keys, scales)
        dv_ref[:, k] = dv_in_ref[:, k] + expand_levels(e1_ref.at[h % 2], d_values, scales)


def f32(*shape):
    return jax.ShapeDtypeStruct(shape, jnp.float32)


def params():
    return pltpu.CompilerParams(vmem_limit_bytes=VMEM_BYTES)


def cost(flops, size):
    return pl.CostEstimate(flops=int(flops), bytes_accessed=int(size), transcendentals=0)


def whole_call(kernel, outs, scratch, flops, size, *operands):
    spec = pl.BlockSpec(memory_space=pltpu.VMEM)
    return pl.pallas_call(
        kernel,
        out_shape=outs,
        in_specs=[spec] * len(operands),
        out_specs=[spec] * len(outs),
        scratch_shapes=[pltpu.VMEM(shape, jnp.float32) for shape in scratch],
        compiler_params=params(),
        cost_estimate=cost(flops, size),
    )(*operands)


BLOCK_FLOPS = 2.0 * BLOCK * BLOCK * DHEAD * HEADS * 6


def column():
    return pl.BlockSpec((BLOCK, DHEAD), lambda h: (0, h))


def slab(blocks):
    return pl.BlockSpec((1, BLOCK, blocks * BLOCK), lambda h: (h, 0, 0))


def head_call(kernel, outs, out_specs, in_specs, blocks, *operands):
    return pl.pallas_call(
        kernel,
        grid=(HEADS,),
        out_shape=outs,
        in_specs=in_specs,
        out_specs=out_specs,
        compiler_params=params(),
        cost_estimate=cost(blocks * BLOCK_FLOPS, 4e6),
    )(*operands)


def near_inner(query, keys, values):
    k = column()
    outs = [f32(HEADS, BLOCK, 2 * BLOCK)] + [f32(BLOCK, WIDTH)] * 3
    return head_call(near_inner_kernel, outs, [slab(2), k, k, k], [k] * 5, 4, query, *keys, *values)


def near_outer(edge, query, keys, values):
    k = column()
    outs = [f32(HEADS, BLOCK, BLOCK)] + [f32(BLOCK, WIDTH)] * 3
    edge_spec = pl.BlockSpec((8, BLOCK), lambda h: (0, 0))
    return head_call(near_outer_kernel, outs, [slab(1), k, k, k], [edge_spec, k, k, k], 2, edge, query, keys, values)


def near_query(w0, w1, peak0, peak1, lse, delta, d_out, keys, values):
    k = column()
    specs = [slab(2), slab(1)] + [k] * 11
    return head_call(
        near_query_kernel, f32(BLOCK, WIDTH), k, specs, 6, w0, w1, peak0, peak1, lse, delta, d_out, *keys, *values
    )


def stat_rows():
    return pl.BlockSpec((8, 256), lambda h: (BLOCK // 8, 0))


def inner_key(key, value, query, query_in, d_out, d_in):
    k, t = column(), stat_rows()
    return head_call(
        inner_key_kernel, [f32(BLOCK, WIDTH)] * 2, [k, k], [k] * 6 + [t, t], 8,
        key, value, query, query_in, d_out, d_in, d_out, d_in,
    )


def outer_key(key, value, query_out, d_far, dk, dv):
    k, t = column(), stat_rows()
    return head_call(
        outer_key_kernel, [f32(BLOCK, WIDTH)] * 2, [k, k], [k] * 4 + [t, k, k], 4,
        key, value, query_out, d_far, d_far, dk, dv,
    )


def pool(key, value, query):
    vmem = pl.BlockSpec(memory_space=pltpu.VMEM)
    hbm = pl.BlockSpec(memory_space=pltpu.HBM)
    return pl.pallas_call(
        pool_kernel,
        out_shape=[
            f32(OWN, 3 * WIDTH), f32(64, KV), f32(16, KV), f32(4, KV), f32(OWN, FAR), f32(8, BLOCK),
        ],
        in_specs=[vmem] + [hbm] * 3,
        out_specs=[vmem] * 6,
        scratch_shapes=[
            pltpu.VMEM((2, BLOCK, DHEAD), jnp.float32),
            pltpu.VMEM((64, DHEAD), jnp.float32),
            pltpu.VMEM((16, DHEAD), jnp.float32),
            pltpu.VMEM((3, BLOCK, WIDTH), jnp.float32),
            pltpu.SemaphoreType.DMA((3, 4)),
        ],
        compiler_params=pltpu.CompilerParams(vmem_limit_bytes=POOL_VMEM_BYTES),
        cost_estimate=cost(1e6, 2e6),
    )(jnp.asarray(slot_table()), key, value, query)


def far_forward(bias, own, far, inner, outer, upstream, gain):
    return whole_call(
        far_forward_kernel,
        [f32(BLOCK, WIDTH), f32(BLOCK, WIDTH), f32(8, 256)],
        [(2, BLOCK, DHEAD)] * 3 + [(BLOCK, DHEAD)] * 2,
        BLOCK_FLOPS,
        8e6,
        bias, own, *far, *inner, *outer, upstream, gain,
    )


def cotangent(stats, others, own, attention, lse, upstream, gain):
    return whole_call(
        cotangent_kernel,
        [f32(BLOCK, WIDTH), f32(BLOCK + 8, WIDTH), f32(BLOCK, WIDTH), f32(64, GRAD), f32(16, GRAD), f32(4, GRAD)],
        [(2, BLOCK, DHEAD)] * 3,
        1e6,
        4e6,
        stats, *others, own, attention, lse, upstream, gain,
    )


def far_query(bias, own, far, first, second, third, near):
    (grad,) = whole_call(
        far_query_kernel,
        [f32(BLOCK, WIDTH)],
        [(2, BLOCK, DHEAD)],
        BLOCK_FLOPS,
        6e6,
        bias, own, *far, first, second, third, near,
    )
    return grad


def early_key(bias, own, grads):
    return whole_call(early_key_kernel, [f32(OWN, WIDTH)] * 2, [], BLOCK_FLOPS, 3e6, bias, own, *grads)


def late_key(bias, own, grads, far_dk, far_dv, near_dk, near_dv):
    return whole_call(
        late_key_kernel,
        [f32(BLOCK, WIDTH)] * 2,
        [(2, BLOCK, DHEAD)] * 2,
        BLOCK_FLOPS,
        3e6,
        bias, own, *grads, far_dk, far_dv, near_dk, near_dv,
    )


def body(query, key, value, norm_gain, upstream):
    count = lax.axis_size("seq")
    head_count = lax.axis_size("head")

    def exchange(array, mask):
        return lax.ppermute(array, "seq", [(i, i ^ mask) for i in range(count)])

    def exchange_outer(array):
        pairs = [(i, i + 1 if i % 2 else i - 1) for i in range(1, count - 1)]
        return lax.ppermute(array, "seq", pairs)

    def after(array, *tokens):
        return lax.optimization_barrier((array,) + tokens)[0]

    def packed(second, thirds):
        return whole_call(pack_kernel, [f32(28, second.shape[1])], [], 1e4, 1e5, second, *thirds)[0]

    def doubled(pack, other):
        return whole_call(double_kernel, [f32(56, pack.shape[1])], [], 1e4, 1e5, pack, other)[0]

    def merged(first, double, other):
        width = first.shape[1]
        return whole_call(merge_kernel, [f32(96, width), f32(160, width)], [], 1e4, 1e5, first, double, other)

    gain = norm_gain.reshape(1, WIDTH)
    out_k, out_v = exchange_outer(key), exchange_outer(value)
    own, first, second, third, bias, edge = pool(key, value, query)

    planes = [exchange(third, mask) for mask in PLANES]
    l1a = exchange(first, 2)
    pack = packed(after(second, out_k, out_v), planes)
    in_k, in_v = exchange(after(key, pack), 1), exchange(after(value, pack), 1)
    double = doubled(after(pack, l1a), exchange(pack, 4))
    other = exchange(double, 12)
    w0, *inner = near_inner(query, (key, after(in_k, double)), (value, in_v))
    w1, *outer = near_outer(edge, query, after(out_k, double), out_v)
    l2a, bundle = merged(l1a, after(double, w0, w1), other)
    l2b = exchange(l2a, 2)
    core1 = exchange(bundle, 1)
    core2 = exchange(l2b, 1)
    query_in = exchange(after(query, core2), 1)
    query_out = exchange_outer(after(query, core2))
    far = (l1a, l2a, core1, l2b, core2)
    attention, lse, stats = far_forward(bias, own, far, inner, outer, upstream, gain)

    others = [
        lax.ppermute(stats, "head", [(i, i ^ mask) for i in range(head_count)]) for mask in range(1, head_count)
    ]
    attention = after(attention, query_in, query_out)
    attended, d_out, delta, g1, g2, g3 = cotangent(stats, others, own, attention, lse, upstream, gain)

    d_far = exchange_outer(d_out)
    planes = [exchange(g3, mask) for mask in PLANES]
    l1a = exchange(g1, 2)
    pack = packed(after(g2, d_far), planes)
    d_in = exchange(after(d_out, pack), 1)
    quad = exchange(pack, 4)
    near_dq = near_query(
        w0, w1, inner[0], outer[0], lse, delta, after(d_out, pack), (key, in_k, out_k), (value, in_v, out_v)
    )
    double = doubled(after(pack, near_dq, l1a), quad)
    other = exchange(double, 12)
    near_dk, near_dv = inner_key(key, value, query, query_in, d_out, after(d_in, double))
    query_grad = far_query(bias, own, far, after(g1, double), g2, g3, near_dq)
    l2a, bundle = merged(l1a, after(double, near_dk, query_grad), other)
    l2b = exchange(l2a, 2)
    core1 = exchange(bundle, 1)
    near_dk, near_dv = outer_key(key, value, query_out, after(d_far, l2a), near_dk, near_dv)
    far_dk, far_dv = early_key(bias, own, (l1a, after(l2a, near_dk), core1))
    core2 = exchange(after(l2b, near_dk), 1)
    key_grad, value_grad = late_key(bias, own, (l2b, core2), far_dk, far_dv, near_dk, near_dv)
    return attended, query_grad, key_grad, value_grad


def solution(mesh):
    return jax.shard_map(
        body,
        mesh=mesh,
        in_specs=(
            P("seq", "head"),
            P("seq", "head"),
            P("seq", "head"),
            P("head"),
            P("seq", "head"),
        ),
        out_specs=(P("seq", "head"), P("seq", "head"), P("seq", "head"), P("seq", "head")),
        check_vma=False,
    )
```

```python
import math

import jax
import jax.numpy as jnp
import numpy as np
from jax import lax
from jax.experimental import pallas as pl
from jax.experimental.pallas import tpu as pltpu
from jax.sharding import PartitionSpec as P

DHEAD = 128
BLOCK = 256
FEAT = 2048
HEADS = 4
WIDTH = HEADS * DHEAD
NEGATIVE_FILL = -1e30
FLOOR = -1e25
EPSILON = 1e-06
INV_ROOT = 1.0 / math.sqrt(DHEAD)
LN4 = math.log(4.0)
VMEM_BYTES = 24 * 1024 * 1024
POOL_VMEM_BYTES = 56 * 1024 * 1024

OWN = 96
LEVEL_ROWS = ((0, 64), (64, 80), (80, 84))
FAR = 512
KV = 2 * WIDTH
GRAD = 2 * WIDTH + DHEAD

QUAD = (4, 12, 8)
PLANES = (16, 32, 48)
THIRD_BLOCKS = tuple(y ^ o for o in (0,) + QUAD for y in PLANES)


def flipped(blocks, mask):
    return tuple(o ^ mask for o in blocks)


SLOTS = (
    (1, (2, 3)),
    (2, QUAD),
    (2, flipped(QUAD, 1)),
    (3, THIRD_BLOCKS),
    (3, flipped(THIRD_BLOCKS, 1)),
    (2, flipped(QUAD, 2)),
    (2, flipped(QUAD, 3)),
    (3, flipped(THIRD_BLOCKS, 2)),
    (3, flipped(THIRD_BLOCKS, 3)),
)
EARLY = 320


def slot_table():
    rows = {1: 64, 2: 16, 3: 4}
    offset = np.concatenate([np.repeat(np.array(blocks, np.int32), rows[n]) for n, blocks in SLOTS])
    level = np.concatenate([np.full(len(blocks) * rows[n], n, np.int32) for n, blocks in SLOTS])
    table = np.zeros((8, FAR), np.int32)
    table[0], table[1] = offset, level
    return table


def split3(x):
    high = x.astype(jnp.bfloat16)
    rest = x - high.astype(jnp.float32)
    middle = rest.astype(jnp.bfloat16)
    return high, middle, (rest - middle.astype(jnp.float32)).astype(jnp.bfloat16)


def dot(a, b, dims):
    return lax.dot_general(a, b, (dims, ((), ())), preferred_element_type=jnp.float32)


def nt3(a, b):
    a1, a2, a3 = split3(a)
    b1, b2, b3 = split3(b)
    left = jnp.concatenate([a1, a2, a1, a2, a1, a3], axis=1)
    right = jnp.concatenate([b1, b1, b2, b2, b3, b1], axis=1)
    return dot(left, right, ((1,), (1,)))


def nn3(a, b):
    a1, a2, a3 = split3(a)
    b1, b2, b3 = split3(b)
    right = jnp.concatenate([b1, b2], axis=1)
    main = dot(jnp.concatenate([a1, a2], axis=1), jnp.concatenate([right, right], axis=0), ((1,), (0,)))
    small = dot(jnp.concatenate([a1, a3], axis=1), jnp.concatenate([b3, b1], axis=0), ((1,), (0,)))
    return main[:, :DHEAD] + (main[:, DHEAD:] + small)


def cols(h, base=0):
    return slice(base + h * DHEAD, base + (h + 1) * DHEAD)


def quarters(ref, value):
    rows = value.shape[0] // 4
    ref[pl.ds(0, 4 * rows), :] = value
    return [ref[pl.ds(j, rows, stride=4), :] for j in range(4)]


def mean4(ref, value):
    parts = quarters(ref, value)
    return ((parts[0] + parts[1]) + (parts[2] + parts[3])) * 0.25


def expand(ref, value):
    rows = value.shape[0]
    for j in range(4):
        ref[pl.ds(j, rows, stride=4), :] = value
    return ref[pl.ds(0, 4 * rows), :]


def expand_levels(ref, value, scales):
    total = value[80:84] * scales[2]
    total = value[64:80] * scales[1] + expand(ref, total)
    total = value[0:64] * scales[0] + expand(ref, total)
    return expand(ref, total)


def lane_index(rows):
    return lax.broadcasted_iota(jnp.int32, (rows, DHEAD), 1)


def wide(column):
    return jnp.broadcast_to(column, (column.shape[0], DHEAD))


def early(refs, lanes):
    l1a, l2a, core1 = refs
    pieces = [l1a[:, lanes], core1[0:64, lanes], l2a[0:48, lanes], core1[64:112, lanes]]
    return pieces + [l2a[48:96, lanes], core1[112:160, lanes]]


def late(refs, lanes):
    l2b, core2 = refs
    return [l2b[0:48, lanes], core2[0:48, lanes], l2b[48:96, lanes], core2[48:96, lanes]]


def gathered(refs, lanes):
    return jnp.concatenate(early(refs[0:3], lanes) + late(refs[3:5], lanes), axis=0)


def pool_kernel(
    table_ref, k_ref, v_ref, q_ref,
    own_ref, first_ref, second_ref, third_ref, bias_ref, edge_ref,
    e0_ref, e1_ref, e2_ref, in_ref, sems,
):
    copies = []
    for i, ref in enumerate((k_ref, v_ref, q_ref)):
        for j in range(4):
            rows = pl.ds(64 * j, 64)
            copies.append(pltpu.make_async_copy(ref.at[rows, :], in_ref.at[i, rows, :], sems.at[i, j]))
    for copy in copies:
        copy.start()
    place = lax.axis_index("seq")
    last = lax.axis_size("seq") - 1
    offset = table_ref[0:1, :]
    level = table_ref[1:2, :]
    row = lax.broadcasted_iota(jnp.int32, (OWN, FAR), 0)
    mine = jnp.where(row < 64, 1, jnp.where(row < 80, 2, jnp.where(row < 84, 3, 0)))
    allowed = (jnp.abs((offset ^ place) - place) > 1) & (level == mine)
    bias_ref[...] = jnp.where(allowed, level.astype(jnp.float32) * LN4, NEGATIVE_FILL)
    alone = (place == 0) | (place == last)
    edge_ref[...] = jnp.full((8, BLOCK), jnp.where(alone, NEGATIVE_FILL, 0.0), jnp.float32)
    own_ref[84:96, :] = jnp.zeros((12, 3 * WIDTH), jnp.float32)
    for part in range(3):
        for copy in copies[4 * part : 4 * part + 4]:
            copy.wait()
        for h in range(HEADS):
            dst = cols(h, part * WIDTH)
            value = in_ref[part, :, cols(h)]
            one = mean4(e0_ref.at[(part * HEADS + h) % 2], value)
            two = mean4(e1_ref, one)
            three = mean4(e2_ref, two)
            own_ref[0:64, dst] = one
            own_ref[64:80, dst] = two
            own_ref[80:84, dst] = three
            if part < 2:
                first_ref[:, dst] = one
                second_ref[:, dst] = two
                third_ref[:, dst] = three


def pack_kernel(second_ref, a_ref, b_ref, c_ref, out_ref):
    out_ref[0:16, :] = second_ref[...]
    out_ref[16:20, :] = a_ref[...]
    out_ref[20:24, :] = b_ref[...]
    out_ref[24:28, :] = c_ref[...]


def double_kernel(own_ref, other_ref, out_ref):
    out_ref[0:28, :] = own_ref[...]
    out_ref[28:56, :] = other_ref[...]


def merge_kernel(first_ref, double_ref, other_ref, out_ref, bundle_ref):
    bundle_ref[0:64, :] = first_ref[...]
    parts = (double_ref[28:56, :], other_ref[0:28, :], other_ref[28:56, :])
    pieces = [(16 * i, part[0:16]) for i, part in enumerate(parts)]
    pieces += [(48 + 12 * i, part[16:28]) for i, part in enumerate((double_ref[0:28, :],) + parts)]
    for start, piece in pieces:
        stop = start + piece.shape[0]
        out_ref[start:stop, :] = piece
        bundle_ref[64 + start : 64 + stop, :] = piece


def near_state(scores, values, w_ref, peak_ref, mass_ref, sum_ref):
    peak = jnp.maximum(jnp.max(scores, axis=1, keepdims=True), FLOOR)
    weights = jnp.exp(scores - peak)
    w_ref[0] = weights
    peak_ref[...] = wide(peak)
    mass_ref[...] = wide(jnp.sum(weights, axis=1, keepdims=True))
    sum_ref[...] = nn3(weights, values)


def near_inner_kernel(q_ref, ko_ref, ki_ref, vo_ref, vi_ref, *outs):
    keys = jnp.concatenate([ko_ref[...], ki_ref[...]], axis=0)
    values = jnp.concatenate([vo_ref[...], vi_ref[...]], axis=0)
    near_state(nt3(q_ref[...], keys) * INV_ROOT, values, *outs)


def near_outer_kernel(edge_ref, q_ref, k_ref, v_ref, *outs):
    near_state(nt3(q_ref[...], k_ref[...]) * INV_ROOT + edge_ref[0:1, :], v_ref[...], *outs)


def merge(one, two):
    peak = jnp.maximum(one[0], two[0])
    left = jnp.exp(one[0] - peak)
    right = jnp.exp(two[0] - peak)
    return peak, left * one[1] + right * two[1], left * one[2] + right * two[2]


def far_forward_kernel(
    bias_ref, own_ref, a0, a1, a2, a3, a4,
    peak0_ref, mass0_ref, sum0_ref, peak1_ref, mass1_ref, sum1_ref, up_ref, gain_ref,
    att_ref, lse_ref, stat_ref,
    e0_ref, e1_ref, e2_ref, square_ref, cross_ref,
):
    far = (a0, a1, a2, a3, a4)
    bias = bias_ref[...]
    for h in range(HEADS):
        k = cols(h)
        v = cols(h, WIDTH)
        scores = nt3(own_ref[:, cols(h, 2 * WIDTH)], gathered(far, k)) * INV_ROOT + bias
        peak = jnp.maximum(jnp.max(scores, axis=1, keepdims=True), FLOOR)
        weights = jnp.exp(scores - peak)
        mass = jnp.sum(weights, axis=1, keepdims=True)
        levels = (wide(peak), wide(mass), nn3(weights, gathered(far, v)))
        state = tuple(x[80:84] for x in levels)
        for start, stop in (LEVEL_ROWS[1], LEVEL_ROWS[0]):
            state = tuple(expand(ref.at[h % 2], x) for ref, x in zip((e0_ref, e1_ref, e2_ref), state))
            state = merge(state, tuple(x[start:stop] for x in levels))
        state = tuple(expand(ref.at[h % 2], x) for ref, x in zip((e0_ref, e1_ref, e2_ref), state))
        near = merge(
            (peak0_ref[:, k], mass0_ref[:, k], sum0_ref[:, k]), (peak1_ref[:, k], mass1_ref[:, k], sum1_ref[:, k])
        )
        state = merge(state, near)
        attention = state[2] / state[1]
        att_ref[:, k] = attention
        lse_ref[:, k] = state[0] + jnp.log(state[1])
        square = attention * attention
        cross = up_ref[:, k] * gain_ref[0:1, k] * attention
        if h == 0:
            square_ref[...] = square
            cross_ref[...] = cross
        else:
            square_ref[...] += square
            cross_ref[...] += cross
    square = wide(jnp.sum(square_ref[...], axis=1, keepdims=True))
    cross = wide(jnp.sum(cross_ref[...], axis=1, keepdims=True))
    packed = jnp.where(lane_index(BLOCK) == 0, square, cross)
    stat_ref[...] = jnp.transpose(packed)[0:8, :]


def pooled_cotangent(scratch, lows, dots, grads):
    lows, dots, grads = (quarters(ref, x) for ref, x in zip(scratch, (lows, dots, grads)))
    low = jnp.minimum(jnp.minimum(lows[0], lows[1]), jnp.minimum(lows[2], lows[3]))
    scale = [jnp.exp(low - x) for x in lows]
    total = scale[0] * dots[0]
    grad = scale[0] * grads[0]
    for j in range(1, 4):
        total = total + scale[j] * dots[j]
        grad = grad + scale[j] * grads[j]
    return low, total, grad


def cotangent_kernel(
    s0_ref, s1_ref, s2_ref, s3_ref, own_ref, att_ref, lse_ref, up_ref, gain_ref,
    out_ref, dout_ref, delta_ref, first_ref, second_ref, third_ref,
    e0_ref, e1_ref, e2_ref,
):
    total = (s0_ref[...] + s1_ref[...]) + (s2_ref[...] + s3_ref[...])
    square = jnp.transpose(jnp.broadcast_to(total[0:1, :], (DHEAD, BLOCK)))
    cross = jnp.transpose(jnp.broadcast_to(total[1:2, :], (DHEAD, BLOCK)))
    inverse = lax.rsqrt(square / FEAT + EPSILON)
    pull = inverse * inverse * inverse * cross / FEAT
    lane = lane_index(BLOCK)
    packed = jnp.zeros((BLOCK, DHEAD), jnp.float32)
    stats = [jnp.zeros((rows, DHEAD), jnp.float32) for rows in (64, 16, 4)]
    first_ref[:, WIDTH:KV] = own_ref[0:64, KV:]
    second_ref[:, WIDTH:KV] = own_ref[64:80, KV:]
    third_ref[:, WIDTH:KV] = own_ref[80:84, KV:]
    for h in range(HEADS):
        k = cols(h)
        attention = att_ref[:, k]
        out_ref[:, k] = attention * inverse * gain_ref[0:1, k]
        d_out = inverse * (up_ref[:, k] * gain_ref[0:1, k]) - attention * pull
        dout_ref[0:BLOCK, k] = d_out
        delta = wide(jnp.sum(d_out * attention, axis=1, keepdims=True))
        delta_ref[:, k] = delta
        packed = jnp.where(lane == h, lse_ref[:, k], packed)
        packed = jnp.where(lane == HEADS + h, delta, packed)
        level = (lse_ref[:, k], delta, d_out)
        for n, ref in enumerate((first_ref, second_ref, third_ref)):
            level = pooled_cotangent([e.at[h % 2] for e in (e0_ref, e1_ref, e2_ref)], *level)
            rows = level[0].shape[0]
            ref[:, k] = level[2]
            short = lane[0:rows]
            stats[n] = jnp.where(short == h, level[0], jnp.where(short == HEADS + h, level[1], stats[n]))
    first_ref[:, KV:] = stats[0]
    second_ref[:, KV:] = stats[1]
    third_ref[:, KV:] = stats[2]
    dout_ref[BLOCK:, 0:256] = jnp.transpose(packed)[0:8, :]
    dout_ref[BLOCK:, 256:] = jnp.zeros((8, 256), jnp.float32)


def near_query_kernel(
    w0_ref, w1_ref, peak0_ref, peak1_ref, lse_ref, delta_ref, dout_ref,
    k0_ref, k1_ref, k2_ref, v0_ref, v1_ref, v2_ref, dq_ref,
):
    keys = jnp.concatenate([k0_ref[...], k1_ref[...], k2_ref[...]], axis=0)
    values = jnp.concatenate([v0_ref[...], v1_ref[...], v2_ref[...]], axis=0)
    lse = lse_ref[:, 0:1]
    inner = w0_ref[0] * jnp.exp(peak0_ref[:, 0:1] - lse)
    outer = w1_ref[0] * jnp.exp(peak1_ref[:, 0:1] - lse)
    weights = jnp.concatenate([inner, outer], axis=1)
    d_scores = weights * (nt3(dout_ref[...], values) - delta_ref[:, 0:1])
    dq_ref[...] = nn3(d_scores, keys) * INV_ROOT


def far_query_kernel(
    bias_ref, own_ref, a0, a1, a2, a3, a4, first_ref, second_ref, third_ref, near_ref, dq_ref, e0_ref
):
    far = (a0, a1, a2, a3, a4)
    bias = bias_ref[...]

    def grads(lanes):
        fill = jnp.zeros((12, DHEAD), jnp.float32)
        return jnp.concatenate([first_ref[:, lanes], second_ref[:, lanes], third_ref[:, lanes], fill], axis=0)

    stats = grads(slice(KV, GRAD))
    for h in range(HEADS):
        k = cols(h)
        keys = gathered(far, k)
        scores = nt3(own_ref[:, cols(h, 2 * WIDTH)], keys) * INV_ROOT + bias
        weights = jnp.exp(scores - stats[:, h : h + 1])
        d_probs = nt3(grads(k), gathered(far, cols(h, WIDTH)))
        d_scores = weights * (d_probs - stats[:, HEADS + h : HEADS + h + 1])
        grad = nn3(d_scores, keys)
        scales = [INV_ROOT / 4**n for n in (1, 2, 3)]
        dq_ref[:, k] = near_ref[:, k] + expand_levels(e0_ref.at[h % 2], grad, scales)


def near_key_parts(k_ref, v_ref, queries, grads, stats):
    h = pl.program_id(0)
    low = jnp.concatenate([ref[pl.ds(h, 1), :] for ref in stats], axis=1)
    total = jnp.concatenate([ref[pl.ds(h + HEADS, 1), :] for ref in stats], axis=1)
    weights = jnp.exp(nt3(k_ref[...], queries) * INV_ROOT - low)
    d_scores = weights * (nt3(v_ref[...], grads) - total)
    return nn3(d_scores, queries) * INV_ROOT, nn3(weights, grads)


def inner_key_kernel(k_ref, v_ref, q0_ref, q1_ref, d0_ref, d1_ref, t0_ref, t1_ref, dk_ref, dv_ref):
    queries = jnp.concatenate([q0_ref[...], q1_ref[...]], axis=0)
    grads = jnp.concatenate([d0_ref[...], d1_ref[...]], axis=0)
    dk_ref[...], dv_ref[...] = near_key_parts(k_ref, v_ref, queries, grads, (t0_ref, t1_ref))


def outer_key_kernel(k_ref, v_ref, q_ref, d_ref, t_ref, dk_in_ref, dv_in_ref, dk_ref, dv_ref):
    d_keys, d_values = near_key_parts(k_ref, v_ref, q_ref[...], d_ref[...], (t_ref,))
    dk_ref[...] = dk_in_ref[...] + d_keys
    dv_ref[...] = dv_in_ref[...] + d_values


def far_key_parts(own_ref, bias, pieces, h):
    def take(lanes):
        return jnp.concatenate(pieces(lanes), axis=0)

    stats = take(slice(KV, GRAD))
    fill = jnp.zeros((64, DHEAD), jnp.float32)
    stats = jnp.transpose(jnp.concatenate([stats, fill], axis=0))[0:8, 0 : stats.shape[0]]
    queries = take(cols(h, WIDTH))
    grads = take(cols(h))
    scores = nt3(own_ref[:, cols(h)], queries) * INV_ROOT + bias
    weights = jnp.exp(scores - stats[h : h + 1, :])
    d_scores = weights * (nt3(own_ref[:, cols(h, WIDTH)], grads) - stats[HEADS + h : HEADS + h + 1, :])
    return nn3(d_scores, queries) * INV_ROOT, nn3(weights, grads)


def early_key_kernel(bias_ref, own_ref, a0, a1, a2, dk_ref, dv_ref):
    bias = bias_ref[:, 0:EARLY]
    for h in range(HEADS):
        k = cols(h)
        dk_ref[:, k], dv_ref[:, k] = far_key_parts(own_ref, bias, lambda lanes: early((a0, a1, a2), lanes), h)


def late_key_kernel(
    bias_ref, own_ref, a0, a1, far_dk_ref, far_dv_ref, dk_in_ref, dv_in_ref, dk_ref, dv_ref, e0_ref, e1_ref
):
    bias = bias_ref[:, EARLY:FAR]
    scales = [1.0 / 4**n for n in (1, 2, 3)]
    for h in range(HEADS):
        k = cols(h)
        d_keys, d_values = far_key_parts(own_ref, bias, lambda lanes: late((a0, a1), lanes), h)
        d_keys = far_dk_ref[:, k] + d_keys
        d_values = far_dv_ref[:, k] + d_values
        dk_ref[:, k] = dk_in_ref[:, k] + expand_levels(e0_ref.at[h % 2], d_keys, scales)
        dv_ref[:, k] = dv_in_ref[:, k] + expand_levels(e1_ref.at[h % 2], d_values, scales)


def f32(*shape):
    return jax.ShapeDtypeStruct(shape, jnp.float32)


def params():
    return pltpu.CompilerParams(vmem_limit_bytes=VMEM_BYTES)


def cost(flops, size):
    return pl.CostEstimate(flops=int(flops), bytes_accessed=int(size), transcendentals=0)


def whole_call(kernel, outs, scratch, flops, size, *operands):
    spec = pl.BlockSpec(memory_space=pltpu.VMEM)
    return pl.pallas_call(
        kernel,
        out_shape=outs,
        in_specs=[spec] * len(operands),
        out_specs=[spec] * len(outs),
        scratch_shapes=[pltpu.VMEM(shape, jnp.float32) for shape in scratch],
        compiler_params=params(),
        cost_estimate=cost(flops, size),
    )(*operands)


BLOCK_FLOPS = 2.0 * BLOCK * BLOCK * DHEAD * HEADS * 6


def column():
    return pl.BlockSpec((BLOCK, DHEAD), lambda h: (0, h))


def slab(blocks):
    return pl.BlockSpec((1, BLOCK, blocks * BLOCK), lambda h: (h, 0, 0))


def head_call(kernel, outs, out_specs, in_specs, blocks, *operands):
    return pl.pallas_call(
        kernel,
        grid=(HEADS,),
        out_shape=outs,
        in_specs=in_specs,
        out_specs=out_specs,
        compiler_params=params(),
        cost_estimate=cost(blocks * BLOCK_FLOPS, 4e6),
    )(*operands)


def near_inner(query, keys, values):
    k = column()
    outs = [f32(HEADS, BLOCK, 2 * BLOCK)] + [f32(BLOCK, WIDTH)] * 3
    return head_call(near_inner_kernel, outs, [slab(2), k, k, k], [k] * 5, 4, query, *keys, *values)


def near_outer(edge, query, keys, values):
    k = column()
    outs = [f32(HEADS, BLOCK, BLOCK)] + [f32(BLOCK, WIDTH)] * 3
    edge_spec = pl.BlockSpec((8, BLOCK), lambda h: (0, 0))
    return head_call(near_outer_kernel, outs, [slab(1), k, k, k], [edge_spec, k, k, k], 2, edge, query, keys, values)


def near_query(w0, w1, peak0, peak1, lse, delta, d_out, keys, values):
    k = column()
    specs = [slab(2), slab(1)] + [k] * 11
    return head_call(
        near_query_kernel, f32(BLOCK, WIDTH), k, specs, 6, w0, w1, peak0, peak1, lse, delta, d_out, *keys, *values
    )


def stat_rows():
    return pl.BlockSpec((8, 256), lambda h: (BLOCK // 8, 0))


def inner_key(key, value, query, query_in, d_out, d_in):
    k, t = column(), stat_rows()
    return head_call(
        inner_key_kernel, [f32(BLOCK, WIDTH)] * 2, [k, k], [k] * 6 + [t, t], 8,
        key, value, query, query_in, d_out, d_in, d_out, d_in,
    )


def outer_key(key, value, query_out, d_far, dk, dv):
    k, t = column(), stat_rows()
    return head_call(
        outer_key_kernel, [f32(BLOCK, WIDTH)] * 2, [k, k], [k] * 4 + [t, k, k], 4,
        key, value, query_out, d_far, d_far, dk, dv,
    )


def pool(key, value, query):
    vmem = pl.BlockSpec(memory_space=pltpu.VMEM)
    hbm = pl.BlockSpec(memory_space=pltpu.HBM)
    return pl.pallas_call(
        pool_kernel,
        out_shape=[
            f32(OWN, 3 * WIDTH), f32(64, KV), f32(16, KV), f32(4, KV), f32(OWN, FAR), f32(8, BLOCK),
        ],
        in_specs=[vmem] + [hbm] * 3,
        out_specs=[vmem] * 6,
        scratch_shapes=[
            pltpu.VMEM((2, BLOCK, DHEAD), jnp.float32),
            pltpu.VMEM((64, DHEAD), jnp.float32),
            pltpu.VMEM((16, DHEAD), jnp.float32),
            pltpu.VMEM((3, BLOCK, WIDTH), jnp.float32),
            pltpu.SemaphoreType.DMA((3, 4)),
        ],
        compiler_params=pltpu.CompilerParams(vmem_limit_bytes=POOL_VMEM_BYTES),
        cost_estimate=cost(1e6, 2e6),
    )(jnp.asarray(slot_table()), key, value, query)


def far_forward(bias, own, far, inner, outer, upstream, gain):
    return whole_call(
        far_forward_kernel,
        [f32(BLOCK, WIDTH), f32(BLOCK, WIDTH), f32(8, 256)],
        [(2, BLOCK, DHEAD)] * 3 + [(BLOCK, DHEAD)] * 2,
        BLOCK_FLOPS,
        8e6,
        bias, own, *far, *inner, *outer, upstream, gain,
    )


def cotangent(stats, others, own, attention, lse, upstream, gain):
    return whole_call(
        cotangent_kernel,
        [f32(BLOCK, WIDTH), f32(BLOCK + 8, WIDTH), f32(BLOCK, WIDTH), f32(64, GRAD), f32(16, GRAD), f32(4, GRAD)],
        [(2, BLOCK, DHEAD)] * 3,
        1e6,
        4e6,
        stats, *others, own, attention, lse, upstream, gain,
    )


def far_query(bias, own, far, first, second, third, near):
    (grad,) = whole_call(
        far_query_kernel,
        [f32(BLOCK, WIDTH)],
        [(2, BLOCK, DHEAD)],
        BLOCK_FLOPS,
        6e6,
        bias, own, *far, first, second, third, near,
    )
    return grad


def early_key(bias, own, grads):
    return whole_call(early_key_kernel, [f32(OWN, WIDTH)] * 2, [], BLOCK_FLOPS, 3e6, bias, own, *grads)


def late_key(bias, own, grads, far_dk, far_dv, near_dk, near_dv):
    return whole_call(
        late_key_kernel,
        [f32(BLOCK, WIDTH)] * 2,
        [(2, BLOCK, DHEAD)] * 2,
        BLOCK_FLOPS,
        3e6,
        bias, own, *grads, far_dk, far_dv, near_dk, near_dv,
    )


def body(query, key, value, norm_gain, upstream):
    count = lax.axis_size("seq")
    head_count = lax.axis_size("head")

    def exchange(array, mask):
        return lax.ppermute(array, "seq", [(i, i ^ mask) for i in range(count)])

    def exchange_outer(array):
        pairs = [(i, i + 1 if i % 2 else i - 1) for i in range(1, count - 1)]
        return lax.ppermute(array, "seq", pairs)

    def after(array, *tokens):
        return lax.optimization_barrier((array,) + tokens)[0]

    def packed(second, thirds):
        return whole_call(pack_kernel, [f32(28, second.shape[1])], [], 1e4, 1e5, second, *thirds)[0]

    def doubled(pack, other):
        return whole_call(double_kernel, [f32(56, pack.shape[1])], [], 1e4, 1e5, pack, other)[0]

    def merged(first, double, other):
        width = first.shape[1]
        return whole_call(merge_kernel, [f32(96, width), f32(160, width)], [], 1e4, 1e5, first, double, other)

    gain = norm_gain.reshape(1, WIDTH)
    out_k, out_v = exchange_outer(key), exchange_outer(value)
    own, first, second, third, bias, edge = pool(key, value, query)

    planes = [exchange(after(third, out_k), PLANES[0])] + [exchange(third, mask) for mask in PLANES[1:]]
    l1a = exchange(first, 2)
    pack = packed(after(second, out_k, out_v, l1a), planes)
    in_k, in_v = exchange(after(key, pack), 1), exchange(after(value, pack), 1)
    double = doubled(pack, exchange(pack, 4))
    other = exchange(double, 12)
    w0, *inner = near_inner(query, (key, after(in_k, double)), (value, in_v))
    w1, *outer = near_outer(edge, query, after(out_k, double), out_v)
    l2a, bundle = merged(l1a, after(double, w0, w1), other)
    l2b = exchange(l2a, 2)
    core1 = exchange(bundle, 1)
    core2 = exchange(after(l2b, core1), 1)
    query_in = exchange(after(query, core2), 1)
    query_out = exchange_outer(after(query, core2))
    far = (l1a, l2a, core1, l2b, core2)
    attention, lse, stats = far_forward(bias, own, far, inner, outer, upstream, gain)

    others = [
        lax.ppermute(stats, "head", [(i, i ^ mask) for i in range(head_count)]) for mask in range(1, head_count)
    ]
    attention = after(attention, query_in, query_out)
    attended, d_out, delta, g1, g2, g3 = cotangent(stats, others, own, attention, lse, upstream, gain)

    planes = [exchange(g3, mask) for mask in PLANES]
    l1a = exchange(g1, 2)
    d_in = exchange(d_out, 1)
    pack = packed(g2, planes)
    quad = exchange(pack, 4)
    near_dq = near_query(
        w0, w1, inner[0], outer[0], lse, delta, after(d_out, pack),
        (key, in_k, out_k), (value, in_v, out_v),
    )
    double = doubled(after(pack, near_dq, l1a), quad)
    other = exchange(double, 12)
    query_grad = far_query(bias, own, far, after(g1, double), g2, g3, near_dq)
    d_far = exchange_outer(after(d_out, query_grad))
    near_dk, near_dv = inner_key(key, value, query, query_in, d_out, after(d_in, double))
    l2a, bundle = merged(l1a, after(double, near_dk, query_grad, d_far), other)
    l2b = exchange(l2a, 2)
    core1 = exchange(bundle, 1)
    near_dk, near_dv = outer_key(key, value, query_out, after(d_far, l2a), near_dk, near_dv)
    far_dk, far_dv = early_key(bias, own, (l1a, after(l2a, near_dk), core1))
    core2 = exchange(after(l2b, far_dk), 1)
    key_grad, value_grad = late_key(bias, own, (l2b, core2), far_dk, far_dv, near_dk, near_dv)
    return attended, query_grad, key_grad, value_grad


def solution(mesh):
    return jax.shard_map(
        body,
        mesh=mesh,
        in_specs=(
            P("seq", "head"),
            P("seq", "head"),
            P("seq", "head"),
            P("head"),
            P("seq", "head"),
        ),
        out_specs=(P("seq", "head"), P("seq", "head"), P("seq", "head"), P("seq", "head")),
        check_vma=False,
    )
```

```python
import math

import jax
import jax.numpy as jnp
import numpy as np
from jax import lax
from jax.experimental import pallas as pl
from jax.experimental.pallas import tpu as pltpu
from jax.sharding import PartitionSpec as P

DHEAD = 128
BLOCK = 256
FEAT = 2048
HEADS = 4
WIDTH = HEADS * DHEAD
NEGATIVE_FILL = -1e30
FLOOR = -1e25
EPSILON = 1e-06
INV_ROOT = 1.0 / math.sqrt(DHEAD)
LN4 = math.log(4.0)
VMEM_BYTES = 24 * 1024 * 1024
POOL_VMEM_BYTES = 56 * 1024 * 1024

OWN = 96
LEVEL_ROWS = ((0, 64), (64, 80), (80, 84))
FAR = 512
KV = 2 * WIDTH
GRAD = 2 * WIDTH + DHEAD

QUAD = (4, 12, 8)
PLANES = (16, 32, 48)
THIRD_BLOCKS = tuple(y ^ o for o in (0,) + QUAD for y in PLANES)


def flipped(blocks, mask):
    return tuple(o ^ mask for o in blocks)


SLOTS = (
    (1, (2, 3)),
    (2, QUAD),
    (2, flipped(QUAD, 1)),
    (3, THIRD_BLOCKS),
    (3, flipped(THIRD_BLOCKS, 1)),
    (2, flipped(QUAD, 2)),
    (2, flipped(QUAD, 3)),
    (3, flipped(THIRD_BLOCKS, 2)),
    (3, flipped(THIRD_BLOCKS, 3)),
)
EARLY = 320


def slot_table():
    rows = {1: 64, 2: 16, 3: 4}
    offset = np.concatenate([np.repeat(np.array(blocks, np.int32), rows[n]) for n, blocks in SLOTS])
    level = np.concatenate([np.full(len(blocks) * rows[n], n, np.int32) for n, blocks in SLOTS])
    table = np.zeros((8, FAR), np.int32)
    table[0], table[1] = offset, level
    return table


def split3(x):
    high = x.astype(jnp.bfloat16)
    rest = x - high.astype(jnp.float32)
    middle = rest.astype(jnp.bfloat16)
    return high, middle, (rest - middle.astype(jnp.float32)).astype(jnp.bfloat16)


def dot(a, b, dims):
    return lax.dot_general(a, b, (dims, ((), ())), preferred_element_type=jnp.float32)


def nt3(a, b):
    a1, a2, a3 = split3(a)
    b1, b2, b3 = split3(b)
    left = jnp.concatenate([a1, a2, a1, a2, a1, a3], axis=1)
    right = jnp.concatenate([b1, b1, b2, b2, b3, b1], axis=1)
    return dot(left, right, ((1,), (1,)))


def nn3(a, b):
    a1, a2, a3 = split3(a)
    b1, b2, b3 = split3(b)
    right = jnp.concatenate([b1, b2], axis=1)
    main = dot(jnp.concatenate([a1, a2], axis=1), jnp.concatenate([right, right], axis=0), ((1,), (0,)))
    small = dot(jnp.concatenate([a1, a3], axis=1), jnp.concatenate([b3, b1], axis=0), ((1,), (0,)))
    return main[:, :DHEAD] + (main[:, DHEAD:] + small)


def cols(h, base=0):
    return slice(base + h * DHEAD, base + (h + 1) * DHEAD)


def quarters(ref, value):
    rows = value.shape[0] // 4
    ref[pl.ds(0, 4 * rows), :] = value
    return [ref[pl.ds(j, rows, stride=4), :] for j in range(4)]


def mean4(ref, value):
    parts = quarters(ref, value)
    return ((parts[0] + parts[1]) + (parts[2] + parts[3])) * 0.25


def expand(ref, value):
    rows = value.shape[0]
    for j in range(4):
        ref[pl.ds(j, rows, stride=4), :] = value
    return ref[pl.ds(0, 4 * rows), :]


def expand_levels(ref, value, scales):
    total = value[80:84] * scales[2]
    total = value[64:80] * scales[1] + expand(ref, total)
    total = value[0:64] * scales[0] + expand(ref, total)
    return expand(ref, total)


def lane_index(rows):
    return lax.broadcasted_iota(jnp.int32, (rows, DHEAD), 1)


def wide(column):
    return jnp.broadcast_to(column, (column.shape[0], DHEAD))


def early(refs, lanes):
    l1a, l2a, core1 = refs
    pieces = [l1a[:, lanes], core1[0:64, lanes], l2a[0:48, lanes], core1[64:112, lanes]]
    return pieces + [l2a[48:96, lanes], core1[112:160, lanes]]


def late(refs, lanes):
    l2b, core2 = refs
    return [l2b[0:48, lanes], core2[0:48, lanes], l2b[48:96, lanes], core2[48:96, lanes]]


def gathered(refs, lanes):
    return jnp.concatenate(early(refs[0:3], lanes) + late(refs[3:5], lanes), axis=0)


def pool_kernel(
    table_ref, k_ref, v_ref, q_ref,
    own_ref, first_ref, second_ref, third_ref, bias_ref, edge_ref,
    e0_ref, e1_ref, e2_ref, in_ref, sems,
):
    copies = []
    for i, ref in enumerate((k_ref, v_ref, q_ref)):
        for j in range(4):
            rows = pl.ds(64 * j, 64)
            copies.append(pltpu.make_async_copy(ref.at[rows, :], in_ref.at[i, rows, :], sems.at[i, j]))
    for copy in copies:
        copy.start()
    place = lax.axis_index("seq")
    last = lax.axis_size("seq") - 1
    offset = table_ref[0:1, :]
    level = table_ref[1:2, :]
    row = lax.broadcasted_iota(jnp.int32, (OWN, FAR), 0)
    mine = jnp.where(row < 64, 1, jnp.where(row < 80, 2, jnp.where(row < 84, 3, 0)))
    allowed = (jnp.abs((offset ^ place) - place) > 1) & (level == mine)
    bias_ref[...] = jnp.where(allowed, level.astype(jnp.float32) * LN4, NEGATIVE_FILL)
    alone = (place == 0) | (place == last)
    edge_ref[...] = jnp.full((8, BLOCK), jnp.where(alone, NEGATIVE_FILL, 0.0), jnp.float32)
    own_ref[84:96, :] = jnp.zeros((12, 3 * WIDTH), jnp.float32)
    for part in range(3):
        for copy in copies[4 * part : 4 * part + 4]:
            copy.wait()
        for h in range(HEADS):
            dst = cols(h, part * WIDTH)
            value = in_ref[part, :, cols(h)]
            one = mean4(e0_ref.at[(part * HEADS + h) % 2], value)
            two = mean4(e1_ref, one)
            three = mean4(e2_ref, two)
            own_ref[0:64, dst] = one
            own_ref[64:80, dst] = two
            own_ref[80:84, dst] = three
            if part < 2:
                first_ref[:, dst] = one
                second_ref[:, dst] = two
                third_ref[:, dst] = three


def pack_kernel(second_ref, a_ref, b_ref, c_ref, out_ref):
    out_ref[0:16, :] = second_ref[...]
    out_ref[16:20, :] = a_ref[...]
    out_ref[20:24, :] = b_ref[...]
    out_ref[24:28, :] = c_ref[...]


def double_kernel(own_ref, other_ref, out_ref):
    out_ref[0:28, :] = own_ref[...]
    out_ref[28:56, :] = other_ref[...]


def merge_kernel(first_ref, double_ref, other_ref, out_ref, bundle_ref):
    bundle_ref[0:64, :] = first_ref[...]
    parts = (double_ref[28:56, :], other_ref[0:28, :], other_ref[28:56, :])
    pieces = [(16 * i, part[0:16]) for i, part in enumerate(parts)]
    pieces += [(48 + 12 * i, part[16:28]) for i, part in enumerate((double_ref[0:28, :],) + parts)]
    for start, piece in pieces:
        stop = start + piece.shape[0]
        out_ref[start:stop, :] = piece
        bundle_ref[64 + start : 64 + stop, :] = piece


def near_state(scores, values, w_ref, peak_ref, mass_ref, sum_ref):
    peak = jnp.maximum(jnp.max(scores, axis=1, keepdims=True), FLOOR)
    weights = jnp.exp(scores - peak)
    w_ref[0] = weights
    peak_ref[...] = wide(peak)
    mass_ref[...] = wide(jnp.sum(weights, axis=1, keepdims=True))
    sum_ref[...] = nn3(weights, values)


def near_inner_kernel(q_ref, ko_ref, ki_ref, vo_ref, vi_ref, *outs):
    keys = jnp.concatenate([ko_ref[...], ki_ref[...]], axis=0)
    values = jnp.concatenate([vo_ref[...], vi_ref[...]], axis=0)
    near_state(nt3(q_ref[...], keys) * INV_ROOT, values, *outs)


def near_outer_kernel(edge_ref, q_ref, k_ref, v_ref, *outs):
    near_state(nt3(q_ref[...], k_ref[...]) * INV_ROOT + edge_ref[0:1, :], v_ref[...], *outs)


def merge(one, two):
    peak = jnp.maximum(one[0], two[0])
    left = jnp.exp(one[0] - peak)
    right = jnp.exp(two[0] - peak)
    return peak, left * one[1] + right * two[1], left * one[2] + right * two[2]


def far_forward_kernel(
    bias_ref, own_ref, a0, a1, a2, a3, a4,
    peak0_ref, mass0_ref, sum0_ref, peak1_ref, mass1_ref, sum1_ref, up_ref, gain_ref,
    att_ref, lse_ref, stat_ref,
    e0_ref, e1_ref, e2_ref, square_ref, cross_ref,
):
    far = (a0, a1, a2, a3, a4)
    bias = bias_ref[...]
    for h in range(HEADS):
        k = cols(h)
        v = cols(h, WIDTH)
        scores = nt3(own_ref[:, cols(h, 2 * WIDTH)], gathered(far, k)) * INV_ROOT + bias
        peak = jnp.maximum(jnp.max(scores, axis=1, keepdims=True), FLOOR)
        weights = jnp.exp(scores - peak)
        mass = jnp.sum(weights, axis=1, keepdims=True)
        levels = (wide(peak), wide(mass), nn3(weights, gathered(far, v)))
        state = tuple(x[80:84] for x in levels)
        for start, stop in (LEVEL_ROWS[1], LEVEL_ROWS[0]):
            state = tuple(expand(ref.at[h % 2], x) for ref, x in zip((e0_ref, e1_ref, e2_ref), state))
            state = merge(state, tuple(x[start:stop] for x in levels))
        state = tuple(expand(ref.at[h % 2], x) for ref, x in zip((e0_ref, e1_ref, e2_ref), state))
        near = merge(
            (peak0_ref[:, k], mass0_ref[:, k], sum0_ref[:, k]), (peak1_ref[:, k], mass1_ref[:, k], sum1_ref[:, k])
        )
        state = merge(state, near)
        attention = state[2] / state[1]
        att_ref[:, k] = attention
        lse_ref[:, k] = state[0] + jnp.log(state[1])
        square = attention * attention
        cross = up_ref[:, k] * gain_ref[0:1, k] * attention
        if h == 0:
            square_ref[...] = square
            cross_ref[...] = cross
        else:
            square_ref[...] += square
            cross_ref[...] += cross
    square = wide(jnp.sum(square_ref[...], axis=1, keepdims=True))
    cross = wide(jnp.sum(cross_ref[...], axis=1, keepdims=True))
    packed = jnp.where(lane_index(BLOCK) == 0, square, cross)
    stat_ref[...] = jnp.transpose(packed)[0:8, :]


def pooled_cotangent(scratch, lows, dots, grads):
    lows, dots, grads = (quarters(ref, x) for ref, x in zip(scratch, (lows, dots, grads)))
    low = jnp.minimum(jnp.minimum(lows[0], lows[1]), jnp.minimum(lows[2], lows[3]))
    scale = [jnp.exp(low - x) for x in lows]
    total = scale[0] * dots[0]
    grad = scale[0] * grads[0]
    for j in range(1, 4):
        total = total + scale[j] * dots[j]
        grad = grad + scale[j] * grads[j]
    return low, total, grad


def cotangent_kernel(
    s0_ref, s1_ref, s2_ref, s3_ref, own_ref, query_ref, att_ref, lse_ref, up_ref, gain_ref,
    out_ref, dout_ref, delta_ref, first_ref, second_ref, third_ref,
    e0_ref, e1_ref, e2_ref,
):
    total = (s0_ref[...] + s1_ref[...]) + (s2_ref[...] + s3_ref[...])
    square = jnp.transpose(jnp.broadcast_to(total[0:1, :], (DHEAD, BLOCK)))
    cross = jnp.transpose(jnp.broadcast_to(total[1:2, :], (DHEAD, BLOCK)))
    inverse = lax.rsqrt(square / FEAT + EPSILON)
    pull = inverse * inverse * inverse * cross / FEAT
    lane = lane_index(BLOCK)
    packed = jnp.zeros((BLOCK, DHEAD), jnp.float32)
    stats = [jnp.zeros((rows, DHEAD), jnp.float32) for rows in (64, 16, 4)]
    first_ref[:, WIDTH:KV] = own_ref[0:64, KV:]
    second_ref[:, WIDTH:KV] = own_ref[64:80, KV:]
    third_ref[:, WIDTH:KV] = own_ref[80:84, KV:]
    for h in range(HEADS):
        k = cols(h)
        attention = att_ref[:, k]
        out_ref[:, k] = attention * inverse * gain_ref[0:1, k]
        d_out = inverse * (up_ref[:, k] * gain_ref[0:1, k]) - attention * pull
        dout_ref[0:BLOCK, k] = d_out
        dout_ref[0:BLOCK, cols(h, WIDTH)] = query_ref[:, k]
        delta = wide(jnp.sum(d_out * attention, axis=1, keepdims=True))
        delta_ref[:, k] = delta
        packed = jnp.where(lane == h, lse_ref[:, k], packed)
        packed = jnp.where(lane == HEADS + h, delta, packed)
        level = (lse_ref[:, k], delta, d_out)
        for n, ref in enumerate((first_ref, second_ref, third_ref)):
            level = pooled_cotangent([e.at[h % 2] for e in (e0_ref, e1_ref, e2_ref)], *level)
            rows = level[0].shape[0]
            ref[:, k] = level[2]
            short = lane[0:rows]
            stats[n] = jnp.where(short == h, level[0], jnp.where(short == HEADS + h, level[1], stats[n]))
    first_ref[:, KV:] = stats[0]
    second_ref[:, KV:] = stats[1]
    third_ref[:, KV:] = stats[2]
    dout_ref[BLOCK:, 0:256] = jnp.transpose(packed)[0:8, :]
    dout_ref[BLOCK:, 256:] = jnp.zeros((8, KV - 256), jnp.float32)


def near_query_kernel(
    w0_ref, w1_ref, peak0_ref, peak1_ref, lse_ref, delta_ref, dout_ref,
    k0_ref, k1_ref, k2_ref, v0_ref, v1_ref, v2_ref, dq_ref,
):
    keys = jnp.concatenate([k0_ref[...], k1_ref[...], k2_ref[...]], axis=0)
    values = jnp.concatenate([v0_ref[...], v1_ref[...], v2_ref[...]], axis=0)
    lse = lse_ref[:, 0:1]
    inner = w0_ref[0] * jnp.exp(peak0_ref[:, 0:1] - lse)
    outer = w1_ref[0] * jnp.exp(peak1_ref[:, 0:1] - lse)
    weights = jnp.concatenate([inner, outer], axis=1)
    d_scores = weights * (nt3(dout_ref[...], values) - delta_ref[:, 0:1])
    dq_ref[...] = nn3(d_scores, keys) * INV_ROOT


def far_query_kernel(
    bias_ref, own_ref, a0, a1, a2, a3, a4, first_ref, second_ref, third_ref, near_ref, dq_ref, e0_ref
):
    far = (a0, a1, a2, a3, a4)
    bias = bias_ref[...]

    def grads(lanes):
        fill = jnp.zeros((12, DHEAD), jnp.float32)
        return jnp.concatenate([first_ref[:, lanes], second_ref[:, lanes], third_ref[:, lanes], fill], axis=0)

    stats = grads(slice(KV, GRAD))
    for h in range(HEADS):
        k = cols(h)
        keys = gathered(far, k)
        scores = nt3(own_ref[:, cols(h, 2 * WIDTH)], keys) * INV_ROOT + bias
        weights = jnp.exp(scores - stats[:, h : h + 1])
        d_probs = nt3(grads(k), gathered(far, cols(h, WIDTH)))
        d_scores = weights * (d_probs - stats[:, HEADS + h : HEADS + h + 1])
        grad = nn3(d_scores, keys)
        scales = [INV_ROOT / 4**n for n in (1, 2, 3)]
        dq_ref[:, k] = near_ref[:, k] + expand_levels(e0_ref.at[h % 2], grad, scales)


def near_key_parts(k_ref, v_ref, queries, grads, stats):
    h = pl.program_id(0)
    low = jnp.concatenate([ref[pl.ds(h, 1), :] for ref in stats], axis=1)
    total = jnp.concatenate([ref[pl.ds(h + HEADS, 1), :] for ref in stats], axis=1)
    weights = jnp.exp(nt3(k_ref[...], queries) * INV_ROOT - low)
    d_scores = weights * (nt3(v_ref[...], grads) - total)
    return nn3(d_scores, queries) * INV_ROOT, nn3(weights, grads)


def inner_key_kernel(k_ref, v_ref, q0_ref, q1_ref, d0_ref, d1_ref, t0_ref, t1_ref, dk_ref, dv_ref):
    queries = jnp.concatenate([q0_ref[...], q1_ref[...]], axis=0)
    grads = jnp.concatenate([d0_ref[...], d1_ref[...]], axis=0)
    dk_ref[...], dv_ref[...] = near_key_parts(k_ref, v_ref, queries, grads, (t0_ref, t1_ref))


def outer_key_kernel(k_ref, v_ref, q_ref, d_ref, t_ref, dk_in_ref, dv_in_ref, dk_ref, dv_ref):
    d_keys, d_values = near_key_parts(k_ref, v_ref, q_ref[...], d_ref[...], (t_ref,))
    dk_ref[...] = dk_in_ref[...] + d_keys
    dv_ref[...] = dv_in_ref[...] + d_values


def far_key_parts(own_ref, bias, pieces, h):
    def take(lanes):
        return jnp.concatenate(pieces(lanes), axis=0)

    stats = take(slice(KV, GRAD))
    fill = jnp.zeros((64, DHEAD), jnp.float32)
    stats = jnp.transpose(jnp.concatenate([stats, fill], axis=0))[0:8, 0 : stats.shape[0]]
    queries = take(cols(h, WIDTH))
    grads = take(cols(h))
    scores = nt3(own_ref[:, cols(h)], queries) * INV_ROOT + bias
    weights = jnp.exp(scores - stats[h : h + 1, :])
    d_scores = weights * (nt3(own_ref[:, cols(h, WIDTH)], grads) - stats[HEADS + h : HEADS + h + 1, :])
    return nn3(d_scores, queries) * INV_ROOT, nn3(weights, grads)


def early_key_kernel(bias_ref, own_ref, a0, a1, a2, dk_ref, dv_ref):
    bias = bias_ref[:, 0:EARLY]
    for h in range(HEADS):
        k = cols(h)
        dk_ref[:, k], dv_ref[:, k] = far_key_parts(own_ref, bias, lambda lanes: early((a0, a1, a2), lanes), h)


def late_key_kernel(
    bias_ref, own_ref, a0, a1, far_dk_ref, far_dv_ref, dk_in_ref, dv_in_ref, dk_ref, dv_ref, e0_ref, e1_ref
):
    bias = bias_ref[:, EARLY:FAR]
    scales = [1.0 / 4**n for n in (1, 2, 3)]
    for h in range(HEADS):
        k = cols(h)
        d_keys, d_values = far_key_parts(own_ref, bias, lambda lanes: late((a0, a1), lanes), h)
        d_keys = far_dk_ref[:, k] + d_keys
        d_values = far_dv_ref[:, k] + d_values
        dk_ref[:, k] = dk_in_ref[:, k] + expand_levels(e0_ref.at[h % 2], d_keys, scales)
        dv_ref[:, k] = dv_in_ref[:, k] + expand_levels(e1_ref.at[h % 2], d_values, scales)


def f32(*shape):
    return jax.ShapeDtypeStruct(shape, jnp.float32)


def params():
    return pltpu.CompilerParams(vmem_limit_bytes=VMEM_BYTES)


def cost(flops, size):
    return pl.CostEstimate(flops=int(flops), bytes_accessed=int(size), transcendentals=0)


def whole_call(kernel, outs, scratch, flops, size, *operands):
    spec = pl.BlockSpec(memory_space=pltpu.VMEM)
    return pl.pallas_call(
        kernel,
        out_shape=outs,
        in_specs=[spec] * len(operands),
        out_specs=[spec] * len(outs),
        scratch_shapes=[pltpu.VMEM(shape, jnp.float32) for shape in scratch],
        compiler_params=params(),
        cost_estimate=cost(flops, size),
    )(*operands)


BLOCK_FLOPS = 2.0 * BLOCK * BLOCK * DHEAD * HEADS * 6


def column(first=0):
    return pl.BlockSpec((BLOCK, DHEAD), lambda h: (0, first + h))


def slab(blocks):
    return pl.BlockSpec((1, BLOCK, blocks * BLOCK), lambda h: (h, 0, 0))


def head_call(kernel, outs, out_specs, in_specs, blocks, *operands):
    return pl.pallas_call(
        kernel,
        grid=(HEADS,),
        out_shape=outs,
        in_specs=in_specs,
        out_specs=out_specs,
        compiler_params=params(),
        cost_estimate=cost(blocks * BLOCK_FLOPS, 4e6),
    )(*operands)


def near_inner(query, keys, values):
    k = column()
    outs = [f32(HEADS, BLOCK, 2 * BLOCK)] + [f32(BLOCK, WIDTH)] * 3
    return head_call(near_inner_kernel, outs, [slab(2), k, k, k], [k] * 5, 4, query, *keys, *values)


def near_outer(edge, query, keys, values):
    k = column()
    outs = [f32(HEADS, BLOCK, BLOCK)] + [f32(BLOCK, WIDTH)] * 3
    edge_spec = pl.BlockSpec((8, BLOCK), lambda h: (0, 0))
    return head_call(near_outer_kernel, outs, [slab(1), k, k, k], [edge_spec, k, k, k], 2, edge, query, keys, values)


def near_query(w0, w1, peak0, peak1, lse, delta, d_out, keys, values):
    k = column()
    specs = [slab(2), slab(1)] + [k] * 11
    return head_call(
        near_query_kernel, f32(BLOCK, WIDTH), k, specs, 6, w0, w1, peak0, peak1, lse, delta, d_out, *keys, *values
    )


def stat_rows():
    return pl.BlockSpec((8, 256), lambda h: (BLOCK // 8, 0))


def inner_key(key, value, d_out, d_in):
    k, q, t = column(), column(HEADS), stat_rows()
    return head_call(
        inner_key_kernel, [f32(BLOCK, WIDTH)] * 2, [k, k], [k, k, q, q, k, k, t, t], 8,
        key, value, d_out, d_in, d_out, d_in, d_out, d_in,
    )


def outer_key(key, value, d_far, dk, dv):
    k, q, t = column(), column(HEADS), stat_rows()
    return head_call(
        outer_key_kernel, [f32(BLOCK, WIDTH)] * 2, [k, k], [k, k, q, k, t, k, k], 4,
        key, value, d_far, d_far, d_far, dk, dv,
    )


def pool(key, value, query):
    vmem = pl.BlockSpec(memory_space=pltpu.VMEM)
    hbm = pl.BlockSpec(memory_space=pltpu.HBM)
    return pl.pallas_call(
        pool_kernel,
        out_shape=[
            f32(OWN, 3 * WIDTH), f32(64, KV), f32(16, KV), f32(4, KV), f32(OWN, FAR), f32(8, BLOCK),
        ],
        in_specs=[vmem] + [hbm] * 3,
        out_specs=[vmem] * 6,
        scratch_shapes=[
            pltpu.VMEM((2, BLOCK, DHEAD), jnp.float32),
            pltpu.VMEM((64, DHEAD), jnp.float32),
            pltpu.VMEM((16, DHEAD), jnp.float32),
            pltpu.VMEM((3, BLOCK, WIDTH), jnp.float32),
            pltpu.SemaphoreType.DMA((3, 4)),
        ],
        compiler_params=pltpu.CompilerParams(vmem_limit_bytes=POOL_VMEM_BYTES),
        cost_estimate=cost(1e6, 2e6),
    )(jnp.asarray(slot_table()), key, value, query)


def far_forward(bias, own, far, inner, outer, upstream, gain):
    return whole_call(
        far_forward_kernel,
        [f32(BLOCK, WIDTH), f32(BLOCK, WIDTH), f32(8, 256)],
        [(2, BLOCK, DHEAD)] * 3 + [(BLOCK, DHEAD)] * 2,
        BLOCK_FLOPS,
        8e6,
        bias, own, *far, *inner, *outer, upstream, gain,
    )


def cotangent(stats, others, own, query, attention, lse, upstream, gain):
    return whole_call(
        cotangent_kernel,
        [f32(BLOCK, WIDTH), f32(BLOCK + 8, KV), f32(BLOCK, WIDTH), f32(64, GRAD), f32(16, GRAD), f32(4, GRAD)],
        [(2, BLOCK, DHEAD)] * 3,
        1e6,
        4e6,
        stats, *others, own, query, attention, lse, upstream, gain,
    )


def far_query(bias, own, far, first, second, third, near):
    (grad,) = whole_call(
        far_query_kernel,
        [f32(BLOCK, WIDTH)],
        [(2, BLOCK, DHEAD)],
        BLOCK_FLOPS,
        6e6,
        bias, own, *far, first, second, third, near,
    )
    return grad


def early_key(bias, own, grads):
    return whole_call(early_key_kernel, [f32(OWN, WIDTH)] * 2, [], BLOCK_FLOPS, 3e6, bias, own, *grads)


def late_key(bias, own, grads, far_dk, far_dv, near_dk, near_dv):
    return whole_call(
        late_key_kernel,
        [f32(BLOCK, WIDTH)] * 2,
        [(2, BLOCK, DHEAD)] * 2,
        BLOCK_FLOPS,
        3e6,
        bias, own, *grads, far_dk, far_dv, near_dk, near_dv,
    )


def body(query, key, value, norm_gain, upstream):
    count = lax.axis_size("seq")
    head_count = lax.axis_size("head")

    def exchange(array, mask):
        return lax.ppermute(array, "seq", [(i, i ^ mask) for i in range(count)])

    def exchange_outer(array):
        pairs = [(i, i + 1 if i % 2 else i - 1) for i in range(1, count - 1)]
        return lax.ppermute(array, "seq", pairs)

    def after(array, *tokens):
        return lax.optimization_barrier((array,) + tokens)[0]

    def packed(second, thirds):
        return whole_call(pack_kernel, [f32(28, second.shape[1])], [], 1e4, 1e5, second, *thirds)[0]

    def doubled(pack, other):
        return whole_call(double_kernel, [f32(56, pack.shape[1])], [], 1e4, 1e5, pack, other)[0]

    def merged(first, double, other):
        width = first.shape[1]
        return whole_call(merge_kernel, [f32(96, width), f32(160, width)], [], 1e4, 1e5, first, double, other)

    gain = norm_gain.reshape(1, WIDTH)
    out_k, out_v = exchange_outer(key), exchange_outer(value)
    in_k, in_v = exchange(key, 1), exchange(value, 1)
    own, first, second, third, bias, edge = pool(key, value, query)

    held = after(third, in_k, in_v)
    planes = [exchange(after(held, out_k), PLANES[0])] + [exchange(held, mask) for mask in PLANES[1:]]
    l1a = exchange(first, 2)
    pack = packed(after(second, out_k), planes)
    double = doubled(after(pack, l1a), exchange(pack, 4))
    other = exchange(double, 12)
    w0, *inner = near_inner(query, (key, after(in_k, double)), (value, in_v))
    w1, *outer = near_outer(edge, query, after(out_k, double), out_v)
    l2a, bundle = merged(l1a, after(double, w0, w1), other)
    l2b = exchange(l2a, 2)
    core1 = exchange(bundle, 1)
    core2 = exchange(after(l2b, core1), 1)
    far = (l1a, l2a, core1, l2b, core2)
    attention, lse, stats = far_forward(bias, own, far, inner, outer, upstream, gain)

    others = [
        lax.ppermute(stats, "head", [(i, i ^ mask) for i in range(head_count)]) for mask in range(1, head_count)
    ]
    attended, d_out, delta, g1, g2, g3 = cotangent(stats, others, own, query, attention, lse, upstream, gain)

    planes = [exchange(g3, mask) for mask in PLANES]
    l1a = exchange(g1, 2)
    d_far = exchange_outer(d_out)
    pack = packed(g2, planes)
    d_in = exchange(after(d_out, pack), 1)
    quad = exchange(pack, 4)
    near_dq = near_query(
        w0, w1, inner[0], outer[0], lse, delta, after(d_out, pack),
        (key, in_k, out_k), (value, in_v, out_v),
    )
    double = doubled(after(pack, near_dq, d_far), quad)
    other = exchange(double, 12)
    near_dk, near_dv = inner_key(key, value, d_out, after(d_in, double))
    query_grad = far_query(bias, own, far, after(g1, double), g2, g3, near_dq)
    l2a, bundle = merged(l1a, after(double, near_dk, query_grad), other)
    l2b = exchange(l2a, 2)
    core1 = exchange(bundle, 1)
    near_dk, near_dv = outer_key(key, value, after(d_far, l2a), near_dk, near_dv)
    far_dk, far_dv = early_key(bias, own, (l1a, after(l2a, near_dk), core1))
    core2 = exchange(after(l2b, far_dk), 1)
    key_grad, value_grad = late_key(bias, own, (l2b, core2), far_dk, far_dv, near_dk, near_dv)
    return attended, query_grad, key_grad, value_grad


def solution(mesh):
    return jax.shard_map(
        body,
        mesh=mesh,
        in_specs=(
            P("seq", "head"),
            P("seq", "head"),
            P("seq", "head"),
            P("head"),
            P("seq", "head"),
        ),
        out_specs=(P("seq", "head"), P("seq", "head"), P("seq", "head"), P("seq", "head")),
        check_vma=False,
    )
```

```python
import math

import jax
import jax.numpy as jnp
import numpy as np
from jax import lax
from jax.experimental import pallas as pl
from jax.experimental.pallas import tpu as pltpu
from jax.sharding import PartitionSpec as P

DHEAD = 128
BLOCK = 256
FEAT = 2048
HEADS = 4
WIDTH = HEADS * DHEAD
NEGATIVE_FILL = -1e30
FLOOR = -1e25
EPSILON = 1e-06
INV_ROOT = 1.0 / math.sqrt(DHEAD)
LN4 = math.log(4.0)
VMEM_BYTES = 24 * 1024 * 1024
POOL_VMEM_BYTES = 56 * 1024 * 1024

OWN = 96
LEVEL_ROWS = ((0, 64), (64, 80), (80, 84))
FAR = 512
KV = 2 * WIDTH
GRAD = 2 * WIDTH + DHEAD

QUAD = (4, 12, 8)
PLANES = (16, 32, 48)
THIRD_BLOCKS = tuple(y ^ o for o in (0,) + QUAD for y in PLANES)


def flipped(blocks, mask):
    return tuple(o ^ mask for o in blocks)


SLOTS = (
    (1, (2, 3)),
    (2, QUAD),
    (2, flipped(QUAD, 1)),
    (3, THIRD_BLOCKS),
    (3, flipped(THIRD_BLOCKS, 1)),
    (2, flipped(QUAD, 2)),
    (2, flipped(QUAD, 3)),
    (3, flipped(THIRD_BLOCKS, 2)),
    (3, flipped(THIRD_BLOCKS, 3)),
)
EARLY = 320


def slot_table():
    rows = {1: 64, 2: 16, 3: 4}
    offset = np.concatenate([np.repeat(np.array(blocks, np.int32), rows[n]) for n, blocks in SLOTS])
    level = np.concatenate([np.full(len(blocks) * rows[n], n, np.int32) for n, blocks in SLOTS])
    table = np.zeros((8, FAR), np.int32)
    table[0], table[1] = offset, level
    return table


def split3(x):
    high = x.astype(jnp.bfloat16)
    rest = x - high.astype(jnp.float32)
    middle = rest.astype(jnp.bfloat16)
    return high, middle, (rest - middle.astype(jnp.float32)).astype(jnp.bfloat16)


def dot(a, b, dims):
    return lax.dot_general(a, b, (dims, ((), ())), preferred_element_type=jnp.float32)


def nt3(a, b):
    a1, a2, a3 = split3(a)
    b1, b2, b3 = split3(b)
    left = jnp.concatenate([a1, a2, a1, a2, a1, a3], axis=1)
    right = jnp.concatenate([b1, b1, b2, b2, b3, b1], axis=1)
    return dot(left, right, ((1,), (1,)))


def nn3(a, b):
    a1, a2, a3 = split3(a)
    b1, b2, b3 = split3(b)
    right = jnp.concatenate([b1, b2], axis=1)
    main = dot(jnp.concatenate([a1, a2], axis=1), jnp.concatenate([right, right], axis=0), ((1,), (0,)))
    small = dot(jnp.concatenate([a1, a3], axis=1), jnp.concatenate([b3, b1], axis=0), ((1,), (0,)))
    return main[:, :DHEAD] + (main[:, DHEAD:] + small)


def cols(h, base=0):
    return slice(base + h * DHEAD, base + (h + 1) * DHEAD)


def quarters(ref, value):
    rows = value.shape[0] // 4
    ref[pl.ds(0, 4 * rows), :] = value
    return [ref[pl.ds(j, rows, stride=4), :] for j in range(4)]


def mean4(ref, value):
    parts = quarters(ref, value)
    return ((parts[0] + parts[1]) + (parts[2] + parts[3])) * 0.25


def expand(ref, value):
    rows = value.shape[0]
    for j in range(4):
        ref[pl.ds(j, rows, stride=4), :] = value
    return ref[pl.ds(0, 4 * rows), :]


def expand_levels(ref, value, scales):
    total = value[80:84] * scales[2]
    total = value[64:80] * scales[1] + expand(ref, total)
    total = value[0:64] * scales[0] + expand(ref, total)
    return expand(ref, total)


def lane_index(rows):
    return lax.broadcasted_iota(jnp.int32, (rows, DHEAD), 1)


def wide(column):
    return jnp.broadcast_to(column, (column.shape[0], DHEAD))


def early(refs, lanes):
    l1a, l2a, core1 = refs
    pieces = [l1a[:, lanes], core1[0:64, lanes], l2a[0:48, lanes], core1[64:112, lanes]]
    return pieces + [l2a[48:96, lanes], core1[112:160, lanes]]


def late(refs, lanes):
    l2b, core2 = refs
    return [l2b[0:48, lanes], core2[0:48, lanes], l2b[48:96, lanes], core2[48:96, lanes]]


def gathered(refs, lanes):
    return jnp.concatenate(early(refs[0:3], lanes) + late(refs[3:5], lanes), axis=0)


def pool_kernel(
    table_ref, k_ref, v_ref, q_ref,
    own_ref, first_ref, second_ref, third_ref, bias_ref, edge_ref,
    e0_ref, e1_ref, e2_ref, in_ref, sems,
):
    copies = []
    for i, ref in enumerate((k_ref, v_ref, q_ref)):
        for j in range(4):
            rows = pl.ds(64 * j, 64)
            copies.append(pltpu.make_async_copy(ref.at[rows, :], in_ref.at[i, rows, :], sems.at[i, j]))
    for copy in copies:
        copy.start()
    place = lax.axis_index("seq")
    last = lax.axis_size("seq") - 1
    offset = table_ref[0:1, :]
    level = table_ref[1:2, :]
    row = lax.broadcasted_iota(jnp.int32, (OWN, FAR), 0)
    mine = jnp.where(row < 64, 1, jnp.where(row < 80, 2, jnp.where(row < 84, 3, 0)))
    allowed = (jnp.abs((offset ^ place) - place) > 1) & (level == mine)
    bias_ref[...] = jnp.where(allowed, level.astype(jnp.float32) * LN4, NEGATIVE_FILL)
    alone = (place == 0) | (place == last)
    edge_ref[...] = jnp.full((8, BLOCK), jnp.where(alone, NEGATIVE_FILL, 0.0), jnp.float32)
    own_ref[84:96, :] = jnp.zeros((12, 3 * WIDTH), jnp.float32)
    for part in range(3):
        for copy in copies[4 * part : 4 * part + 4]:
            copy.wait()
        for h in range(HEADS):
            dst = cols(h, part * WIDTH)
            value = in_ref[part, :, cols(h)]
            one = mean4(e0_ref.at[(part * HEADS + h) % 2], value)
            two = mean4(e1_ref, one)
            three = mean4(e2_ref, two)
            own_ref[0:64, dst] = one
            own_ref[64:80, dst] = two
            own_ref[80:84, dst] = three
            if part < 2:
                first_ref[:, dst] = one
                second_ref[:, dst] = two
                third_ref[:, dst] = three


def pack_kernel(second_ref, a_ref, b_ref, c_ref, out_ref):
    out_ref[0:16, :] = second_ref[...]
    out_ref[16:20, :] = a_ref[...]
    out_ref[20:24, :] = b_ref[...]
    out_ref[24:28, :] = c_ref[...]


def double_kernel(own_ref, other_ref, out_ref):
    out_ref[0:28, :] = own_ref[...]
    out_ref[28:56, :] = other_ref[...]


def merge_kernel(first_ref, double_ref, other_ref, out_ref, bundle_ref):
    bundle_ref[0:64, :] = first_ref[...]
    parts = (double_ref[28:56, :], other_ref[0:28, :], other_ref[28:56, :])
    pieces = [(16 * i, part[0:16]) for i, part in enumerate(parts)]
    pieces += [(48 + 12 * i, part[16:28]) for i, part in enumerate((double_ref[0:28, :],) + parts)]
    for start, piece in pieces:
        stop = start + piece.shape[0]
        out_ref[start:stop, :] = piece
        bundle_ref[64 + start : 64 + stop, :] = piece


def near_state(scores, values, w_ref, peak_ref, mass_ref, sum_ref):
    peak = jnp.maximum(jnp.max(scores, axis=1, keepdims=True), FLOOR)
    weights = jnp.exp(scores - peak)
    w_ref[0] = weights
    peak_ref[...] = wide(peak)
    mass_ref[...] = wide(jnp.sum(weights, axis=1, keepdims=True))
    sum_ref[...] = nn3(weights, values)


def near_inner_kernel(q_ref, ko_ref, ki_ref, vo_ref, vi_ref, *outs):
    keys = jnp.concatenate([ko_ref[...], ki_ref[...]], axis=0)
    values = jnp.concatenate([vo_ref[...], vi_ref[...]], axis=0)
    near_state(nt3(q_ref[...], keys) * INV_ROOT, values, *outs)


def near_outer_kernel(edge_ref, q_ref, k_ref, v_ref, *outs):
    near_state(nt3(q_ref[...], k_ref[...]) * INV_ROOT + edge_ref[0:1, :], v_ref[...], *outs)


def merge(one, two):
    peak = jnp.maximum(one[0], two[0])
    left = jnp.exp(one[0] - peak)
    right = jnp.exp(two[0] - peak)
    return peak, left * one[1] + right * two[1], left * one[2] + right * two[2]


def far_forward_kernel(
    bias_ref, own_ref, a0, a1, a2, a3, a4,
    peak0_ref, mass0_ref, sum0_ref, peak1_ref, mass1_ref, sum1_ref, up_ref, gain_ref,
    att_ref, lse_ref, stat_ref,
    e0_ref, e1_ref, e2_ref, square_ref, cross_ref,
):
    far = (a0, a1, a2, a3, a4)
    bias = bias_ref[...]
    for h in range(HEADS):
        k = cols(h)
        v = cols(h, WIDTH)
        scores = nt3(own_ref[:, cols(h, 2 * WIDTH)], gathered(far, k)) * INV_ROOT + bias
        peak = jnp.maximum(jnp.max(scores, axis=1, keepdims=True), FLOOR)
        weights = jnp.exp(scores - peak)
        mass = jnp.sum(weights, axis=1, keepdims=True)
        levels = (wide(peak), wide(mass), nn3(weights, gathered(far, v)))
        state = tuple(x[80:84] for x in levels)
        for start, stop in (LEVEL_ROWS[1], LEVEL_ROWS[0]):
            state = tuple(expand(ref.at[h % 2], x) for ref, x in zip((e0_ref, e1_ref, e2_ref), state))
            state = merge(state, tuple(x[start:stop] for x in levels))
        state = tuple(expand(ref.at[h % 2], x) for ref, x in zip((e0_ref, e1_ref, e2_ref), state))
        near = merge(
            (peak0_ref[:, k], mass0_ref[:, k], sum0_ref[:, k]), (peak1_ref[:, k], mass1_ref[:, k], sum1_ref[:, k])
        )
        state = merge(state, near)
        attention = state[2] / state[1]
        att_ref[:, k] = attention
        lse_ref[:, k] = state[0] + jnp.log(state[1])
        square = attention * attention
        cross = up_ref[:, k] * gain_ref[0:1, k] * attention
        if h == 0:
            square_ref[...] = square
            cross_ref[...] = cross
        else:
            square_ref[...] += square
            cross_ref[...] += cross
    square = wide(jnp.sum(square_ref[...], axis=1, keepdims=True))
    cross = wide(jnp.sum(cross_ref[...], axis=1, keepdims=True))
    packed = jnp.where(lane_index(BLOCK) == 0, square, cross)
    stat_ref[...] = jnp.transpose(packed)[0:8, :]


def pooled_cotangent(scratch, lows, dots, grads):
    lows, dots, grads = (quarters(ref, x) for ref, x in zip(scratch, (lows, dots, grads)))
    low = jnp.minimum(jnp.minimum(lows[0], lows[1]), jnp.minimum(lows[2], lows[3]))
    scale = [jnp.exp(low - x) for x in lows]
    total = scale[0] * dots[0]
    grad = scale[0] * grads[0]
    for j in range(1, 4):
        total = total + scale[j] * dots[j]
        grad = grad + scale[j] * grads[j]
    return low, total, grad


def cotangent_kernel(
    s0_ref, s1_ref, s2_ref, s3_ref, own_ref, att_ref, lse_ref, up_ref, gain_ref,
    out_ref, dout_ref, delta_ref, first_ref, second_ref, third_ref,
    e0_ref, e1_ref, e2_ref,
):
    total = (s0_ref[...] + s1_ref[...]) + (s2_ref[...] + s3_ref[...])
    square = jnp.transpose(jnp.broadcast_to(total[0:1, :], (DHEAD, BLOCK)))
    cross = jnp.transpose(jnp.broadcast_to(total[1:2, :], (DHEAD, BLOCK)))
    inverse = lax.rsqrt(square / FEAT + EPSILON)
    pull = inverse * inverse * inverse * cross / FEAT
    lane = lane_index(BLOCK)
    packed = jnp.zeros((BLOCK, DHEAD), jnp.float32)
    stats = [jnp.zeros((rows, DHEAD), jnp.float32) for rows in (64, 16, 4)]
    first_ref[:, WIDTH:KV] = own_ref[0:64, KV:]
    second_ref[:, WIDTH:KV] = own_ref[64:80, KV:]
    third_ref[:, WIDTH:KV] = own_ref[80:84, KV:]
    for h in range(HEADS):
        k = cols(h)
        attention = att_ref[:, k]
        out_ref[:, k] = attention * inverse * gain_ref[0:1, k]
        d_out = inverse * (up_ref[:, k] * gain_ref[0:1, k]) - attention * pull
        dout_ref[0:BLOCK, k] = d_out
        delta = wide(jnp.sum(d_out * attention, axis=1, keepdims=True))
        delta_ref[:, k] = delta
        packed = jnp.where(lane == h, lse_ref[:, k], packed)
        packed = jnp.where(lane == HEADS + h, delta, packed)
        level = (lse_ref[:, k], delta, d_out)
        for n, ref in enumerate((first_ref, second_ref, third_ref)):
            level = pooled_cotangent([e.at[h % 2] for e in (e0_ref, e1_ref, e2_ref)], *level)
            rows = level[0].shape[0]
            ref[:, k] = level[2]
            short = lane[0:rows]
            stats[n] = jnp.where(short == h, level[0], jnp.where(short == HEADS + h, level[1], stats[n]))
    first_ref[:, KV:] = stats[0]
    second_ref[:, KV:] = stats[1]
    third_ref[:, KV:] = stats[2]
    dout_ref[BLOCK:, 0:256] = jnp.transpose(packed)[0:8, :]
    dout_ref[BLOCK:, 256:] = jnp.zeros((8, 256), jnp.float32)


def near_query_kernel(
    w0_ref, w1_ref, peak0_ref, peak1_ref, lse_ref, delta_ref, dout_ref,
    k0_ref, k1_ref, k2_ref, v0_ref, v1_ref, v2_ref, dq_ref,
):
    keys = jnp.concatenate([k0_ref[...], k1_ref[...], k2_ref[...]], axis=0)
    values = jnp.concatenate([v0_ref[...], v1_ref[...], v2_ref[...]], axis=0)
    lse = lse_ref[:, 0:1]
    inner = w0_ref[0] * jnp.exp(peak0_ref[:, 0:1] - lse)
    outer = w1_ref[0] * jnp.exp(peak1_ref[:, 0:1] - lse)
    weights = jnp.concatenate([inner, outer], axis=1)
    d_scores = weights * (nt3(dout_ref[...], values) - delta_ref[:, 0:1])
    dq_ref[...] = nn3(d_scores, keys) * INV_ROOT


def far_query_kernel(
    bias_ref, own_ref, a0, a1, a2, a3, a4, first_ref, second_ref, third_ref, near_ref, dq_ref, e0_ref
):
    far = (a0, a1, a2, a3, a4)
    bias = bias_ref[...]

    def grads(lanes):
        fill = jnp.zeros((12, DHEAD), jnp.float32)
        return jnp.concatenate([first_ref[:, lanes], second_ref[:, lanes], third_ref[:, lanes], fill], axis=0)

    stats = grads(slice(KV, GRAD))
    for h in range(HEADS):
        k = cols(h)
        keys = gathered(far, k)
        scores = nt3(own_ref[:, cols(h, 2 * WIDTH)], keys) * INV_ROOT + bias
        weights = jnp.exp(scores - stats[:, h : h + 1])
        d_probs = nt3(grads(k), gathered(far, cols(h, WIDTH)))
        d_scores = weights * (d_probs - stats[:, HEADS + h : HEADS + h + 1])
        grad = nn3(d_scores, keys)
        scales = [INV_ROOT / 4**n for n in (1, 2, 3)]
        dq_ref[:, k] = near_ref[:, k] + expand_levels(e0_ref.at[h % 2], grad, scales)


def near_key_parts(k_ref, v_ref, queries, grads, stats):
    h = pl.program_id(0)
    low = jnp.concatenate([ref[pl.ds(h, 1), :] for ref in stats], axis=1)
    total = jnp.concatenate([ref[pl.ds(h + HEADS, 1), :] for ref in stats], axis=1)
    weights = jnp.exp(nt3(k_ref[...], queries) * INV_ROOT - low)
    d_scores = weights * (nt3(v_ref[...], grads) - total)
    return nn3(d_scores, queries) * INV_ROOT, nn3(weights, grads)


def inner_key_kernel(k_ref, v_ref, q0_ref, q1_ref, d0_ref, d1_ref, t0_ref, t1_ref, dk_ref, dv_ref):
    queries = jnp.concatenate([q0_ref[...], q1_ref[...]], axis=0)
    grads = jnp.concatenate([d0_ref[...], d1_ref[...]], axis=0)
    dk_ref[...], dv_ref[...] = near_key_parts(k_ref, v_ref, queries, grads, (t0_ref, t1_ref))


def outer_key_kernel(k_ref, v_ref, q_ref, d_ref, t_ref, dk_in_ref, dv_in_ref, dk_ref, dv_ref):
    d_keys, d_values = near_key_parts(k_ref, v_ref, q_ref[...], d_ref[...], (t_ref,))
    dk_ref[...] = dk_in_ref[...] + d_keys
    dv_ref[...] = dv_in_ref[...] + d_values


def far_key_parts(own_ref, bias, pieces, h):
    def take(lanes):
        return jnp.concatenate(pieces(lanes), axis=0)

    stats = take(slice(KV, GRAD))
    fill = jnp.zeros((64, DHEAD), jnp.float32)
    stats = jnp.transpose(jnp.concatenate([stats, fill], axis=0))[0:8, 0 : stats.shape[0]]
    queries = take(cols(h, WIDTH))
    grads = take(cols(h))
    scores = nt3(own_ref[:, cols(h)], queries) * INV_ROOT + bias
    weights = jnp.exp(scores - stats[h : h + 1, :])
    d_scores = weights * (nt3(own_ref[:, cols(h, WIDTH)], grads) - stats[HEADS + h : HEADS + h + 1, :])
    return nn3(d_scores, queries) * INV_ROOT, nn3(weights, grads)


def early_key_kernel(bias_ref, own_ref, a0, a1, a2, dk_ref, dv_ref):
    bias = bias_ref[:, 0:EARLY]
    for h in range(HEADS):
        k = cols(h)
        dk_ref[:, k], dv_ref[:, k] = far_key_parts(own_ref, bias, lambda lanes: early((a0, a1, a2), lanes), h)


def late_key_kernel(
    bias_ref, own_ref, a0, a1, far_dk_ref, far_dv_ref, dk_in_ref, dv_in_ref, dk_ref, dv_ref, e0_ref, e1_ref
):
    bias = bias_ref[:, EARLY:FAR]
    scales = [1.0 / 4**n for n in (1, 2, 3)]
    for h in range(HEADS):
        k = cols(h)
        d_keys, d_values = far_key_parts(own_ref, bias, lambda lanes: late((a0, a1), lanes), h)
        d_keys = far_dk_ref[:, k] + d_keys
        d_values = far_dv_ref[:, k] + d_values
        dk_ref[:, k] = dk_in_ref[:, k] + expand_levels(e0_ref.at[h % 2], d_keys, scales)
        dv_ref[:, k] = dv_in_ref[:, k] + expand_levels(e1_ref.at[h % 2], d_values, scales)


def f32(*shape):
    return jax.ShapeDtypeStruct(shape, jnp.float32)


def params():
    return pltpu.CompilerParams(vmem_limit_bytes=VMEM_BYTES)


def cost(flops, size):
    return pl.CostEstimate(flops=int(flops), bytes_accessed=int(size), transcendentals=0)


def whole_call(kernel, outs, scratch, flops, size, *operands):
    spec = pl.BlockSpec(memory_space=pltpu.VMEM)
    return pl.pallas_call(
        kernel,
        out_shape=outs,
        in_specs=[spec] * len(operands),
        out_specs=[spec] * len(outs),
        scratch_shapes=[pltpu.VMEM(shape, jnp.float32) for shape in scratch],
        compiler_params=params(),
        cost_estimate=cost(flops, size),
    )(*operands)


BLOCK_FLOPS = 2.0 * BLOCK * BLOCK * DHEAD * HEADS * 6


def column():
    return pl.BlockSpec((BLOCK, DHEAD), lambda h: (0, h))


def slab(blocks):
    return pl.BlockSpec((1, BLOCK, blocks * BLOCK), lambda h: (h, 0, 0))


def head_call(kernel, outs, out_specs, in_specs, blocks, *operands):
    return pl.pallas_call(
        kernel,
        grid=(HEADS,),
        out_shape=outs,
        in_specs=in_specs,
        out_specs=out_specs,
        compiler_params=params(),
        cost_estimate=cost(blocks * BLOCK_FLOPS, 4e6),
    )(*operands)


def near_inner(query, keys, values):
    k = column()
    outs = [f32(HEADS, BLOCK, 2 * BLOCK)] + [f32(BLOCK, WIDTH)] * 3
    return head_call(near_inner_kernel, outs, [slab(2), k, k, k], [k] * 5, 4, query, *keys, *values)


def near_outer(edge, query, keys, values):
    k = column()
    outs = [f32(HEADS, BLOCK, BLOCK)] + [f32(BLOCK, WIDTH)] * 3
    edge_spec = pl.BlockSpec((8, BLOCK), lambda h: (0, 0))
    return head_call(near_outer_kernel, outs, [slab(1), k, k, k], [edge_spec, k, k, k], 2, edge, query, keys, values)


def near_query(w0, w1, peak0, peak1, lse, delta, d_out, keys, values):
    k = column()
    specs = [slab(2), slab(1)] + [k] * 11
    return head_call(
        near_query_kernel, f32(BLOCK, WIDTH), k, specs, 6, w0, w1, peak0, peak1, lse, delta, d_out, *keys, *values
    )


def stat_rows():
    return pl.BlockSpec((8, 256), lambda h: (BLOCK // 8, 0))


def inner_key(key, value, query, query_in, d_out, d_in):
    k, t = column(), stat_rows()
    return head_call(
        inner_key_kernel, [f32(BLOCK, WIDTH)] * 2, [k, k], [k] * 6 + [t, t], 8,
        key, value, query, query_in, d_out, d_in, d_out, d_in,
    )


def outer_key(key, value, query_out, d_far, dk, dv):
    k, t = column(), stat_rows()
    return head_call(
        outer_key_kernel, [f32(BLOCK, WIDTH)] * 2, [k, k], [k] * 4 + [t, k, k], 4,
        key, value, query_out, d_far, d_far, dk, dv,
    )


def pool(key, value, query):
    vmem = pl.BlockSpec(memory_space=pltpu.VMEM)
    hbm = pl.BlockSpec(memory_space=pltpu.HBM)
    return pl.pallas_call(
        pool_kernel,
        out_shape=[
            f32(OWN, 3 * WIDTH), f32(64, KV), f32(16, KV), f32(4, KV), f32(OWN, FAR), f32(8, BLOCK),
        ],
        in_specs=[vmem] + [hbm] * 3,
        out_specs=[vmem] * 6,
        scratch_shapes=[
            pltpu.VMEM((2, BLOCK, DHEAD), jnp.float32),
            pltpu.VMEM((64, DHEAD), jnp.float32),
            pltpu.VMEM((16, DHEAD), jnp.float32),
            pltpu.VMEM((3, BLOCK, WIDTH), jnp.float32),
            pltpu.SemaphoreType.DMA((3, 4)),
        ],
        compiler_params=pltpu.CompilerParams(vmem_limit_bytes=POOL_VMEM_BYTES),
        cost_estimate=cost(1e6, 2e6),
    )(jnp.asarray(slot_table()), key, value, query)


def far_forward(bias, own, far, inner, outer, upstream, gain):
    return whole_call(
        far_forward_kernel,
        [f32(BLOCK, WIDTH), f32(BLOCK, WIDTH), f32(8, 256)],
        [(2, BLOCK, DHEAD)] * 3 + [(BLOCK, DHEAD)] * 2,
        BLOCK_FLOPS,
        8e6,
        bias, own, *far, *inner, *outer, upstream, gain,
    )


def cotangent(stats, others, own, attention, lse, upstream, gain):
    return whole_call(
        cotangent_kernel,
        [f32(BLOCK, WIDTH), f32(BLOCK + 8, WIDTH), f32(BLOCK, WIDTH), f32(64, GRAD), f32(16, GRAD), f32(4, GRAD)],
        [(2, BLOCK, DHEAD)] * 3,
        1e6,
        4e6,
        stats, *others, own, attention, lse, upstream, gain,
    )


def far_query(bias, own, far, first, second, third, near):
    (grad,) = whole_call(
        far_query_kernel,
        [f32(BLOCK, WIDTH)],
        [(2, BLOCK, DHEAD)],
        BLOCK_FLOPS,
        6e6,
        bias, own, *far, first, second, third, near,
    )
    return grad


def early_key(bias, own, grads):
    return whole_call(early_key_kernel, [f32(OWN, WIDTH)] * 2, [], BLOCK_FLOPS, 3e6, bias, own, *grads)


def late_key(bias, own, grads, far_dk, far_dv, near_dk, near_dv):
    return whole_call(
        late_key_kernel,
        [f32(BLOCK, WIDTH)] * 2,
        [(2, BLOCK, DHEAD)] * 2,
        BLOCK_FLOPS,
        3e6,
        bias, own, *grads, far_dk, far_dv, near_dk, near_dv,
    )


def body(query, key, value, norm_gain, upstream):
    count = lax.axis_size("seq")
    head_count = lax.axis_size("head")

    def exchange(array, mask):
        return lax.ppermute(array, "seq", [(i, i ^ mask) for i in range(count)])

    def exchange_outer(array):
        pairs = [(i, i + 1 if i % 2 else i - 1) for i in range(1, count - 1)]
        return lax.ppermute(array, "seq", pairs)

    def after(array, *tokens):
        return lax.optimization_barrier((array,) + tokens)[0]

    def packed(second, thirds):
        return whole_call(pack_kernel, [f32(28, second.shape[1])], [], 1e4, 1e5, second, *thirds)[0]

    def doubled(pack, other):
        return whole_call(double_kernel, [f32(56, pack.shape[1])], [], 1e4, 1e5, pack, other)[0]

    def merged(first, double, other):
        width = first.shape[1]
        return whole_call(merge_kernel, [f32(96, width), f32(160, width)], [], 1e4, 1e5, first, double, other)

    gain = norm_gain.reshape(1, WIDTH)
    out_k, out_v = exchange_outer(key), exchange_outer(value)
    in_k, in_v = exchange(key, 1), exchange(value, 1)
    own, first, second, third, bias, edge = pool(key, value, query)

    held = after(third, in_k, in_v)
    planes = [exchange(after(held, out_k), PLANES[0])] + [exchange(held, mask) for mask in PLANES[1:]]
    l1a = exchange(first, 2)
    pack = packed(after(second, out_k), planes)
    double = doubled(after(pack, l1a), exchange(pack, 4))
    other = exchange(double, 12)
    w0, *inner = near_inner(query, (key, after(in_k, double)), (value, in_v))
    w1, *outer = near_outer(edge, query, after(out_k, double), out_v)
    l2a, bundle = merged(l1a, after(double, w0, w1), other)
    l2b = exchange(l2a, 2)
    core1 = exchange(bundle, 1)
    core2 = exchange(after(l2b, core1), 1)
    query_in = exchange(after(query, l2a), 1)
    query_out = exchange_outer(after(query, l2a))
    far = (l1a, l2a, core1, l2b, core2)
    attention, lse, stats = far_forward(bias, own, far, inner, outer, upstream, gain)

    others = [
        lax.ppermute(stats, "head", [(i, i ^ mask) for i in range(head_count)]) for mask in range(1, head_count)
    ]
    attention = after(attention, query_in, query_out)
    attended, d_out, delta, g1, g2, g3 = cotangent(stats, others, own, attention, lse, upstream, gain)

    planes = [exchange(g3, mask) for mask in PLANES]
    l1a = exchange(g1, 2)
    d_in = exchange(d_out, 1)
    pack = packed(g2, planes)
    quad = exchange(pack, 4)
    near_dq = near_query(
        w0, w1, inner[0], outer[0], lse, delta, after(d_out, pack), (key, in_k, out_k), (value, in_v, out_v)
    )
    double = doubled(after(pack, near_dq, l1a), quad)
    other = exchange(double, 12)
    d_far = exchange_outer(after(d_out, double))
    near_dk, near_dv = inner_key(key, value, query, query_in, d_out, after(d_in, double))
    query_grad = far_query(bias, own, far, after(g1, double), g2, g3, near_dq)
    l2a, bundle = merged(l1a, after(double, near_dk, query_grad, d_far), other)
    l2b = exchange(l2a, 2)
    core1 = exchange(bundle, 1)
    near_dk, near_dv = outer_key(key, value, query_out, after(d_far, l2a), near_dk, near_dv)
    far_dk, far_dv = early_key(bias, own, (l1a, after(l2a, near_dk), core1))
    core2 = exchange(after(l2b, far_dk), 1)
    key_grad, value_grad = late_key(bias, own, (l2b, core2), far_dk, far_dv, near_dk, near_dv)
    return attended, query_grad, key_grad, value_grad


def solution(mesh):
    return jax.shard_map(
        body,
        mesh=mesh,
        in_specs=(
            P("seq", "head"),
            P("seq", "head"),
            P("seq", "head"),
            P("head"),
            P("seq", "head"),
        ),
        out_specs=(P("seq", "head"), P("seq", "head"), P("seq", "head"), P("seq", "head")),
        check_vma=False,
    )
```

```python
import math

import jax
import jax.numpy as jnp
import numpy as np
from jax import lax
from jax.experimental import pallas as pl
from jax.experimental.pallas import tpu as pltpu
from jax.sharding import PartitionSpec as P

DHEAD = 128
BLOCK = 256
FEAT = 2048
HEADS = 4
WIDTH = HEADS * DHEAD
NEGATIVE_FILL = -1e30
FLOOR = -1e25
EPSILON = 1e-06
INV_ROOT = 1.0 / math.sqrt(DHEAD)
LN4 = math.log(4.0)
VMEM_BYTES = 24 * 1024 * 1024
POOL_VMEM_BYTES = 56 * 1024 * 1024

OWN = 96
LEVEL_ROWS = ((0, 64), (64, 80), (80, 84))
FAR = 512
KV = 2 * WIDTH
GRAD = 2 * WIDTH + DHEAD

QUAD = (4, 12, 8)
PLANES = (16, 32, 48)
THIRD_BLOCKS = tuple(y ^ o for o in (0,) + QUAD for y in PLANES)


def flipped(blocks, mask):
    return tuple(o ^ mask for o in blocks)


SLOTS = (
    (1, (2, 3)),
    (2, QUAD),
    (3, THIRD_BLOCKS),
    (2, flipped(QUAD, 1)),
    (3, flipped(THIRD_BLOCKS, 1)),
    (2, flipped(QUAD, 2)),
    (2, flipped(QUAD, 3)),
    (3, flipped(THIRD_BLOCKS, 2)),
    (3, flipped(THIRD_BLOCKS, 3)),
)
EARLY = 224


def slot_table():
    rows = {1: 64, 2: 16, 3: 4}
    offset = np.concatenate([np.repeat(np.array(blocks, np.int32), rows[n]) for n, blocks in SLOTS])
    level = np.concatenate([np.full(len(blocks) * rows[n], n, np.int32) for n, blocks in SLOTS])
    table = np.zeros((8, FAR), np.int32)
    table[0], table[1] = offset, level
    return table


def split3(x):
    high = x.astype(jnp.bfloat16)
    rest = x - high.astype(jnp.float32)
    middle = rest.astype(jnp.bfloat16)
    return high, middle, (rest - middle.astype(jnp.float32)).astype(jnp.bfloat16)


def dot(a, b, dims):
    return lax.dot_general(a, b, (dims, ((), ())), preferred_element_type=jnp.float32)


def nt3(a, b):
    a1, a2, a3 = split3(a)
    b1, b2, b3 = split3(b)
    left = jnp.concatenate([a1, a2, a1, a2, a1, a3], axis=1)
    right = jnp.concatenate([b1, b1, b2, b2, b3, b1], axis=1)
    return dot(left, right, ((1,), (1,)))


def nn3(a, b):
    a1, a2, a3 = split3(a)
    b1, b2, b3 = split3(b)
    right = jnp.concatenate([b1, b2], axis=1)
    main = dot(jnp.concatenate([a1, a2], axis=1), jnp.concatenate([right, right], axis=0), ((1,), (0,)))
    small = dot(jnp.concatenate([a1, a3], axis=1), jnp.concatenate([b3, b1], axis=0), ((1,), (0,)))
    return main[:, :DHEAD] + (main[:, DHEAD:] + small)


def cols(h, base=0):
    return slice(base + h * DHEAD, base + (h + 1) * DHEAD)


def quarters(ref, value):
    rows = value.shape[0] // 4
    ref[pl.ds(0, 4 * rows), :] = value
    return [ref[pl.ds(j, rows, stride=4), :] for j in range(4)]


def mean4(ref, value):
    parts = quarters(ref, value)
    return ((parts[0] + parts[1]) + (parts[2] + parts[3])) * 0.25


def expand(ref, value):
    rows = value.shape[0]
    for j in range(4):
        ref[pl.ds(j, rows, stride=4), :] = value
    return ref[pl.ds(0, 4 * rows), :]


def expand_levels(ref, value, scales):
    total = value[80:84] * scales[2]
    total = value[64:80] * scales[1] + expand(ref, total)
    total = value[0:64] * scales[0] + expand(ref, total)
    return expand(ref, total)


def lane_index(rows):
    return lax.broadcasted_iota(jnp.int32, (rows, DHEAD), 1)


def wide(column):
    return jnp.broadcast_to(column, (column.shape[0], DHEAD))


def early(refs, lanes):
    l1a, l1b, l2a = refs
    return [l1a[:, lanes], l1b[:, lanes], l2a[:, lanes]]


def late(refs, lanes):
    core1, l2b, core2 = refs
    pieces = [core1[:, lanes], l2b[0:48, lanes], core2[0:48, lanes]]
    return pieces + [l2b[48:96, lanes], core2[48:96, lanes]]


def gathered(refs, lanes):
    return jnp.concatenate(early(refs[0:3], lanes) + late(refs[3:6], lanes), axis=0)


def pool_kernel(
    table_ref, k_ref, v_ref, q_ref,
    own_ref, first_ref, second_ref, third_ref, bias_ref, edge_ref,
    e0_ref, e1_ref, e2_ref, in_ref, sems,
):
    copies = []
    for i, ref in enumerate((k_ref, v_ref, q_ref)):
        for j in range(4):
            rows = pl.ds(64 * j, 64)
            copies.append(pltpu.make_async_copy(ref.at[rows, :], in_ref.at[i, rows, :], sems.at[i, j]))
    for copy in copies:
        copy.start()
    place = lax.axis_index("seq")
    last = lax.axis_size("seq") - 1
    offset = table_ref[0:1, :]
    level = table_ref[1:2, :]
    row = lax.broadcasted_iota(jnp.int32, (OWN, FAR), 0)
    mine = jnp.where(row < 64, 1, jnp.where(row < 80, 2, jnp.where(row < 84, 3, 0)))
    allowed = (jnp.abs((offset ^ place) - place) > 1) & (level == mine)
    bias_ref[...] = jnp.where(allowed, level.astype(jnp.float32) * LN4, NEGATIVE_FILL)
    alone = (place == 0) | (place == last)
    edge_ref[...] = jnp.full((8, BLOCK), jnp.where(alone, NEGATIVE_FILL, 0.0), jnp.float32)
    own_ref[84:96, :] = jnp.zeros((12, 3 * WIDTH), jnp.float32)
    for part in range(3):
        for copy in copies[4 * part : 4 * part + 4]:
            copy.wait()
        for h in range(HEADS):
            dst = cols(h, part * WIDTH)
            value = in_ref[part, :, cols(h)]
            one = mean4(e0_ref.at[(part * HEADS + h) % 2], value)
            two = mean4(e1_ref, one)
            three = mean4(e2_ref, two)
            own_ref[0:64, dst] = one
            own_ref[64:80, dst] = two
            own_ref[80:84, dst] = three
            if part < 2:
                first_ref[:, dst] = one
                second_ref[:, dst] = two
                third_ref[:, dst] = three


def pack_kernel(second_ref, a_ref, b_ref, c_ref, out_ref):
    out_ref[0:16, :] = second_ref[...]
    out_ref[16:20, :] = a_ref[...]
    out_ref[20:24, :] = b_ref[...]
    out_ref[24:28, :] = c_ref[...]


def double_kernel(own_ref, other_ref, out_ref):
    out_ref[0:28, :] = own_ref[...]
    out_ref[28:56, :] = other_ref[...]


def merge_kernel(double_ref, other_ref, out_ref):
    parts = (double_ref[28:56, :], other_ref[0:28, :], other_ref[28:56, :])
    pieces = [(16 * i, part[0:16]) for i, part in enumerate(parts)]
    pieces += [(48 + 12 * i, part[16:28]) for i, part in enumerate((double_ref[0:28, :],) + parts)]
    for start, piece in pieces:
        stop = start + piece.shape[0]
        out_ref[start:stop, :] = piece


def near_state(scores, values, w_ref, peak_ref, mass_ref, sum_ref):
    peak = jnp.maximum(jnp.max(scores, axis=1, keepdims=True), FLOOR)
    weights = jnp.exp(scores - peak)
    w_ref[0] = weights
    peak_ref[...] = wide(peak)
    mass_ref[...] = wide(jnp.sum(weights, axis=1, keepdims=True))
    sum_ref[...] = nn3(weights, values)


def near_inner_kernel(q_ref, ko_ref, ki_ref, vo_ref, vi_ref, *outs):
    keys = jnp.concatenate([ko_ref[...], ki_ref[...]], axis=0)
    values = jnp.concatenate([vo_ref[...], vi_ref[...]], axis=0)
    near_state(nt3(q_ref[...], keys) * INV_ROOT, values, *outs)


def near_outer_kernel(edge_ref, q_ref, k_ref, v_ref, *outs):
    near_state(nt3(q_ref[...], k_ref[...]) * INV_ROOT + edge_ref[0:1, :], v_ref[...], *outs)


def merge(one, two):
    peak = jnp.maximum(one[0], two[0])
    left = jnp.exp(one[0] - peak)
    right = jnp.exp(two[0] - peak)
    return peak, left * one[1] + right * two[1], left * one[2] + right * two[2]


def far_forward_kernel(
    bias_ref, own_ref, a0, a1, a2, a3, a4, a5,
    peak0_ref, mass0_ref, sum0_ref, peak1_ref, mass1_ref, sum1_ref, up_ref, gain_ref,
    att_ref, lse_ref, stat_ref,
    e0_ref, e1_ref, e2_ref, square_ref, cross_ref,
):
    far = (a0, a1, a2, a3, a4, a5)
    bias = bias_ref[...]
    for h in range(HEADS):
        k = cols(h)
        v = cols(h, WIDTH)
        scores = nt3(own_ref[:, cols(h, 2 * WIDTH)], gathered(far, k)) * INV_ROOT + bias
        peak = jnp.maximum(jnp.max(scores, axis=1, keepdims=True), FLOOR)
        weights = jnp.exp(scores - peak)
        mass = jnp.sum(weights, axis=1, keepdims=True)
        levels = (wide(peak), wide(mass), nn3(weights, gathered(far, v)))
        state = tuple(x[80:84] for x in levels)
        for start, stop in (LEVEL_ROWS[1], LEVEL_ROWS[0]):
            state = tuple(expand(ref.at[h % 2], x) for ref, x in zip((e0_ref, e1_ref, e2_ref), state))
            state = merge(state, tuple(x[start:stop] for x in levels))
        state = tuple(expand(ref.at[h % 2], x) for ref, x in zip((e0_ref, e1_ref, e2_ref), state))
        near = merge(
            (peak0_ref[:, k], mass0_ref[:, k], sum0_ref[:, k]), (peak1_ref[:, k], mass1_ref[:, k], sum1_ref[:, k])
        )
        state = merge(state, near)
        attention = state[2] / state[1]
        att_ref[:, k] = attention
        lse_ref[:, k] = state[0] + jnp.log(state[1])
        square = attention * attention
        cross = up_ref[:, k] * gain_ref[0:1, k] * attention
        if h == 0:
            square_ref[...] = square
            cross_ref[...] = cross
        else:
            square_ref[...] += square
            cross_ref[...] += cross
    square = wide(jnp.sum(square_ref[...], axis=1, keepdims=True))
    cross = wide(jnp.sum(cross_ref[...], axis=1, keepdims=True))
    packed = jnp.where(lane_index(BLOCK) == 0, square, cross)
    stat_ref[...] = jnp.transpose(packed)[0:8, :]


def pooled_cotangent(scratch, lows, dots, grads):
    lows, dots, grads = (quarters(ref, x) for ref, x in zip(scratch, (lows, dots, grads)))
    low = jnp.minimum(jnp.minimum(lows[0], lows[1]), jnp.minimum(lows[2], lows[3]))
    scale = [jnp.exp(low - x) for x in lows]
    total = scale[0] * dots[0]
    grad = scale[0] * grads[0]
    for j in range(1, 4):
        total = total + scale[j] * dots[j]
        grad = grad + scale[j] * grads[j]
    return low, total, grad


def cotangent_kernel(
    s0_ref, s1_ref, s2_ref, s3_ref, own_ref, att_ref, lse_ref, up_ref, gain_ref,
    out_ref, dout_ref, delta_ref, first_ref, second_ref, third_ref,
    e0_ref, e1_ref, e2_ref,
):
    total = (s0_ref[...] + s1_ref[...]) + (s2_ref[...] + s3_ref[...])
    square = jnp.transpose(jnp.broadcast_to(total[0:1, :], (DHEAD, BLOCK)))
    cross = jnp.transpose(jnp.broadcast_to(total[1:2, :], (DHEAD, BLOCK)))
    inverse = lax.rsqrt(square / FEAT + EPSILON)
    pull = inverse * inverse * inverse * cross / FEAT
    lane = lane_index(BLOCK)
    packed = jnp.zeros((BLOCK, DHEAD), jnp.float32)
    stats = [jnp.zeros((rows, DHEAD), jnp.float32) for rows in (64, 16, 4)]
    first_ref[:, WIDTH:KV] = own_ref[0:64, KV:]
    second_ref[:, WIDTH:KV] = own_ref[64:80, KV:]
    third_ref[:, WIDTH:KV] = own_ref[80:84, KV:]
    for h in range(HEADS):
        k = cols(h)
        attention = att_ref[:, k]
        out_ref[:, k] = attention * inverse * gain_ref[0:1, k]
        d_out = inverse * (up_ref[:, k] * gain_ref[0:1, k]) - attention * pull
        dout_ref[0:BLOCK, k] = d_out
        delta = wide(jnp.sum(d_out * attention, axis=1, keepdims=True))
        delta_ref[:, k] = delta
        packed = jnp.where(lane == h, lse_ref[:, k], packed)
        packed = jnp.where(lane == HEADS + h, delta, packed)
        level = (lse_ref[:, k], delta, d_out)
        for n, ref in enumerate((first_ref, second_ref, third_ref)):
            level = pooled_cotangent([e.at[h % 2] for e in (e0_ref, e1_ref, e2_ref)], *level)
            rows = level[0].shape[0]
            ref[:, k] = level[2]
            short = lane[0:rows]
            stats[n] = jnp.where(short == h, level[0], jnp.where(short == HEADS + h, level[1], stats[n]))
    first_ref[:, KV:] = stats[0]
    second_ref[:, KV:] = stats[1]
    third_ref[:, KV:] = stats[2]
    dout_ref[BLOCK:, 0:256] = jnp.transpose(packed)[0:8, :]
    dout_ref[BLOCK:, 256:] = jnp.zeros((8, 256), jnp.float32)


def near_query_kernel(
    w0_ref, w1_ref, peak0_ref, peak1_ref, lse_ref, delta_ref, dout_ref,
    k0_ref, k1_ref, k2_ref, v0_ref, v1_ref, v2_ref, dq_ref,
):
    keys = jnp.concatenate([k0_ref[...], k1_ref[...], k2_ref[...]], axis=0)
    values = jnp.concatenate([v0_ref[...], v1_ref[...], v2_ref[...]], axis=0)
    lse = lse_ref[:, 0:1]
    inner = w0_ref[0] * jnp.exp(peak0_ref[:, 0:1] - lse)
    outer = w1_ref[0] * jnp.exp(peak1_ref[:, 0:1] - lse)
    weights = jnp.concatenate([inner, outer], axis=1)
    d_scores = weights * (nt3(dout_ref[...], values) - delta_ref[:, 0:1])
    dq_ref[...] = nn3(d_scores, keys) * INV_ROOT


def far_query_kernel(
    bias_ref, own_ref, a0, a1, a2, a3, a4, a5, first_ref, second_ref, third_ref, near_ref, dq_ref, e0_ref
):
    far = (a0, a1, a2, a3, a4, a5)
    bias = bias_ref[...]

    def grads(lanes):
        fill = jnp.zeros((12, DHEAD), jnp.float32)
        return jnp.concatenate([first_ref[:, lanes], second_ref[:, lanes], third_ref[:, lanes], fill], axis=0)

    stats = grads(slice(KV, GRAD))
    for h in range(HEADS):
        k = cols(h)
        keys = gathered(far, k)
        scores = nt3(own_ref[:, cols(h, 2 * WIDTH)], keys) * INV_ROOT + bias
        weights = jnp.exp(scores - stats[:, h : h + 1])
        d_probs = nt3(grads(k), gathered(far, cols(h, WIDTH)))
        d_scores = weights * (d_probs - stats[:, HEADS + h : HEADS + h + 1])
        grad = nn3(d_scores, keys)
        scales = [INV_ROOT / 4**n for n in (1, 2, 3)]
        dq_ref[:, k] = near_ref[:, k] + expand_levels(e0_ref.at[h % 2], grad, scales)


def near_key_parts(k_ref, v_ref, queries, grads, stats):
    h = pl.program_id(0)
    low = jnp.concatenate([ref[pl.ds(h, 1), :] for ref in stats], axis=1)
    total = jnp.concatenate([ref[pl.ds(h + HEADS, 1), :] for ref in stats], axis=1)
    weights = jnp.exp(nt3(k_ref[...], queries) * INV_ROOT - low)
    d_scores = weights * (nt3(v_ref[...], grads) - total)
    return nn3(d_scores, queries) * INV_ROOT, nn3(weights, grads)


def inner_key_kernel(k_ref, v_ref, q0_ref, q1_ref, d0_ref, d1_ref, t0_ref, t1_ref, dk_ref, dv_ref):
    queries = jnp.concatenate([q0_ref[...], q1_ref[...]], axis=0)
    grads = jnp.concatenate([d0_ref[...], d1_ref[...]], axis=0)
    dk_ref[...], dv_ref[...] = near_key_parts(k_ref, v_ref, queries, grads, (t0_ref, t1_ref))


def outer_key_kernel(k_ref, v_ref, q_ref, d_ref, t_ref, dk_in_ref, dv_in_ref, dk_ref, dv_ref):
    d_keys, d_values = near_key_parts(k_ref, v_ref, q_ref[...], d_ref[...], (t_ref,))
    dk_ref[...] = dk_in_ref[...] + d_keys
    dv_ref[...] = dv_in_ref[...] + d_values


def far_key_parts(own_ref, bias, pieces, h):
    def take(lanes):
        return jnp.concatenate(pieces(lanes), axis=0)

    stats = take(slice(KV, GRAD))
    fill = jnp.zeros((-stats.shape[0] % DHEAD, DHEAD), jnp.float32)
    stats = jnp.transpose(jnp.concatenate([stats, fill], axis=0))[0:8, 0 : stats.shape[0]]
    queries = take(cols(h, WIDTH))
    grads = take(cols(h))
    scores = nt3(own_ref[:, cols(h)], queries) * INV_ROOT + bias
    weights = jnp.exp(scores - stats[h : h + 1, :])
    d_scores = weights * (nt3(own_ref[:, cols(h, WIDTH)], grads) - stats[HEADS + h : HEADS + h + 1, :])
    return nn3(d_scores, queries) * INV_ROOT, nn3(weights, grads)


def early_key_kernel(bias_ref, own_ref, a0, a1, a2, dk_ref, dv_ref):
    bias = bias_ref[:, 0:EARLY]
    for h in range(HEADS):
        k = cols(h)
        dk_ref[:, k], dv_ref[:, k] = far_key_parts(own_ref, bias, lambda lanes: early((a0, a1, a2), lanes), h)


def late_key_kernel(
    bias_ref, own_ref, a0, a1, a2, far_dk_ref, far_dv_ref, dk_in_ref, dv_in_ref, dk_ref, dv_ref, e0_ref, e1_ref
):
    bias = bias_ref[:, EARLY:FAR]
    scales = [1.0 / 4**n for n in (1, 2, 3)]
    for h in range(HEADS):
        k = cols(h)
        d_keys, d_values = far_key_parts(own_ref, bias, lambda lanes: late((a0, a1, a2), lanes), h)
        d_keys = far_dk_ref[:, k] + d_keys
        d_values = far_dv_ref[:, k] + d_values
        dk_ref[:, k] = dk_in_ref[:, k] + expand_levels(e0_ref.at[h % 2], d_keys, scales)
        dv_ref[:, k] = dv_in_ref[:, k] + expand_levels(e1_ref.at[h % 2], d_values, scales)


def f32(*shape):
    return jax.ShapeDtypeStruct(shape, jnp.float32)


def params():
    return pltpu.CompilerParams(vmem_limit_bytes=VMEM_BYTES)


def cost(flops, size):
    return pl.CostEstimate(flops=int(flops), bytes_accessed=int(size), transcendentals=0)


def whole_call(kernel, outs, scratch, flops, size, *operands):
    spec = pl.BlockSpec(memory_space=pltpu.VMEM)
    return pl.pallas_call(
        kernel,
        out_shape=outs,
        in_specs=[spec] * len(operands),
        out_specs=[spec] * len(outs),
        scratch_shapes=[pltpu.VMEM(shape, jnp.float32) for shape in scratch],
        compiler_params=params(),
        cost_estimate=cost(flops, size),
    )(*operands)


BLOCK_FLOPS = 2.0 * BLOCK * BLOCK * DHEAD * HEADS * 6


def column():
    return pl.BlockSpec((BLOCK, DHEAD), lambda h: (0, h))


def slab(blocks):
    return pl.BlockSpec((1, BLOCK, blocks * BLOCK), lambda h: (h, 0, 0))


def head_call(kernel, outs, out_specs, in_specs, blocks, *operands):
    return pl.pallas_call(
        kernel,
        grid=(HEADS,),
        out_shape=outs,
        in_specs=in_specs,
        out_specs=out_specs,
        compiler_params=params(),
        cost_estimate=cost(blocks * BLOCK_FLOPS, 4e6),
    )(*operands)


def near_inner(query, keys, values):
    k = column()
    outs = [f32(HEADS, BLOCK, 2 * BLOCK)] + [f32(BLOCK, WIDTH)] * 3
    return head_call(near_inner_kernel, outs, [slab(2), k, k, k], [k] * 5, 4, query, *keys, *values)


def near_outer(edge, query, keys, values):
    k = column()
    outs = [f32(HEADS, BLOCK, BLOCK)] + [f32(BLOCK, WIDTH)] * 3
    edge_spec = pl.BlockSpec((8, BLOCK), lambda h: (0, 0))
    return head_call(near_outer_kernel, outs, [slab(1), k, k, k], [edge_spec, k, k, k], 2, edge, query, keys, values)


def near_query(w0, w1, peak0, peak1, lse, delta, d_out, keys, values):
    k = column()
    specs = [slab(2), slab(1)] + [k] * 11
    return head_call(
        near_query_kernel, f32(BLOCK, WIDTH), k, specs, 6, w0, w1, peak0, peak1, lse, delta, d_out, *keys, *values
    )


def stat_rows():
    return pl.BlockSpec((8, 256), lambda h: (BLOCK // 8, 0))


def inner_key(key, value, query, query_in, d_out, d_in):
    k, t = column(), stat_rows()
    return head_call(
        inner_key_kernel, [f32(BLOCK, WIDTH)] * 2, [k, k], [k] * 6 + [t, t], 8,
        key, value, query, query_in, d_out, d_in, d_out, d_in,
    )


def outer_key(key, value, query_out, d_far, dk, dv):
    k, t = column(), stat_rows()
    return head_call(
        outer_key_kernel, [f32(BLOCK, WIDTH)] * 2, [k, k], [k] * 4 + [t, k, k], 4,
        key, value, query_out, d_far, d_far, dk, dv,
    )


def pool(key, value, query):
    vmem = pl.BlockSpec(memory_space=pltpu.VMEM)
    hbm = pl.BlockSpec(memory_space=pltpu.HBM)
    return pl.pallas_call(
        pool_kernel,
        out_shape=[
            f32(OWN, 3 * WIDTH), f32(64, KV), f32(16, KV), f32(4, KV), f32(OWN, FAR), f32(8, BLOCK),
        ],
        in_specs=[vmem] + [hbm] * 3,
        out_specs=[vmem] * 6,
        scratch_shapes=[
            pltpu.VMEM((2, BLOCK, DHEAD), jnp.float32),
            pltpu.VMEM((64, DHEAD), jnp.float32),
            pltpu.VMEM((16, DHEAD), jnp.float32),
            pltpu.VMEM((3, BLOCK, WIDTH), jnp.float32),
            pltpu.SemaphoreType.DMA((3, 4)),
        ],
        compiler_params=pltpu.CompilerParams(vmem_limit_bytes=POOL_VMEM_BYTES),
        cost_estimate=cost(1e6, 2e6),
    )(jnp.asarray(slot_table()), key, value, query)


def far_forward(bias, own, far, inner, outer, upstream, gain):
    return whole_call(
        far_forward_kernel,
        [f32(BLOCK, WIDTH), f32(BLOCK, WIDTH), f32(8, 256)],
        [(2, BLOCK, DHEAD)] * 3 + [(BLOCK, DHEAD)] * 2,
        BLOCK_FLOPS,
        8e6,
        bias, own, *far, *inner, *outer, upstream, gain,
    )


def cotangent(stats, others, own, attention, lse, upstream, gain):
    return whole_call(
        cotangent_kernel,
        [f32(BLOCK, WIDTH), f32(BLOCK + 8, WIDTH), f32(BLOCK, WIDTH), f32(64, GRAD), f32(16, GRAD), f32(4, GRAD)],
        [(2, BLOCK, DHEAD)] * 3,
        1e6,
        4e6,
        stats, *others, own, attention, lse, upstream, gain,
    )


def far_query(bias, own, far, first, second, third, near):
    (grad,) = whole_call(
        far_query_kernel,
        [f32(BLOCK, WIDTH)],
        [(2, BLOCK, DHEAD)],
        BLOCK_FLOPS,
        6e6,
        bias, own, *far, first, second, third, near,
    )
    return grad


def early_key(bias, own, grads):
    return whole_call(early_key_kernel, [f32(OWN, WIDTH)] * 2, [], BLOCK_FLOPS, 3e6, bias, own, *grads)


def late_key(bias, own, grads, far_dk, far_dv, near_dk, near_dv):
    return whole_call(
        late_key_kernel,
        [f32(BLOCK, WIDTH)] * 2,
        [(2, BLOCK, DHEAD)] * 2,
        BLOCK_FLOPS,
        3e6,
        bias, own, *grads, far_dk, far_dv, near_dk, near_dv,
    )


def body(query, key, value, norm_gain, upstream):
    count = lax.axis_size("seq")
    head_count = lax.axis_size("head")

    def exchange(array, mask):
        return lax.ppermute(array, "seq", [(i, i ^ mask) for i in range(count)])

    def exchange_outer(array):
        pairs = [(i, i + 1 if i % 2 else i - 1) for i in range(1, count - 1)]
        return lax.ppermute(array, "seq", pairs)

    def after(array, *tokens):
        return lax.optimization_barrier((array,) + tokens)[0]

    def packed(second, thirds):
        return whole_call(pack_kernel, [f32(28, second.shape[1])], [], 1e4, 1e5, second, *thirds)[0]

    def doubled(pack, other):
        return whole_call(double_kernel, [f32(56, pack.shape[1])], [], 1e4, 1e5, pack, other)[0]

    def merged(double, other):
        return whole_call(merge_kernel, [f32(96, double.shape[1])], [], 1e4, 1e5, double, other)[0]

    gain = norm_gain.reshape(1, WIDTH)
    out_k, out_v = exchange_outer(key), exchange_outer(value)
    in_k, in_v = exchange(key, 1), exchange(value, 1)
    own, first, second, third, bias, edge = pool(key, value, query)

    held = after(third, in_k, in_v)
    planes = [exchange(after(held, out_k), PLANES[0])] + [exchange(held, mask) for mask in PLANES[1:]]
    l1a = exchange(first, 2)
    pack = packed(after(second, out_k), planes)
    double = doubled(after(pack, l1a), exchange(pack, 4))
    other = exchange(double, 12)
    w0, *inner = near_inner(query, (key, after(in_k, double)), (value, in_v))
    w1, *outer = near_outer(edge, query, after(out_k, double), out_v)
    l1b = exchange(after(l1a, double), 1)
    l2a = merged(after(double, w0, w1, l1b), other)
    l2b = exchange(l2a, 2)
    core1 = exchange(l2a, 1)
    core2 = exchange(after(l2b, core1), 1)
    query_in = exchange(after(query, l2a), 1)
    query_out = exchange_outer(after(query, l2a))
    far = (l1a, l1b, l2a, core1, l2b, core2)
    attention, lse, stats = far_forward(bias, own, far, inner, outer, upstream, gain)

    others = [
        lax.ppermute(stats, "head", [(i, i ^ mask) for i in range(head_count)]) for mask in range(1, head_count)
    ]
    attention = after(attention, query_in, query_out)
    attended, d_out, delta, g1, g2, g3 = cotangent(stats, others, own, attention, lse, upstream, gain)

    planes = [exchange(g3, mask) for mask in PLANES]
    l1a = exchange(g1, 2)
    d_in = exchange(d_out, 1)
    pack = packed(g2, planes)
    quad = exchange(pack, 4)
    near_dq = near_query(
        w0, w1, inner[0], outer[0], lse, delta, after(d_out, pack), (key, in_k, out_k), (value, in_v, out_v)
    )
    double = doubled(after(pack, near_dq, l1a), quad)
    other = exchange(double, 12)
    d_far = exchange_outer(after(d_out, double))
    near_dk, near_dv = inner_key(key, value, query, query_in, d_out, after(d_in, double))
    query_grad = far_query(bias, own, far, after(g1, double), g2, g3, near_dq)
    l1b = exchange(after(l1a, double), 1)
    l2a = merged(after(double, near_dk, query_grad, d_far, l1b), other)
    l2b = exchange(l2a, 2)
    core1 = exchange(l2a, 1)
    near_dk, near_dv = outer_key(key, value, query_out, after(d_far, l2a), near_dk, near_dv)
    far_dk, far_dv = early_key(bias, own, (l1a, l1b, after(l2a, near_dk)))
    core2 = exchange(after(l2b, far_dk), 1)
    key_grad, value_grad = late_key(bias, own, (core1, l2b, core2), far_dk, far_dv, near_dk, near_dv)
    return attended, query_grad, key_grad, value_grad


def solution(mesh):
    return jax.shard_map(
        body,
        mesh=mesh,
        in_specs=(
            P("seq", "head"),
            P("seq", "head"),
            P("seq", "head"),
            P("head"),
            P("seq", "head"),
        ),
        out_specs=(P("seq", "head"), P("seq", "head"), P("seq", "head"), P("seq", "head")),
        check_vma=False,
    )
```

```python
import math

import jax
import jax.numpy as jnp
import numpy as np
from jax import lax
from jax.experimental import pallas as pl
from jax.experimental.pallas import tpu as pltpu
from jax.sharding import PartitionSpec as P

DHEAD = 128
BLOCK = 256
FEAT = 2048
HEADS = 4
WIDTH = HEADS * DHEAD
NEGATIVE_FILL = -1e30
FLOOR = -1e25
EPSILON = 1e-06
INV_ROOT = 1.0 / math.sqrt(DHEAD)
LN4 = math.log(4.0)
VMEM_BYTES = 24 * 1024 * 1024
POOL_VMEM_BYTES = 56 * 1024 * 1024

OWN = 96
LEVEL_ROWS = ((0, 64), (64, 80), (80, 84))
FAR = 512
KV = 2 * WIDTH
GRAD = 2 * WIDTH + DHEAD

QUAD = (4, 12, 8)
PLANES = (16, 32, 48)
THIRD_BLOCKS = tuple(y ^ o for o in (0,) + QUAD for y in PLANES)


def flipped(blocks, mask):
    return tuple(o ^ mask for o in blocks)


SLOTS = (
    (1, (2, 3)),
    (2, QUAD),
    (3, THIRD_BLOCKS),
    (2, flipped(QUAD, 1)),
    (3, flipped(THIRD_BLOCKS, 1)),
    (2, flipped(QUAD, 2)),
    (2, flipped(QUAD, 3)),
    (3, flipped(THIRD_BLOCKS, 2)),
    (3, flipped(THIRD_BLOCKS, 3)),
)
EARLY = 224


def slot_table():
    rows = {1: 64, 2: 16, 3: 4}
    offset = np.concatenate([np.repeat(np.array(blocks, np.int32), rows[n]) for n, blocks in SLOTS])
    level = np.concatenate([np.full(len(blocks) * rows[n], n, np.int32) for n, blocks in SLOTS])
    table = np.zeros((8, FAR), np.int32)
    table[0], table[1] = offset, level
    return table


def split3(x):
    high = x.astype(jnp.bfloat16)
    rest = x - high.astype(jnp.float32)
    middle = rest.astype(jnp.bfloat16)
    return high, middle, (rest - middle.astype(jnp.float32)).astype(jnp.bfloat16)


def dot(a, b, dims):
    return lax.dot_general(a, b, (dims, ((), ())), preferred_element_type=jnp.float32)


def nt3(a, b):
    a1, a2, a3 = split3(a)
    b1, b2, b3 = split3(b)
    left = jnp.concatenate([a1, a2, a1, a2, a1, a3], axis=1)
    right = jnp.concatenate([b1, b1, b2, b2, b3, b1], axis=1)
    return dot(left, right, ((1,), (1,)))


def nn3(a, b):
    a1, a2, a3 = split3(a)
    b1, b2, b3 = split3(b)
    right = jnp.concatenate([b1, b2], axis=1)
    main = dot(jnp.concatenate([a1, a2], axis=1), jnp.concatenate([right, right], axis=0), ((1,), (0,)))
    small = dot(jnp.concatenate([a1, a3], axis=1), jnp.concatenate([b3, b1], axis=0), ((1,), (0,)))
    return main[:, :DHEAD] + (main[:, DHEAD:] + small)


def cols(h, base=0):
    return slice(base + h * DHEAD, base + (h + 1) * DHEAD)


def quarters(ref, value):
    rows = value.shape[0] // 4
    ref[pl.ds(0, 4 * rows), :] = value
    return [ref[pl.ds(j, rows, stride=4), :] for j in range(4)]


def mean4(ref, value):
    parts = quarters(ref, value)
    return ((parts[0] + parts[1]) + (parts[2] + parts[3])) * 0.25


def expand(ref, value):
    rows = value.shape[0]
    for j in range(4):
        ref[pl.ds(j, rows, stride=4), :] = value
    return ref[pl.ds(0, 4 * rows), :]


def expand_levels(ref, value, scales):
    total = value[80:84] * scales[2]
    total = value[64:80] * scales[1] + expand(ref, total)
    total = value[0:64] * scales[0] + expand(ref, total)
    return expand(ref, total)


def lane_index(rows):
    return lax.broadcasted_iota(jnp.int32, (rows, DHEAD), 1)


def wide(column):
    return jnp.broadcast_to(column, (column.shape[0], DHEAD))


def early(refs, lanes):
    l1a, l1b, l2a = refs
    return [l1a[:, lanes], l1b[:, lanes], l2a[:, lanes]]


def late(refs, lanes):
    core1, l2b, core2 = refs
    pieces = [core1[:, lanes], l2b[0:48, lanes], core2[0:48, lanes]]
    return pieces + [l2b[48:96, lanes], core2[48:96, lanes]]


def gathered(refs, lanes):
    return jnp.concatenate(early(refs[0:3], lanes) + late(refs[3:6], lanes), axis=0)


def pool_kernel(
    table_ref, k_ref, v_ref, q_ref,
    own_ref, first_ref, second_ref, third_ref, bias_ref, edge_ref,
    e0_ref, e1_ref, e2_ref, in_ref, sems,
):
    copies = []
    for i, ref in enumerate((k_ref, v_ref, q_ref)):
        for j in range(4):
            rows = pl.ds(64 * j, 64)
            copies.append(pltpu.make_async_copy(ref.at[rows, :], in_ref.at[i, rows, :], sems.at[i, j]))
    for copy in copies:
        copy.start()
    place = lax.axis_index("seq")
    last = lax.axis_size("seq") - 1
    offset = table_ref[0:1, :]
    level = table_ref[1:2, :]
    row = lax.broadcasted_iota(jnp.int32, (OWN, FAR), 0)
    mine = jnp.where(row < 64, 1, jnp.where(row < 80, 2, jnp.where(row < 84, 3, 0)))
    allowed = (jnp.abs((offset ^ place) - place) > 1) & (level == mine)
    bias_ref[...] = jnp.where(allowed, level.astype(jnp.float32) * LN4, NEGATIVE_FILL)
    alone = (place == 0) | (place == last)
    edge_ref[...] = jnp.full((8, BLOCK), jnp.where(alone, NEGATIVE_FILL, 0.0), jnp.float32)
    own_ref[84:96, :] = jnp.zeros((12, 3 * WIDTH), jnp.float32)
    for part in range(3):
        for copy in copies[4 * part : 4 * part + 4]:
            copy.wait()
        for h in range(HEADS):
            dst = cols(h, part * WIDTH)
            value = in_ref[part, :, cols(h)]
            one = mean4(e0_ref.at[(part * HEADS + h) % 2], value)
            two = mean4(e1_ref, one)
            three = mean4(e2_ref, two)
            own_ref[0:64, dst] = one
            own_ref[64:80, dst] = two
            own_ref[80:84, dst] = three
            if part < 2:
                first_ref[:, dst] = one
                second_ref[:, dst] = two
                third_ref[:, dst] = three


def pack_kernel(second_ref, a_ref, b_ref, c_ref, out_ref):
    out_ref[0:16, :] = second_ref[...]
    out_ref[16:20, :] = a_ref[...]
    out_ref[20:24, :] = b_ref[...]
    out_ref[24:28, :] = c_ref[...]


def double_kernel(own_ref, other_ref, out_ref):
    out_ref[0:28, :] = own_ref[...]
    out_ref[28:56, :] = other_ref[...]


def merge_kernel(double_ref, other_ref, out_ref):
    parts = (double_ref[28:56, :], other_ref[0:28, :], other_ref[28:56, :])
    pieces = [(16 * i, part[0:16]) for i, part in enumerate(parts)]
    pieces += [(48 + 12 * i, part[16:28]) for i, part in enumerate((double_ref[0:28, :],) + parts)]
    for start, piece in pieces:
        stop = start + piece.shape[0]
        out_ref[start:stop, :] = piece


def near_state(scores, values, w_ref, peak_ref, mass_ref, sum_ref):
    peak = jnp.maximum(jnp.max(scores, axis=1, keepdims=True), FLOOR)
    weights = jnp.exp(scores - peak)
    w_ref[0] = weights
    peak_ref[...] = wide(peak)
    mass_ref[...] = wide(jnp.sum(weights, axis=1, keepdims=True))
    sum_ref[...] = nn3(weights, values)


def near_inner_kernel(q_ref, ko_ref, ki_ref, vo_ref, vi_ref, *outs):
    keys = jnp.concatenate([ko_ref[...], ki_ref[...]], axis=0)
    values = jnp.concatenate([vo_ref[...], vi_ref[...]], axis=0)
    near_state(nt3(q_ref[...], keys) * INV_ROOT, values, *outs)


def near_outer_kernel(edge_ref, q_ref, k_ref, v_ref, *outs):
    near_state(nt3(q_ref[...], k_ref[...]) * INV_ROOT + edge_ref[0:1, :], v_ref[...], *outs)


def merge(one, two):
    peak = jnp.maximum(one[0], two[0])
    left = jnp.exp(one[0] - peak)
    right = jnp.exp(two[0] - peak)
    return peak, left * one[1] + right * two[1], left * one[2] + right * two[2]


def far_forward_kernel(
    bias_ref, own_ref, a0, a1, a2, a3, a4, a5,
    peak0_ref, mass0_ref, sum0_ref, peak1_ref, mass1_ref, sum1_ref, up_ref, gain_ref,
    att_ref, lse_ref, stat_ref,
    e0_ref, e1_ref, e2_ref, square_ref, cross_ref,
):
    far = (a0, a1, a2, a3, a4, a5)
    bias = bias_ref[...]
    for h in range(HEADS):
        k = cols(h)
        v = cols(h, WIDTH)
        scores = nt3(own_ref[:, cols(h, 2 * WIDTH)], gathered(far, k)) * INV_ROOT + bias
        peak = jnp.maximum(jnp.max(scores, axis=1, keepdims=True), FLOOR)
        weights = jnp.exp(scores - peak)
        mass = jnp.sum(weights, axis=1, keepdims=True)
        levels = (wide(peak), wide(mass), nn3(weights, gathered(far, v)))
        state = tuple(x[80:84] for x in levels)
        for start, stop in (LEVEL_ROWS[1], LEVEL_ROWS[0]):
            state = tuple(expand(ref.at[h % 2], x) for ref, x in zip((e0_ref, e1_ref, e2_ref), state))
            state = merge(state, tuple(x[start:stop] for x in levels))
        state = tuple(expand(ref.at[h % 2], x) for ref, x in zip((e0_ref, e1_ref, e2_ref), state))
        near = merge(
            (peak0_ref[:, k], mass0_ref[:, k], sum0_ref[:, k]), (peak1_ref[:, k], mass1_ref[:, k], sum1_ref[:, k])
        )
        state = merge(state, near)
        attention = state[2] / state[1]
        att_ref[:, k] = attention
        lse_ref[:, k] = state[0] + jnp.log(state[1])
        square = attention * attention
        cross = up_ref[:, k] * gain_ref[0:1, k] * attention
        if h == 0:
            square_ref[...] = square
            cross_ref[...] = cross
        else:
            square_ref[...] += square
            cross_ref[...] += cross
    square = wide(jnp.sum(square_ref[...], axis=1, keepdims=True))
    cross = wide(jnp.sum(cross_ref[...], axis=1, keepdims=True))
    packed = jnp.where(lane_index(BLOCK) == 0, square, cross)
    stat_ref[...] = jnp.transpose(packed)[0:8, :]


def pooled_cotangent(scratch, lows, dots, grads):
    lows, dots, grads = (quarters(ref, x) for ref, x in zip(scratch, (lows, dots, grads)))
    low = jnp.minimum(jnp.minimum(lows[0], lows[1]), jnp.minimum(lows[2], lows[3]))
    scale = [jnp.exp(low - x) for x in lows]
    total = scale[0] * dots[0]
    grad = scale[0] * grads[0]
    for j in range(1, 4):
        total = total + scale[j] * dots[j]
        grad = grad + scale[j] * grads[j]
    return low, total, grad


def cotangent_kernel(
    s0_ref, s1_ref, s2_ref, s3_ref, own_ref, att_ref, lse_ref, up_ref, gain_ref,
    out_ref, dout_ref, delta_ref, first_ref, second_ref, third_ref,
    e0_ref, e1_ref, e2_ref,
):
    total = (s0_ref[...] + s1_ref[...]) + (s2_ref[...] + s3_ref[...])
    square = jnp.transpose(jnp.broadcast_to(total[0:1, :], (DHEAD, BLOCK)))
    cross = jnp.transpose(jnp.broadcast_to(total[1:2, :], (DHEAD, BLOCK)))
    inverse = lax.rsqrt(square / FEAT + EPSILON)
    pull = inverse * inverse * inverse * cross / FEAT
    lane = lane_index(BLOCK)
    packed = jnp.zeros((BLOCK, DHEAD), jnp.float32)
    stats = [jnp.zeros((rows, DHEAD), jnp.float32) for rows in (64, 16, 4)]
    first_ref[:, WIDTH:KV] = own_ref[0:64, KV:]
    second_ref[:, WIDTH:KV] = own_ref[64:80, KV:]
    third_ref[:, WIDTH:KV] = own_ref[80:84, KV:]
    for h in range(HEADS):
        k = cols(h)
        attention = att_ref[:, k]
        out_ref[:, k] = attention * inverse * gain_ref[0:1, k]
        d_out = inverse * (up_ref[:, k] * gain_ref[0:1, k]) - attention * pull
        dout_ref[0:BLOCK, k] = d_out
        delta = wide(jnp.sum(d_out * attention, axis=1, keepdims=True))
        delta_ref[:, k] = delta
        packed = jnp.where(lane == h, lse_ref[:, k], packed)
        packed = jnp.where(lane == HEADS + h, delta, packed)
        level = (lse_ref[:, k], delta, d_out)
        for n, ref in enumerate((first_ref, second_ref, third_ref)):
            level = pooled_cotangent([e.at[h % 2] for e in (e0_ref, e1_ref, e2_ref)], *level)
            rows = level[0].shape[0]
            ref[:, k] = level[2]
            short = lane[0:rows]
            stats[n] = jnp.where(short == h, level[0], jnp.where(short == HEADS + h, level[1], stats[n]))
    first_ref[:, KV:] = stats[0]
    second_ref[:, KV:] = stats[1]
    third_ref[:, KV:] = stats[2]
    dout_ref[BLOCK:, 0:256] = jnp.transpose(packed)[0:8, :]
    dout_ref[BLOCK:, 256:] = jnp.zeros((8, 256), jnp.float32)


def near_query_kernel(
    w0_ref, w1_ref, peak0_ref, peak1_ref, lse_ref, delta_ref, dout_ref,
    k0_ref, k1_ref, k2_ref, v0_ref, v1_ref, v2_ref, dq_ref,
):
    keys = jnp.concatenate([k0_ref[...], k1_ref[...], k2_ref[...]], axis=0)
    values = jnp.concatenate([v0_ref[...], v1_ref[...], v2_ref[...]], axis=0)
    lse = lse_ref[:, 0:1]
    inner = w0_ref[0] * jnp.exp(peak0_ref[:, 0:1] - lse)
    outer = w1_ref[0] * jnp.exp(peak1_ref[:, 0:1] - lse)
    weights = jnp.concatenate([inner, outer], axis=1)
    d_scores = weights * (nt3(dout_ref[...], values) - delta_ref[:, 0:1])
    dq_ref[...] = nn3(d_scores, keys) * INV_ROOT


def far_query_kernel(
    bias_ref, own_ref, a0, a1, a2, a3, a4, a5, first_ref, second_ref, third_ref, near_ref, dq_ref, e0_ref
):
    far = (a0, a1, a2, a3, a4, a5)
    bias = bias_ref[...]

    def grads(lanes):
        fill = jnp.zeros((12, DHEAD), jnp.float32)
        return jnp.concatenate([first_ref[:, lanes], second_ref[:, lanes], third_ref[:, lanes], fill], axis=0)

    stats = grads(slice(KV, GRAD))
    for h in range(HEADS):
        k = cols(h)
        keys = gathered(far, k)
        scores = nt3(own_ref[:, cols(h, 2 * WIDTH)], keys) * INV_ROOT + bias
        weights = jnp.exp(scores - stats[:, h : h + 1])
        d_probs = nt3(grads(k), gathered(far, cols(h, WIDTH)))
        d_scores = weights * (d_probs - stats[:, HEADS + h : HEADS + h + 1])
        grad = nn3(d_scores, keys)
        scales = [INV_ROOT / 4**n for n in (1, 2, 3)]
        dq_ref[:, k] = near_ref[:, k] + expand_levels(e0_ref.at[h % 2], grad, scales)


def near_key_parts(k_ref, v_ref, queries, grads, stats):
    h = pl.program_id(0)
    low = jnp.concatenate([ref[pl.ds(h, 1), :] for ref in stats], axis=1)
    total = jnp.concatenate([ref[pl.ds(h + HEADS, 1), :] for ref in stats], axis=1)
    weights = jnp.exp(nt3(k_ref[...], queries) * INV_ROOT - low)
    d_scores = weights * (nt3(v_ref[...], grads) - total)
    return nn3(d_scores, queries) * INV_ROOT, nn3(weights, grads)


def inner_key_kernel(k_ref, v_ref, q0_ref, q1_ref, d0_ref, d1_ref, t0_ref, t1_ref, dk_ref, dv_ref):
    queries = jnp.concatenate([q0_ref[...], q1_ref[...]], axis=0)
    grads = jnp.concatenate([d0_ref[...], d1_ref[...]], axis=0)
    dk_ref[...], dv_ref[...] = near_key_parts(k_ref, v_ref, queries, grads, (t0_ref, t1_ref))


def outer_key_kernel(k_ref, v_ref, q_ref, d_ref, t_ref, dk_in_ref, dv_in_ref, dk_ref, dv_ref):
    d_keys, d_values = near_key_parts(k_ref, v_ref, q_ref[...], d_ref[...], (t_ref,))
    dk_ref[...] = dk_in_ref[...] + d_keys
    dv_ref[...] = dv_in_ref[...] + d_values


def far_key_parts(own_ref, bias, pieces, h):
    def take(lanes):
        return jnp.concatenate(pieces(lanes), axis=0)

    stats = take(slice(KV, GRAD))
    fill = jnp.zeros((-stats.shape[0] % DHEAD, DHEAD), jnp.float32)
    stats = jnp.transpose(jnp.concatenate([stats, fill], axis=0))[0:8, 0 : stats.shape[0]]
    queries = take(cols(h, WIDTH))
    grads = take(cols(h))
    scores = nt3(own_ref[:, cols(h)], queries) * INV_ROOT + bias
    weights = jnp.exp(scores - stats[h : h + 1, :])
    d_scores = weights * (nt3(own_ref[:, cols(h, WIDTH)], grads) - stats[HEADS + h : HEADS + h + 1, :])
    return nn3(d_scores, queries) * INV_ROOT, nn3(weights, grads)


def early_key_kernel(bias_ref, own_ref, a0, a1, a2, dk_ref, dv_ref):
    bias = bias_ref[:, 0:EARLY]
    for h in range(HEADS):
        k = cols(h)
        dk_ref[:, k], dv_ref[:, k] = far_key_parts(own_ref, bias, lambda lanes: early((a0, a1, a2), lanes), h)


def late_key_kernel(
    bias_ref, own_ref, a0, a1, a2, far_dk_ref, far_dv_ref, dk_in_ref, dv_in_ref, dk_ref, dv_ref, e0_ref, e1_ref
):
    bias = bias_ref[:, EARLY:FAR]
    scales = [1.0 / 4**n for n in (1, 2, 3)]
    for h in range(HEADS):
        k = cols(h)
        d_keys, d_values = far_key_parts(own_ref, bias, lambda lanes: late((a0, a1, a2), lanes), h)
        d_keys = far_dk_ref[:, k] + d_keys
        d_values = far_dv_ref[:, k] + d_values
        dk_ref[:, k] = dk_in_ref[:, k] + expand_levels(e0_ref.at[h % 2], d_keys, scales)
        dv_ref[:, k] = dv_in_ref[:, k] + expand_levels(e1_ref.at[h % 2], d_values, scales)


def f32(*shape):
    return jax.ShapeDtypeStruct(shape, jnp.float32)


def params():
    return pltpu.CompilerParams(vmem_limit_bytes=VMEM_BYTES)


def cost(flops, size):
    return pl.CostEstimate(flops=int(flops), bytes_accessed=int(size), transcendentals=0)


def whole_call(kernel, outs, scratch, flops, size, *operands):
    spec = pl.BlockSpec(memory_space=pltpu.VMEM)
    return pl.pallas_call(
        kernel,
        out_shape=outs,
        in_specs=[spec] * len(operands),
        out_specs=[spec] * len(outs),
        scratch_shapes=[pltpu.VMEM(shape, jnp.float32) for shape in scratch],
        compiler_params=params(),
        cost_estimate=cost(flops, size),
    )(*operands)


BLOCK_FLOPS = 2.0 * BLOCK * BLOCK * DHEAD * HEADS * 6


def column():
    return pl.BlockSpec((BLOCK, DHEAD), lambda h: (0, h))


def slab(blocks):
    return pl.BlockSpec((1, BLOCK, blocks * BLOCK), lambda h: (h, 0, 0))


def head_call(kernel, outs, out_specs, in_specs, blocks, *operands):
    return pl.pallas_call(
        kernel,
        grid=(HEADS,),
        out_shape=outs,
        in_specs=in_specs,
        out_specs=out_specs,
        compiler_params=params(),
        cost_estimate=cost(blocks * BLOCK_FLOPS, 4e6),
    )(*operands)


def near_inner(query, keys, values):
    k = column()
    outs = [f32(HEADS, BLOCK, 2 * BLOCK)] + [f32(BLOCK, WIDTH)] * 3
    return head_call(near_inner_kernel, outs, [slab(2), k, k, k], [k] * 5, 4, query, *keys, *values)


def near_outer(edge, query, keys, values):
    k = column()
    outs = [f32(HEADS, BLOCK, BLOCK)] + [f32(BLOCK, WIDTH)] * 3
    edge_spec = pl.BlockSpec((8, BLOCK), lambda h: (0, 0))
    return head_call(near_outer_kernel, outs, [slab(1), k, k, k], [edge_spec, k, k, k], 2, edge, query, keys, values)


def near_query(w0, w1, peak0, peak1, lse, delta, d_out, keys, values):
    k = column()
    specs = [slab(2), slab(1)] + [k] * 11
    return head_call(
        near_query_kernel, f32(BLOCK, WIDTH), k, specs, 6, w0, w1, peak0, peak1, lse, delta, d_out, *keys, *values
    )


def stat_rows():
    return pl.BlockSpec((8, 256), lambda h: (BLOCK // 8, 0))


def inner_key(key, value, query, query_in, d_out, d_in):
    k, t = column(), stat_rows()
    return head_call(
        inner_key_kernel, [f32(BLOCK, WIDTH)] * 2, [k, k], [k] * 6 + [t, t], 8,
        key, value, query, query_in, d_out, d_in, d_out, d_in,
    )


def outer_key(key, value, query_out, d_far, dk, dv):
    k, t = column(), stat_rows()
    return head_call(
        outer_key_kernel, [f32(BLOCK, WIDTH)] * 2, [k, k], [k] * 4 + [t, k, k], 4,
        key, value, query_out, d_far, d_far, dk, dv,
    )


def pool(key, value, query):
    vmem = pl.BlockSpec(memory_space=pltpu.VMEM)
    hbm = pl.BlockSpec(memory_space=pltpu.HBM)
    return pl.pallas_call(
        pool_kernel,
        out_shape=[
            f32(OWN, 3 * WIDTH), f32(64, KV), f32(16, KV), f32(4, KV), f32(OWN, FAR), f32(8, BLOCK),
        ],
        in_specs=[vmem] + [hbm] * 3,
        out_specs=[vmem] * 6,
        scratch_shapes=[
            pltpu.VMEM((2, BLOCK, DHEAD), jnp.float32),
            pltpu.VMEM((64, DHEAD), jnp.float32),
            pltpu.VMEM((16, DHEAD), jnp.float32),
            pltpu.VMEM((3, BLOCK, WIDTH), jnp.float32),
            pltpu.SemaphoreType.DMA((3, 4)),
        ],
        compiler_params=pltpu.CompilerParams(vmem_limit_bytes=POOL_VMEM_BYTES),
        cost_estimate=cost(1e6, 2e6),
    )(jnp.asarray(slot_table()), key, value, query)


def far_forward(bias, own, far, inner, outer, upstream, gain):
    return whole_call(
        far_forward_kernel,
        [f32(BLOCK, WIDTH), f32(BLOCK, WIDTH), f32(8, 256)],
        [(2, BLOCK, DHEAD)] * 3 + [(BLOCK, DHEAD)] * 2,
        BLOCK_FLOPS,
        8e6,
        bias, own, *far, *inner, *outer, upstream, gain,
    )


def cotangent(stats, others, own, attention, lse, upstream, gain):
    return whole_call(
        cotangent_kernel,
        [f32(BLOCK, WIDTH), f32(BLOCK + 8, WIDTH), f32(BLOCK, WIDTH), f32(64, GRAD), f32(16, GRAD), f32(4, GRAD)],
        [(2, BLOCK, DHEAD)] * 3,
        1e6,
        4e6,
        stats, *others, own, attention, lse, upstream, gain,
    )


def far_query(bias, own, far, first, second, third, near):
    (grad,) = whole_call(
        far_query_kernel,
        [f32(BLOCK, WIDTH)],
        [(2, BLOCK, DHEAD)],
        BLOCK_FLOPS,
        6e6,
        bias, own, *far, first, second, third, near,
    )
    return grad


def early_key(bias, own, grads):
    return whole_call(early_key_kernel, [f32(OWN, WIDTH)] * 2, [], BLOCK_FLOPS, 3e6, bias, own, *grads)


def late_key(bias, own, grads, far_dk, far_dv, near_dk, near_dv):
    return whole_call(
        late_key_kernel,
        [f32(BLOCK, WIDTH)] * 2,
        [(2, BLOCK, DHEAD)] * 2,
        BLOCK_FLOPS,
        3e6,
        bias, own, *grads, far_dk, far_dv, near_dk, near_dv,
    )


def body(query, key, value, norm_gain, upstream):
    count = lax.axis_size("seq")
    head_count = lax.axis_size("head")

    def exchange(array, mask):
        return lax.ppermute(array, "seq", [(i, i ^ mask) for i in range(count)])

    def exchange_outer(array):
        pairs = [(i, i + 1 if i % 2 else i - 1) for i in range(1, count - 1)]
        return lax.ppermute(array, "seq", pairs)

    def after(array, *tokens):
        return lax.optimization_barrier((array,) + tokens)[0]

    def packed(second, thirds):
        return whole_call(pack_kernel, [f32(28, second.shape[1])], [], 1e4, 1e5, second, *thirds)[0]

    def doubled(pack, other):
        return whole_call(double_kernel, [f32(56, pack.shape[1])], [], 1e4, 1e5, pack, other)[0]

    def merged(double, other):
        return whole_call(merge_kernel, [f32(96, double.shape[1])], [], 1e4, 1e5, double, other)[0]

    gain = norm_gain.reshape(1, WIDTH)
    out_k, out_v = exchange_outer(key), exchange_outer(value)
    in_k, in_v = exchange(key, 1), exchange(value, 1)
    own, first, second, third, bias, edge = pool(key, value, query)

    held = after(third, in_k, in_v)
    planes = [exchange(after(held, out_k), PLANES[0])] + [exchange(held, mask) for mask in PLANES[1:]]
    l1a = exchange(first, 2)
    pack = packed(after(second, out_k), planes)
    double = doubled(after(pack, l1a), exchange(pack, 4))
    other = exchange(double, 12)
    w0, *inner = near_inner(query, (key, after(in_k, double)), (value, in_v))
    w1, *outer = near_outer(edge, query, after(out_k, double), out_v)
    l2a = merged(after(double, w0, w1), other)
    l1b = exchange(after(l1a, l2a), 1)
    l2b = exchange(l2a, 2)
    core1 = exchange(l2a, 1)
    core2 = exchange(after(l2b, core1), 1)
    query_in = exchange(after(query, l2a), 1)
    query_out = exchange_outer(after(query, l2a))
    far = (l1a, l1b, l2a, core1, l2b, core2)
    attention, lse, stats = far_forward(bias, own, far, inner, outer, upstream, gain)

    others = [
        lax.ppermute(stats, "head", [(i, i ^ mask) for i in range(head_count)]) for mask in range(1, head_count)
    ]
    attention = after(attention, query_in, query_out)
    attended, d_out, delta, g1, g2, g3 = cotangent(stats, others, own, attention, lse, upstream, gain)

    planes = [exchange(g3, mask) for mask in PLANES]
    l1a = exchange(g1, 2)
    d_in = exchange(d_out, 1)
    pack = packed(g2, planes)
    quad = exchange(pack, 4)
    near_dq = near_query(
        w0, w1, inner[0], outer[0], lse, delta, after(d_out, pack), (key, in_k, out_k), (value, in_v, out_v)
    )
    double = doubled(after(pack, near_dq, l1a), quad)
    other = exchange(double, 12)
    d_far = exchange_outer(after(d_out, double))
    near_dk, near_dv = inner_key(key, value, query, query_in, d_out, after(d_in, double))
    query_grad = far_query(bias, own, far, after(g1, double), g2, g3, near_dq)
    l1b = exchange(after(l1a, double), 1)
    l2a = merged(after(double, near_dk, query_grad, d_far, l1b), other)
    l2b = exchange(l2a, 2)
    core1 = exchange(l2a, 1)
    near_dk, near_dv = outer_key(key, value, query_out, after(d_far, l2a), near_dk, near_dv)
    far_dk, far_dv = early_key(bias, own, (l1a, l1b, after(l2a, near_dk)))
    core2 = exchange(after(l2b, far_dk), 1)
    key_grad, value_grad = late_key(bias, own, (core1, l2b, core2), far_dk, far_dv, near_dk, near_dv)
    return attended, query_grad, key_grad, value_grad


def solution(mesh):
    return jax.shard_map(
        body,
        mesh=mesh,
        in_specs=(
            P("seq", "head"),
            P("seq", "head"),
            P("seq", "head"),
            P("head"),
            P("seq", "head"),
        ),
        out_specs=(P("seq", "head"), P("seq", "head"), P("seq", "head"), P("seq", "head")),
        check_vma=False,
    )
```
